32 devices in a mesh: dp: 8 (over z, y), mp: 4 (over x, core).
Axes of the slice: x: 2, y: 2, z: 4, core: 2. Of those that a mesh axis runs over, the one named last changes fastest.
Arguments:
- latents: float32 [8192, 16], P('dp'), may hold values from -6 to 6
- noise: float32 [8192, 16], P('dp'), may hold values from -6 to 6
- segment_ids: int32 [8192], P('dp'), may hold values from 0 to 3, as said below
- timesteps: int32 [8, 4], P('dp'), may hold values from 0 to 999
- labels: int32 [8, 4], P('dp'), may hold values from 0 to 1000
- w_qkv: float32 [768, 3, 768], P('dp', None, 'mp'), may hold values from -0.3125 to 0.3125
- w_out: float32 [768, 768], P('dp', 'mp'), may hold values from -0.625 to 0.625
- w_fc1: float32 [768, 3072], P('dp', 'mp'), may hold values from -0.21875 to 0.21875
- w_fc2: float32 [768, 3072], P('dp', 'mp'), may hold values from -0.109375 to 0.109375
- w_mod: float32 [768, 8, 768], P('dp', None, 'mp'), may hold values from -0.21875 to 0.21875
- w_head: float32 [768, 16], P('dp'), may hold values from -0.21875 to 0.21875
- w_cond: float32 [768, 2041], P('dp'), may hold values from -5 to 5
- mom_qkv: float32 [768, 3, 768], P('dp', None, 'mp'), may hold values from -0.00021362305 to 0.00021362305
- mom_out: float32 [768, 768], P('dp', 'mp'), may hold values from -0.00021362305 to 0.00021362305
- mom_fc1: float32 [768, 3072], P('dp', 'mp'), may hold values from -0.00021362305 to 0.00021362305
- mom_fc2: float32 [768, 3072], P('dp', 'mp'), may hold values from -0.00021362305 to 0.00021362305
- mom_mod: float32 [768, 8, 768], P('dp', None, 'mp'), may hold values from -0.00021362305 to 0.00021362305
- first_head: float32 [768, 16], P('dp'), may hold values from -2.2888184e-05 to 2.2888184e-05
- second_head: float32 [768, 16], P('dp'), may hold values from 9.718714e-12 to 3.9622448e-11
- first_cond: float32 [768, 2041], P('dp'), may hold values from -2.2888184e-05 to 2.2888184e-05
- second_cond: float32 [768, 2041], P('dp'), may hold values from 9.718714e-12 to 3.9622448e-11
Outputs:
- new_qkv: float32 [768, 3, 768], P('dp', None, 'mp')
- new_out: float32 [768, 768], P('dp', 'mp')
- new_fc1: float32 [768, 3072], P('dp', 'mp')
- new_fc2: float32 [768, 3072], P('dp', 'mp')
- new_mod: float32 [768, 8, 768], P('dp', None, 'mp')
- new_head: float32 [768, 16], P('dp')
- new_cond: float32 [768, 2041], P('dp')
- momentum_qkv: float32 [768, 3, 768], P('dp', None, 'mp')
- momentum_out: float32 [768, 768], P('dp', 'mp')
- momentum_fc1: float32 [768, 3072], P('dp', 'mp')
- momentum_fc2: float32 [768, 3072], P('dp', 'mp')
- momentum_mod: float32 [768, 8, 768], P('dp', None, 'mp')
- new_first_head: float32 [768, 16], P('dp')
- new_second_head: float32 [768, 16], P('dp')
- new_first_cond: float32 [768, 2041], P('dp')
- new_second_cond: float32 [768, 2041], P('dp')
- loss_sum: float32 [], replicated
- weight_total: float32 [], replicated
- grad_norm: float32 [], replicated
The draws below stay inside these ranges and needn't reach their ends.
Inputs may be any that keep to these rules, and one draw needn't show every extreme that they name: `segment_ids`: each row of 1024 tokens is either one latent (all ids 0) or four latents of 256 tokens in order (ids 0, 1, 2, 3); at least one row holds four latents.
All inputs are finite; a program needn't handle non-finite values.
Results may differ from the reference program's by a relative error of at most 0.012.
Values may be sent and summed in bfloat16 or wider, within the bound.
No kernel may reach another device: no remote copies, remote signals or barrier semaphores. Data moves between devices by JAX's collectives and lax.ppermute only.
A program may use at most 256 MiB of HBM per device.

```python
import math
import jax
import jax.numpy as jnp
from jax import lax

SIDE = 32
ROW_LEN = 1024
ROWS = 8
TOKENS = 8192
D = 768
HEADS = 12
HEAD_DIM = 64
FF = 3072
CLASSES = 1001
FREQ = 256
PIN = 16
OUT = 16
CC = 2041
STEP = 10
N_MP = 4


def draw_segment_ids(key, part):
    key = jax.random.fold_in(key, 11)
    kind = jax.random.randint(key, (ROWS,), 0, 2)
    chosen = jax.random.randint(jax.random.fold_in(key, 1), (), 0, ROWS)
    kind = jnp.where(jnp.arange(ROWS) == chosen, 1, kind)
    place = jnp.arange(ROW_LEN)
    ids = jnp.where(kind[:, None] == 1, place[None, :] // (ROW_LEN // 4), 0)
    return ids.reshape(-1).astype(jnp.int32)


def draw_w_cond(key, part):
    key = jax.random.fold_in(key, 5)
    column = jnp.arange(PIN + FREQ + D + CLASSES)
    scale = jnp.where(column < PIN, PIN ** (-0.5), jnp.where(column < PIN + FREQ, FREQ ** (-0.5), jnp.where(column < PIN + FREQ + D, D ** (-0.5), 0.3)))
    base = jnp.clip(jax.random.normal(key, (D, PIN + FREQ + D + CLASSES), jnp.float32), -5.0, 5.0)
    return (base * scale[None, :].astype(jnp.float32)).astype(jnp.float32)


def plant(array, key, least, top_value):
    extent = array.shape
    spot = [jax.random.randint(jax.random.fold_in(key, axis), (), 0, extent[axis]) for axis in range(len(extent))]
    array = array.at[tuple(spot)].set(least)
    longest = extent.index(max(extent))
    spot[longest] = (spot[longest] + 1) % extent[longest]
    return array.at[tuple(spot)].set(top_value)


def level_of(rng, extent, split, smallest, largest):
    factor_of, own = 1.0, jax.random.fold_in(rng, 6)
    for dim, blocks in split:
        steps = jnp.exp(jax.random.uniform(jax.random.fold_in(own, dim), (blocks,), jnp.float32, smallest / len(split), largest / len(split)))
        factor_of = factor_of * jnp.repeat(steps, extent[dim] // blocks).reshape([-1 if axis == dim else 1 for axis in range(len(extent))])
    return factor_of


def bell_draw(key, dims, deviation, limit, cuts=(), held_as=jnp.bfloat16):
    values = jax.random.normal(key, dims, jnp.float32) * deviation
    if len(cuts) > 0:
        values = level_of(key, dims, cuts, -0.22, 0.18) * values
    return jnp.clip(values, min=-limit, max=limit).astype(held_as)


def setup_inputs(seed: int = 0) -> dict:
    key_list = jax.random.split(jax.random.key(seed), 22)
    return {
        "latents": bell_draw(key_list[0], (TOKENS, PIN), 1.0, 6.0, ((0, 8),), jnp.float32),
        "noise": bell_draw(key_list[1], (TOKENS, PIN), 1.0, 6.0, ((0, 8),), jnp.float32),
        "segment_ids": draw_segment_ids(jax.random.fold_in(key_list[21], 71), 0),
        "timesteps": plant(jax.random.randint(key_list[3], (ROWS, 4), 0, 1000), jax.random.fold_in(key_list[3], 1), 0, 999).astype(jnp.int32),
        "labels": plant(jax.random.randint(key_list[4], (ROWS, 4), 0, CLASSES), jax.random.fold_in(key_list[4], 1), 0, CLASSES - 1).astype(jnp.int32),
        "w_qkv": bell_draw(key_list[5], (D, 3, D), (D // 2) ** -0.5, 0.3125, ((0, 8), (2, 4)), jnp.float32),
        "w_out": bell_draw(key_list[6], (D, D), (D // 8) ** -0.5, 0.625, ((0, 8), (1, 4)), jnp.float32),
        "w_fc1": bell_draw(key_list[7], (D, FF), D ** -0.5, 0.21875, ((0, 8), (1, 4)), jnp.float32),
        "w_fc2": bell_draw(key_list[8], (D, FF), FF ** -0.5, 0.109375, ((0, 8), (1, 4)), jnp.float32),
        "w_mod": bell_draw(key_list[9], (D, 8, D), D ** -0.5, 0.21875, ((0, 8), (2, 4)), jnp.float32),
        "w_head": bell_draw(key_list[10], (D, OUT), D ** -0.5, 0.21875, ((0, 8),), jnp.float32),
        "w_cond": draw_w_cond(jax.random.fold_in(key_list[21], 71), 0),
        "mom_qkv": bell_draw(key_list[12], (D, 3, D), (0.05 / (20 * D * D + D * (CC + OUT)) ** 0.5), 0.00021362305, ((0, 8), (2, 4)), jnp.float32),
        "mom_out": bell_draw(key_list[13], (D, D), (0.05 / (20 * D * D + D * (CC + OUT)) ** 0.5), 0.00021362305, ((0, 8), (1, 4)), jnp.float32),
        "mom_fc1": bell_draw(key_list[14], (D, FF), (0.05 / (20 * D * D + D * (CC + OUT)) ** 0.5), 0.00021362305, ((0, 8), (1, 4)), jnp.float32),
        "mom_fc2": bell_draw(key_list[15], (D, FF), (0.05 / (20 * D * D + D * (CC + OUT)) ** 0.5), 0.00021362305, ((0, 8), (1, 4)), jnp.float32),
        "mom_mod": bell_draw(key_list[16], (D, 8, D), (0.05 / (20 * D * D + D * (CC + OUT)) ** 0.5), 0.00021362305, ((0, 8), (2, 4)), jnp.float32),
        "first_head": bell_draw(key_list[17], (D, OUT), (0.0056 / (20 * D * D + D * (CC + OUT)) ** 0.5), 2.288818359375e-05, ((0, 8),), jnp.float32),
        "second_head": jnp.clip(jnp.exp(math.log(3.962244768396239e-11) - 1.40534255 * jax.random.uniform(key_list[18], (D, OUT), jnp.float32) ** level_of(key_list[18], (D, OUT), ((0, 8),), -0.2, 0.2)), 9.718713681050595e-12, 3.962244768396239e-11),
        "first_cond": bell_draw(key_list[19], (D, CC), (0.0056 / (20 * D * D + D * (CC + OUT)) ** 0.5), 2.288818359375e-05, ((0, 8),), jnp.float32),
        "second_cond": jnp.clip(jnp.exp(math.log(3.962244768396239e-11) - 1.40534255 * jax.random.uniform(key_list[20], (D, CC), jnp.float32) ** level_of(key_list[20], (D, CC), ((0, 8),), -0.2, 0.2)), 9.718713681050595e-12, 3.962244768396239e-11),
    }


HIGH = lax.Precision.HIGHEST
GAMMA = 5.0
CLIP = 0.05
MU = 0.95
LR_MUON = 0.1
DECAY = 0.01
BETA_ONE = 0.9
BETA_TWO = 0.95
LR_ADAM = 0.08
EPS_ADAM = 1e-08
NS_COEF = (3.4445, -4.775, 2.0315)

@jax.custom_vjp
def low(v):
    return lax.optimization_barrier(v.astype(jnp.bfloat16)).astype(jnp.float32)

@jax.custom_vjp
def low_back(v):
    return v

def low_keep(v):
    return (low(v), None)

def low_pass(kept, grad):
    return (grad,)

def back_keep(v):
    return (v, None)

def back_low(kept, grad):
    return (low(grad),)
low.defvjp(low_keep, low_pass)
low_back.defvjp(back_keep, back_low)

def plan():
    betas = jnp.linspace(0.0001, 0.02, 1000, dtype=jnp.float32)
    return jnp.cumprod(1.0 - betas)

def pick(table, index):
    grid = jnp.arange(table.shape[0], dtype=jnp.int32)
    return lax.optimization_barrier(jnp.sum(jnp.where(index[..., None] == grid, table, 0.0), -1))

def normalize(x):
    mean = lax.optimization_barrier(jnp.mean(x, -1, keepdims=True))
    cent = x - mean
    return cent * lax.rsqrt(lax.optimization_barrier(jnp.mean(cent * cent, -1, keepdims=True)) + 1e-06)

def modulate(x, shift, scale):
    return normalize(x) * (1.0 + scale) + shift

def positions(seg):
    length = seg.shape[-1]
    place = jnp.arange(length, dtype=jnp.int32)
    local = place - seg * (length // 4)
    side = jnp.where(lax.optimization_barrier(jnp.max(seg, -1, keepdims=True)) == 0, SIDE, SIDE // 2).astype(jnp.int32)
    down = (local // side).astype(jnp.float32)[..., None]
    across = (local % side).astype(jnp.float32)[..., None]
    quarter = D // 4
    omega = 1.0 / 10000.0 ** (jnp.arange(quarter, dtype=jnp.float32) / quarter)
    return jnp.concatenate([jnp.sin(down * omega), jnp.cos(down * omega), jnp.sin(across * omega), jnp.cos(across * omega)], -1)

def time_features(steps):
    half = FREQ // 2
    freqs = jnp.exp(-math.log(10000.0) * jnp.arange(half, dtype=jnp.float32) / half)
    angles = steps.astype(jnp.float32)[:, None] * freqs
    return jnp.concatenate([jnp.cos(angles), jnp.sin(angles)], -1)

def mm(form, left, right):
    return jnp.einsum(form, left, right, precision=HIGH)

def slot_weights(steps):
    abar = pick(plan(), steps)
    snr = abar / (1.0 - abar)
    return (abar, jnp.minimum(snr, GAMMA) / snr)

def row_loss(weights, latent, noise, seg, steps, labels):
    w_qkv, w_out, w_fc1, w_fc2, w_mod, w_head, w_cond = [low(w) for w in weights]
    abar, slot_weight = slot_weights(steps)
    select = (seg[:, None] == jnp.arange(4, dtype=jnp.int32)).astype(jnp.float32)
    abar_tok = mm('ts,s->t', select, abar)
    weight_tok = mm('ts,s->t', select, slot_weight)
    noisy = jnp.sqrt(abar_tok)[:, None] * latent + jnp.sqrt(1.0 - abar_tok)[:, None] * noise
    w_patch = w_cond[:, :PIN]
    w_time1 = w_cond[:, PIN:PIN + FREQ]
    w_time2 = w_cond[:, PIN + FREQ:PIN + FREQ + D]
    table = w_cond[:, PIN + FREQ + D:]
    x_in = low_back(mm('tc,dc->td', low(noisy), w_patch)) + positions(seg[None])[0]
    hidden_t = mm('sf,df->sd', low(time_features(steps)), w_time1)
    time_emb = mm('se,de->sd', low(jax.nn.silu(hidden_t)), w_time2)
    onehot = (labels[:, None] == jnp.arange(CLASSES, dtype=jnp.int32)).astype(jnp.float32)
    cond = time_emb + mm('sk,dk->sd', onehot, table)
    mod = low_back(mm('sd,dke->ske', low(jax.nn.silu(cond)), w_mod))
    mods = [mm('ts,sd->td', select, mod[:, k]) for k in range(8)]
    length = x_in.shape[0]
    h_in = low(modulate(x_in, mods[0], mods[1]))
    qkv = low(low_back(mm('td,dke->tke', h_in, w_qkv)))
    query = qkv[:, 0].reshape(length, HEADS, HEAD_DIM)
    key = qkv[:, 1].reshape(length, HEADS, HEAD_DIM)
    value = qkv[:, 2].reshape(length, HEADS, HEAD_DIM)
    score = HEAD_DIM ** (-0.5) * low_back(mm('qhd,khd->hqk', query, key))
    score = jnp.where((seg[:, None] == seg[None, :])[None], score, -1000000000.0)
    probs = low(jax.nn.softmax(score, -1))
    mixed = low(low_back(mm('hqk,khd->qhd', probs, value))).reshape(length, D)
    attn = low_back(mm('te,de->td', mixed, w_out))
    x_mid = x_in + mods[2] * attn
    h_mid = low(modulate(x_mid, mods[3], mods[4]))
    upper = low_back(mm('td,df->tf', h_mid, w_fc1))
    mlp = low_back(mm('tf,df->td', low(jax.nn.gelu(upper, approximate=False)), w_fc2))
    x_out = x_mid + mods[5] * mlp
    h_fin = low(modulate(x_out, mods[6], mods[7]))
    pred = low_back(mm('td,do->to', h_fin, w_head))
    err = lax.optimization_barrier(jnp.sum((pred - noise) ** 2, -1))
    return jnp.sum(weight_tok * err)

def orthogonal(block):
    if block.shape[0] > block.shape[1]:
        return orthogonal(block.T).T
    first, second, third = NS_COEF
    xmat = block / (jnp.sqrt(jnp.sum(block * block)) + 1e-07)
    for turn in range(5):
        gram = jnp.dot(xmat, xmat.T, precision=HIGH)
        poly = second * gram + third * jnp.dot(gram, gram, precision=HIGH)
        xmat = first * xmat + jnp.dot(poly, xmat, precision=HIGH)
    return xmat

def muon(weight, momentum, grad, coef):
    new_mom = MU * momentum + coef * grad
    width = weight.shape[-1] // N_MP
    pieces = []
    for part in range(N_MP):
        block = new_mom[..., part * width:(part + 1) * width]
        flat = block.reshape(block.shape[0], -1)
        scale = 0.2 * math.sqrt(max(flat.shape))
        pieces.append((scale * orthogonal(flat)).reshape(block.shape))
    step = jnp.concatenate(pieces, -1)
    return (weight * (1.0 - LR_MUON * DECAY) - LR_MUON * step, new_mom)

def adamw(weight, first, second, grad, coef):
    clipped = coef * grad
    first = BETA_ONE * first + (1.0 - BETA_ONE) * clipped
    second = BETA_TWO * second + (1.0 - BETA_TWO) * clipped * clipped
    update = first / (1.0 - BETA_ONE ** STEP) / (jnp.sqrt(second / (1.0 - BETA_TWO ** STEP)) + EPS_ADAM)
    return (weight - LR_ADAM * (update + DECAY * weight), first, second)

def reference(latents, noise, segment_ids, timesteps, labels, w_qkv, w_out, w_fc1, w_fc2, w_mod, w_head, w_cond, mom_qkv, mom_out, mom_fc1, mom_fc2, mom_mod, first_head, second_head, first_cond, second_cond):
    weights = (w_qkv, w_out, w_fc1, w_fc2, w_mod, w_head, w_cond)
    rows = timesteps.shape[0]
    lat = latents.reshape(rows, -1, PIN)
    noi = noise.reshape(rows, -1, PIN)
    seg = segment_ids.reshape(rows, -1)
    abar, slot_weight = slot_weights(timesteps)
    select = (seg[:, :, None] == jnp.arange(4, dtype=jnp.int32)).astype(jnp.float32)
    weight_total = jnp.sum(jnp.einsum('rts,rs->rt', select, slot_weight, precision=HIGH))

    def one_row(carry, data):
        grads, loss = carry
        value, back = jax.vjp(lambda ws: row_loss(ws, *data), weights)
        fresh = back(jnp.ones_like(value) / weight_total)[0]
        return ((jax.tree.map(jnp.add, grads, fresh), loss + value), None)
    zeros = jax.tree.map(jnp.zeros_like, weights)
    (grads, loss_sum), _ = lax.scan(one_row, (zeros, jnp.zeros((), jnp.float32)), (lat, noi, seg, timesteps, labels))
    grad_norm = jnp.sqrt(sum((jnp.sum(g * g) for g in grads)))
    coef = jnp.minimum(1.0, CLIP / (grad_norm + 1e-06))
    new_qkv, momentum_qkv = muon(w_qkv, mom_qkv, grads[0], coef)
    new_out, momentum_out = muon(w_out, mom_out, grads[1], coef)
    new_fc1, momentum_fc1 = muon(w_fc1, mom_fc1, grads[2], coef)
    new_fc2, momentum_fc2 = muon(w_fc2, mom_fc2, grads[3], coef)
    new_mod, momentum_mod = muon(w_mod, mom_mod, grads[4], coef)
    new_head, new_first_head, new_second_head = adamw(w_head, first_head, second_head, grads[5], coef)
    new_cond, new_first_cond, new_second_cond = adamw(w_cond, first_cond, second_cond, grads[6], coef)
    return (new_qkv, new_out, new_fc1, new_fc2, new_mod, new_head, new_cond, momentum_qkv, momentum_out, momentum_fc1, momentum_fc2, momentum_mod, new_first_head, new_second_head, new_first_cond, new_second_cond, loss_sum, weight_total, grad_norm)
```

```python
import math

import jax
import jax.numpy as jnp
from jax import lax
from jax.sharding import PartitionSpec as P

SIDE = 32
D = 768
HEAD_DIM = 64
CLASSES = 1001
FREQ = 256
PIN = 16
STEP = 10
SLOTS = 4

HIGH = lax.Precision.HIGHEST
GAMMA = 5.0
CLIP = 0.05
MU = 0.95
LR_MUON = 0.1
DECAY = 0.01
BETA_ONE = 0.9
BETA_TWO = 0.95
LR_ADAM = 0.08
EPS_ADAM = 1e-08
NS_COEF = (3.4445, -4.775, 2.0315)
NS_SHIFT = (0.0, 0.1, 0.5, 0.8, 0.8)
ACROSS = (((1,), (1,)), ((), ()))
DOWN = (((0,), (0,)), ((), ()))
ALONG = (((1,), (0,)), ((), ()))
LOW = jnp.bfloat16
F32 = jnp.float32


def dot(a, b, dims=ALONG):
    return lax.dot_general(a, b, dims, preferred_element_type=F32)


def swap(x, axis, bit):
    size = lax.axis_size(axis)
    return lax.ppermute(x, axis, [(i, i ^ bit) for i in range(size)])


def gather_rows(x, axis):
    size = lax.axis_size(axis)
    me = lax.axis_index(axis)
    cur = x[None]
    bit = size // 2
    while bit >= 1:
        other = swap(cur, axis, bit)
        low_half = (me // bit) % 2 == 0
        cur = jnp.where(low_half, jnp.stack([cur, other], 1), jnp.stack([other, cur], 1))
        cur = cur.reshape((-1,) + x.shape)
        bit //= 2
    return cur.reshape((-1,) + x.shape[1:])


def scatter_sum(x, axis):
    size = lax.axis_size(axis)
    me = lax.axis_index(axis)
    cur = x.reshape((size, x.shape[0] // size) + x.shape[1:])
    bit = 1
    while bit < size:
        pair = cur.reshape((cur.shape[0] // 2, 2) + cur.shape[1:])
        mine = (me // bit) % 2
        keep = lax.dynamic_index_in_dim(pair, mine, 1, keepdims=False)
        send = lax.dynamic_index_in_dim(pair, 1 - mine, 1, keepdims=False)
        cur = keep.astype(F32) + swap(send.astype(LOW), axis, bit).astype(F32)
        bit *= 2
    return cur[0]


def spread(x, axis):
    size = lax.axis_size(axis)
    copies = jnp.broadcast_to(x[None], (size,) + x.shape)
    return lax.all_to_all(copies, axis, 0, 0, tiled=True)


def exchange(x, axis):
    return lax.all_to_all(x, axis, 0, 0, tiled=True)


def plan():
    betas = jnp.linspace(0.0001, 0.02, 1000, dtype=F32)
    return jnp.cumprod(1.0 - betas)


def pick(table, index):
    grid = jnp.arange(table.shape[0], dtype=jnp.int32)
    return jnp.sum(jnp.where(index[..., None] == grid, table, 0.0), -1)


def normalize(x):
    cent = x - jnp.mean(x, -1, keepdims=True)
    inv = lax.rsqrt(jnp.mean(cent * cent, -1, keepdims=True) + 1e-06)
    return cent * inv, inv


def norm_back(grad, unit, inv, scale):
    d_shift = jnp.sum(grad, 0)
    d_scale = jnp.sum(grad * unit, 0)
    g = grad * (1.0 + scale)
    dx = inv * (g - jnp.mean(g, -1, keepdims=True) - unit * jnp.mean(g * unit, -1, keepdims=True))
    return dx, d_shift, d_scale


def positions(single, part, rank, length):
    quarter = D // 4
    omega = 1.0 / 10000.0 ** (jnp.arange(quarter, dtype=F32) / quarter)
    angle = jnp.arange(SIDE, dtype=F32)[:, None] * omega
    sin, cos = jnp.sin(angle), jnp.cos(angle)
    half = SIDE // 2
    rows = part // SIDE

    def spans(table):
        first = lax.dynamic_slice_in_dim(table, rank * rows, rows, 0)
        down_one = jnp.broadcast_to(first[:, None], (rows, SIDE, quarter)).reshape(part, quarter)
        down_four = jnp.broadcast_to(table[:half, None], (half, half, quarter)).reshape(part, quarter)
        across_one = jnp.broadcast_to(table[None], (rows, SIDE, quarter)).reshape(part, quarter)
        across_four = jnp.broadcast_to(table[None, :half], (half, half, quarter)).reshape(part, quarter)
        return jnp.where(single, down_one, down_four), jnp.where(single, across_one, across_four)

    sin_down, sin_across = spans(sin)
    cos_down, cos_across = spans(cos)
    return jnp.concatenate([sin_down, cos_down, sin_across, cos_across], -1)


def time_features(steps):
    half = FREQ // 2
    freqs = jnp.exp(-math.log(10000.0) * jnp.arange(half, dtype=F32) / half)
    angles = steps.astype(F32)[:, None] * freqs
    return jnp.concatenate([jnp.cos(angles), jnp.sin(angles)], -1)


def silu_slope(x):
    s = jax.nn.sigmoid(x)
    return s * (1.0 + x * (1.0 - s))


def heads_of(block):
    return block.reshape(block.shape[0], -1, HEAD_DIM).transpose(1, 0, 2)


def rows_of(block):
    return block.transpose(1, 0, 2).reshape(block.shape[1], -1)


def masked_scores(query, key, seg):
    score = jnp.einsum("hqd,hkd->hqk", query, key, preferred_element_type=F32) * HEAD_DIM ** (-0.5)
    return jnp.where((seg[:, None] == seg[None, :])[None], score, -1000000000.0)


def attend(query, key, value, seg):
    score = masked_scores(query, key, seg)
    top = jnp.max(score, -1, keepdims=True)
    total = top + jnp.log(jnp.sum(jnp.exp(score - top), -1, keepdims=True))
    probs = jnp.exp(score - total).astype(LOW)
    mixed = jnp.einsum("hqk,hkd->hqd", probs, value, preferred_element_type=F32)
    return mixed, total


def attend_back(query, key, value, seg, total, grad):
    probs = jnp.exp(masked_scores(query, key, seg) - total)
    d_probs = jnp.einsum("hqd,hkd->hqk", grad, value, preferred_element_type=F32)
    d_value = jnp.einsum("hqk,hqd->hkd", probs.astype(LOW), grad, preferred_element_type=F32)
    delta = jnp.sum(d_probs * probs, -1, keepdims=True)
    d_score = (probs * (d_probs - delta) * HEAD_DIM ** (-0.5)).astype(LOW)
    d_query = jnp.einsum("hqk,hkd->hqd", d_score, key, preferred_element_type=F32)
    d_key = jnp.einsum("hqk,hqd->hkd", d_score, query, preferred_element_type=F32)
    return d_query, d_key, d_value


def orthogonal_rows(whole, own, count):
    first, second, third = NS_COEF
    wide = whole.shape[0] <= whole.shape[1]
    x = whole / (jnp.sqrt(jnp.sum(whole * whole)) + 1e-07)
    size = min(whole.shape)
    eye = jnp.eye(size, dtype=F32)
    last = len(NS_SHIFT) - 1
    for turn, shift in enumerate(NS_SHIFT):
        xb = x.astype(LOW)
        gram = dot(xb, xb, ACROSS if wide else DOWN) - shift * eye
        gb = gram.astype(LOW)
        centre = first + second * shift + third * shift * shift
        slope = second + 2.0 * third * shift
        if turn == last:
            x = lax.dynamic_slice_in_dim(x, own, count, 0)
            if wide:
                mine = lax.dynamic_slice_in_dim(gram, own, count, 0)
                poly = slope * mine + third * dot(mine.astype(LOW), gb)
                return centre * x + dot(poly.astype(LOW), xb)
            poly = slope * gram + third * dot(gb, gb)
            return centre * x + dot(x.astype(LOW), poly.astype(LOW))
        poly = (slope * gram + third * dot(gb, gb)).astype(LOW)
        x = centre * x + (dot(poly, xb) if wide else dot(xb, poly))


def body(
    latents,
    noise,
    segment_ids,
    timesteps,
    labels,
    w_qkv,
    w_out,
    w_fc1,
    w_fc2,
    w_mod,
    w_head,
    w_cond,
    mom_qkv,
    mom_out,
    mom_fc1,
    mom_fc2,
    mom_mod,
    first_head,
    second_head,
    first_cond,
    second_cond,
):
    n_dp, n_mp = lax.axis_size("dp"), lax.axis_size("mp")
    me, rank = lax.axis_index("dp"), lax.axis_index("mp")
    tokens = latents.shape[0]
    part = tokens // n_mp
    rows = w_qkv.shape[0]
    width = w_qkv.shape[2]
    hidden = w_fc1.shape[1]

    qkv_b = gather_rows(w_qkv.reshape(rows, -1).astype(LOW), "dp")
    rest = gather_rows(jnp.concatenate([w_out, w_fc1, w_fc2], 1).astype(LOW), "dp")
    out_b, fc1_b, fc2_b = rest[:, :width], rest[:, width : width + hidden], rest[:, width + hidden :]

    single = jnp.max(segment_ids) == 0
    note = jnp.concatenate(
        [
            timesteps.reshape(-1).astype(F32),
            labels.reshape(-1).astype(F32),
            single.astype(F32)[None],
            jnp.zeros((2 * PIN - 2 * SLOTS - 1,), F32),
        ]
    )
    thin = jnp.concatenate([w_cond[:, :PIN], w_head], 1)
    packet = spread(jnp.concatenate([thin, jnp.broadcast_to(note, (8, 2 * PIN))], 0), "dp")
    packet = packet.reshape(n_dp, rows + 8, 2 * PIN)
    thin_b = packet[:, :rows].reshape(n_dp * rows, 2 * PIN).astype(LOW)
    patch_b, head_b = thin_b[:, :PIN], thin_b[:, PIN:]
    notes = packet[:, rows]
    steps = notes[:, :SLOTS].astype(jnp.int32)
    kinds = notes[:, SLOTS : 2 * SLOTS].astype(jnp.int32).reshape(-1)
    singles = notes[:, 2 * SLOTS] > 0.5

    abar = pick(plan(), steps)
    snr = abar / (1.0 - abar)
    slot_weight = jnp.minimum(snr, GAMMA) / snr
    weight_total = part * jnp.sum(jnp.where(singles[:, None], n_mp * slot_weight[:, :1] / SLOTS, slot_weight))

    time1_b = w_cond[:, PIN : PIN + FREQ].astype(LOW)
    time2_b = w_cond[:, PIN + FREQ : PIN + FREQ + D].astype(LOW)
    table_b = w_cond[:, PIN + FREQ + D :].astype(LOW)
    mod_b = w_mod.reshape(rows, -1).astype(LOW)
    feat_b = time_features(steps.reshape(-1)).astype(LOW)
    slots_all = feat_b.shape[0]
    hidden_t = dot(feat_b, time1_b, ACROSS)
    silu_t = spread(jax.nn.silu(hidden_t).astype(LOW), "dp").reshape(n_dp, slots_all, rows)
    silu_t_b = silu_t.transpose(1, 0, 2).reshape(slots_all, n_dp * rows)
    onehot = (kinds[:, None] == jnp.arange(CLASSES, dtype=jnp.int32)).astype(F32)
    cond = dot(silu_t_b, time2_b, ACROSS) + dot(onehot.astype(LOW), table_b, ACROSS)
    silu_c_b = jax.nn.silu(cond).astype(LOW)
    mod_part = dot(silu_c_b, mod_b).reshape(n_dp, SLOTS, -1)
    mod_cols = jnp.sum(exchange(mod_part, "dp"), 0).reshape(SLOTS, 8, width)
    mod = lax.all_gather(mod_cols, "mp", axis=2, tiled=True)
    slot = lax.dynamic_index_in_dim(segment_ids, rank * part, 0, keepdims=False)
    mods = lax.dynamic_index_in_dim(mod, slot, 0, keepdims=False)

    my_row = lambda a: lax.dynamic_index_in_dim(a, me, 0, keepdims=False)
    my_slot = lambda a: lax.dynamic_index_in_dim(my_row(a), slot, 0, keepdims=False)
    abar_tok, weight_tok = my_slot(abar), my_slot(slot_weight)
    lat = lax.dynamic_slice_in_dim(latents, rank * part, part, 0)
    noi = lax.dynamic_slice_in_dim(noise, rank * part, part, 0)
    noisy_b = (jnp.sqrt(abar_tok) * lat + jnp.sqrt(1.0 - abar_tok) * noi).astype(LOW)
    x_in = dot(noisy_b, patch_b, ACROSS) + positions(single, part, rank, tokens)
    unit1, inv1 = normalize(x_in)
    h_in = gather_rows((unit1 * (1.0 + mods[1]) + mods[0]).astype(LOW), "mp")

    qkv = dot(h_in, qkv_b).astype(LOW)
    query, key, value = (heads_of(qkv[:, k * width : (k + 1) * width]) for k in range(3))
    mixed, totals = attend(query, key, value, segment_ids)
    mixed_b = rows_of(mixed.astype(LOW))
    attn = scatter_sum(dot(mixed_b, out_b, ACROSS), "mp")
    x_mid = x_in + mods[2] * attn
    unit2, inv2 = normalize(x_mid)
    h_mid = gather_rows((unit2 * (1.0 + mods[4]) + mods[3]).astype(LOW), "mp")
    upper = dot(h_mid, fc1_b)
    act_b = jax.nn.gelu(upper, approximate=False).astype(LOW)
    mlp = scatter_sum(dot(act_b, fc2_b, ACROSS), "mp")
    x_out = x_mid + mods[5] * mlp
    unit3, inv3 = normalize(x_out)
    h_fin = (unit3 * (1.0 + mods[7]) + mods[6]).astype(LOW)
    pred = dot(h_fin, head_b)
    diff = pred - noi
    loss_part = weight_tok * jnp.sum(diff * diff)

    d_pred = (2.0 * diff * (weight_tok / weight_total)).astype(LOW)
    d_head = dot(h_fin, d_pred, DOWN)
    d_out, d_shiftf, d_scalef = norm_back(dot(d_pred, head_b, ACROSS), unit3, inv3, mods[7])
    d_gate2 = jnp.sum(d_out * mlp, 0)
    d_mlp = gather_rows((d_out * mods[5]).astype(LOW), "mp")
    d_fc2 = dot(d_mlp, act_b, DOWN)
    d_act = dot(d_mlp, fc2_b)
    _, gelu_back = jax.vjp(lambda v: jax.nn.gelu(v, approximate=False), upper)
    d_upper = gelu_back(d_act)[0].astype(LOW)
    d_fc1 = dot(h_mid, d_upper, DOWN)
    d_hmid = scatter_sum(dot(d_upper, fc1_b, ACROSS), "mp")
    dx_mid, d_shift2, d_scale2 = norm_back(d_hmid, unit2, inv2, mods[4])
    d_mid = d_out + dx_mid
    d_gate1 = jnp.sum(d_mid * attn, 0)
    d_attn = gather_rows((d_mid * mods[2]).astype(LOW), "mp")
    d_outw = dot(d_attn, mixed_b, DOWN)
    d_mixed = heads_of(dot(d_attn, out_b).astype(LOW))
    d_query, d_key, d_value = attend_back(query, key, value, segment_ids, totals, d_mixed)
    d_qkv = jnp.concatenate([rows_of(g.astype(LOW)) for g in (d_query, d_key, d_value)], 1)
    d_wqkv = dot(h_in, d_qkv, DOWN)
    d_hin = scatter_sum(dot(d_qkv, qkv_b, ACROSS), "mp")
    dx_in, d_shift1, d_scale1 = norm_back(d_hin, unit1, inv1, mods[1])
    d_x = (d_mid + dx_in).astype(LOW)
    d_patch = dot(d_x, noisy_b, DOWN)

    sum_fc = scatter_sum(jnp.concatenate([d_fc1, d_fc2], 1), "dp")
    sum_at = scatter_sum(jnp.concatenate([d_wqkv, d_outw], 1), "dp")
    all_fc = gather_rows(sum_fc.astype(LOW), "dp")
    all_at = gather_rows(sum_at.astype(LOW), "dp")

    d_mods = jnp.stack([d_shift1, d_scale1, d_gate1, d_shift2, d_scale2, d_gate2, d_shiftf, d_scalef])
    blocks = exchange(d_mods.reshape(8, n_mp, width).transpose(1, 0, 2), "mp")
    first_only = (jnp.arange(SLOTS) == 0)[:, None, None]
    d_mod = jnp.where(single, jnp.where(first_only, jnp.sum(blocks, 0, keepdims=True), 0.0), blocks)
    d_mod = d_mod.astype(LOW).reshape(SLOTS, 8 * width)
    bundle = jnp.concatenate([d_mod, silu_c_b.reshape(SLOTS, -1)], 1)
    bundle = spread(bundle, "dp").reshape(n_dp, SLOTS, -1)
    d_mod_all = bundle[:, :, : 8 * width].reshape(slots_all, 8 * width)
    silu_c_all = (
        bundle[:, :, 8 * width :].reshape(n_dp, slots_all, rows).transpose(1, 0, 2).reshape(slots_all, -1)
    )
    g_mod_all = dot(silu_c_all, d_mod_all, DOWN)
    g_mod = dot(silu_c_b, d_mod_all, DOWN)
    d_cond_part = dot(d_mod_all, mod_b, ACROSS) * silu_slope(cond)
    d_silu_t_part = lax.dot_general(d_cond_part, time2_b.astype(F32), ALONG, precision=HIGH)
    thick = jnp.concatenate([d_silu_t_part.T, d_patch, d_head], 1)
    thick = jnp.sum(exchange(thick.reshape(n_dp, rows, -1), "dp"), 0)
    thick = lax.psum(jnp.concatenate([thick, d_cond_part.T], 1), "mp")
    d_silu_t = thick[:, :slots_all].T
    g_patch = thick[:, slots_all : slots_all + PIN]
    g_head = thick[:, slots_all + PIN : slots_all + 2 * PIN]
    d_cond = thick[:, slots_all + 2 * PIN :]
    g_table = lax.dot_general(d_cond, onehot, ALONG, precision=HIGH)
    g_time2 = lax.dot_general(d_cond, silu_t_b.astype(F32), ALONG, precision=HIGH)
    d_hidden = d_silu_t * silu_slope(hidden_t)
    g_time1 = lax.dot_general(d_hidden, feat_b.astype(F32), DOWN, precision=HIGH)
    g_cond = jnp.concatenate([g_patch, g_time1, g_time2, g_table], 1)

    square = lambda g: jnp.sum(g * g)
    split_sq = square(sum_fc) + square(sum_at) + square(g_mod)
    shared = lax.psum(jnp.stack([split_sq, loss_part]), "mp")
    tally = jnp.stack([shared[0] + square(g_head) + square(g_cond), shared[1]])
    tally = jnp.sum(spread(jnp.broadcast_to(tally[:, None], (2, 128)), "dp"), 0)
    grad_norm = jnp.sqrt(tally[0, 0])
    loss_sum = tally[1, 0]
    coef = jnp.minimum(1.0, CLIP / (grad_norm + 1e-06))

    moms = [m.reshape(rows, -1) for m in (mom_qkv, mom_out, mom_fc1, mom_fc2, mom_mod)]
    old = lax.all_gather(jnp.concatenate(moms, 1).astype(LOW), "dp", axis=0, tiled=True)
    masters = (w_qkv, w_out, w_fc1, w_fc2, w_mod)
    fresh = (
        sum_at[:, : 3 * width],
        sum_at[:, 3 * width :],
        sum_fc[:, :hidden],
        sum_fc[:, hidden:],
        g_mod,
    )
    whole = (all_at[:, : 3 * width], all_at[:, 3 * width :], all_fc[:, :hidden], all_fc[:, hidden:], g_mod_all)
    new_weights, new_moms = [], []
    start = 0
    for master, mom, grad, full in zip(masters, moms, fresh, whole):
        cols = mom.shape[1]
        new_moms.append((MU * mom + coef * grad).reshape(master.shape))
        full_mom = MU * old[:, start : start + cols].astype(F32) + coef * full.astype(F32)
        scale = 0.2 * math.sqrt(max(full_mom.shape))
        mine = (scale * orthogonal_rows(full_mom, me * rows, rows)).reshape(master.shape)
        new_weights.append(master * (1.0 - LR_MUON * DECAY) - LR_MUON * mine)
        start += cols

    adam_out = []
    for master, first, second, grad in (
        (w_head, first_head, second_head, g_head),
        (w_cond, first_cond, second_cond, g_cond),
    ):
        clipped = coef * grad
        first = BETA_ONE * first + (1.0 - BETA_ONE) * clipped
        second = BETA_TWO * second + (1.0 - BETA_TWO) * clipped * clipped
        update = first / (1.0 - BETA_ONE**STEP) / (jnp.sqrt(second / (1.0 - BETA_TWO**STEP)) + EPS_ADAM)
        adam_out.append((master - LR_ADAM * (update + DECAY * master), first, second))
    return (
        *new_weights,
        adam_out[0][0],
        adam_out[1][0],
        *new_moms,
        adam_out[0][1],
        adam_out[0][2],
        adam_out[1][1],
        adam_out[1][2],
        loss_sum,
        weight_total,
        grad_norm,
    )


def solution(mesh):
    row, wide, cube = P("dp", None), P("dp", "mp"), P("dp", None, "mp")
    in_specs = (
        *(row, row, P("dp"), row, row),
        *(cube, wide, wide, wide, cube, row, row),
        *(cube, wide, wide, wide, cube),
        *(row, row, row, row),
    )
    out_specs = (
        *(cube, wide, wide, wide, cube, row, row),
        *(cube, wide, wide, wide, cube),
        *(row, row, row, row),
        *(P(), P(), P()),
    )
    return jax.shard_map(body, mesh=mesh, in_specs=in_specs, out_specs=out_specs, check_vma=False)
```

```python
import functools
import math

import jax
import jax.numpy as jnp
from jax import lax
from jax.experimental import pallas as pl
from jax.experimental.pallas import tpu as pltpu
from jax.sharding import PartitionSpec as P

SIDE = 32
D = 768
HEAD_DIM = 64
CLASSES = 1001
FREQ = 256
PIN = 16
STEP = 10
SLOTS = 4

HIGH = lax.Precision.HIGHEST
GAMMA = 5.0
CLIP = 0.05
MU = 0.95
LR_MUON = 0.1
DECAY = 0.01
BETA_ONE = 0.9
BETA_TWO = 0.95
LR_ADAM = 0.08
EPS_ADAM = 1e-08
NS_COEF = (3.4445, -4.775, 2.0315)
NS_SHIFT = (0.0, 0.1, 0.5, 0.8, 0.8)
ACROSS = (((1,), (1,)), ((), ()))
DOWN = (((0,), (0,)), ((), ()))
ALONG = (((1,), (0,)), ((), ()))
LOW = jnp.bfloat16
F32 = jnp.float32


def dot(a, b, dims=ALONG):
    return lax.dot_general(a, b, dims, preferred_element_type=F32)


def swap(x, axis, bit):
    size = lax.axis_size(axis)
    return lax.ppermute(x, axis, [(i, i ^ bit) for i in range(size)])


def after(x, *others):
    return lax.optimization_barrier((x,) + others)[0]


def gather_steps(x, axis):
    size = lax.axis_size(axis)
    me = lax.axis_index(axis)
    cur = x[None]
    bit = size // 2
    while bit >= 1:
        other = swap(cur, axis, bit)
        other = yield other
        low_half = (me // bit) % 2 == 0
        cur = jnp.where(low_half, jnp.stack([cur, other], 1), jnp.stack([other, cur], 1))
        cur = cur.reshape((-1,) + x.shape)
        bit //= 2
    return cur.reshape((-1,) + x.shape[1:])


def sum_steps(x, axis):
    size = lax.axis_size(axis)
    me = lax.axis_index(axis)
    cur = x.reshape((size, x.shape[0] // size) + x.shape[1:])
    bit = 1
    while bit < size:
        pair = cur.reshape((cur.shape[0] // 2, 2) + cur.shape[1:])
        mine = (me // bit) % 2
        keep = lax.dynamic_index_in_dim(pair, mine, 1, keepdims=False)
        send = lax.dynamic_index_in_dim(pair, 1 - mine, 1, keepdims=False)
        other = swap(send.astype(LOW), axis, bit)
        other = yield other
        cur = keep.astype(F32) + other.astype(F32)
        bit *= 2
    return cur[0]


class Course:
    def __init__(self, steps):
        self.steps = steps
        self.result = None
        self.flight = next(steps)

    def step(self, x=None):
        arrived = self.flight
        if arrived is None:
            return x
        if x is not None:
            x = after(x, arrived)
        try:
            self.flight = self.steps.send(arrived)
        except StopIteration as stop:
            self.flight, self.result = None, stop.value
        return x

    def finish(self):
        while self.flight is not None:
            self.step()
        return self.result


def gather_rows(x, axis):
    return Course(gather_steps(x, axis)).finish()


def scatter_sum(x, axis):
    return Course(sum_steps(x, axis)).finish()


def sum_all(x, axis):
    bit = 1
    while bit < lax.axis_size(axis):
        x = x + swap(x, axis, bit)
        bit *= 2
    return x


def spread(x, axis):
    size = lax.axis_size(axis)
    copies = jnp.broadcast_to(x[None], (size,) + x.shape)
    return lax.all_to_all(copies, axis, 0, 0, tiled=True)


def exchange(x, axis):
    return lax.all_to_all(x, axis, 0, 0, tiled=True)


def plan():
    betas = jnp.linspace(0.0001, 0.02, 1000, dtype=F32)
    return jnp.cumprod(1.0 - betas)


def pick(table, index):
    grid = jnp.arange(table.shape[0], dtype=jnp.int32)
    return jnp.sum(jnp.where(index[..., None] == grid, table, 0.0), -1)


def normalize(x):
    cent = x - jnp.mean(x, -1, keepdims=True)
    inv = lax.rsqrt(jnp.mean(cent * cent, -1, keepdims=True) + 1e-06)
    return cent * inv, inv


def norm_back(grad, unit, inv, scale):
    d_shift = jnp.sum(grad, 0)
    d_scale = jnp.sum(grad * unit, 0)
    g = grad * (1.0 + scale)
    dx = inv * (g - jnp.mean(g, -1, keepdims=True) - unit * jnp.mean(g * unit, -1, keepdims=True))
    return dx, d_shift, d_scale


def place_table():
    quarter = D // 4
    column = jnp.arange(D, dtype=jnp.int32)
    omega = 1.0 / 10000.0 ** ((column % quarter).astype(F32) / quarter)
    angle = jnp.arange(SIDE, dtype=F32)[:, None] * omega
    wave = jnp.where((column // quarter) % 2 == 0, jnp.sin(angle), jnp.cos(angle))
    down = column < D // 2
    return jnp.concatenate([jnp.where(down, wave, 0.0), jnp.where(down, 0.0, wave)], 0)


def place_select(single, part, rank):
    local = jnp.arange(part, dtype=jnp.int32)
    full = rank * part + local
    half = SIDE // 2
    down = jnp.where(single, full // SIDE, local // half)
    across = jnp.where(single, full % SIDE, local % half)
    grid = jnp.arange(SIDE, dtype=jnp.int32)
    return jnp.concatenate([down[:, None] == grid, across[:, None] == grid], 1)


def thirds(x):
    high = x.astype(LOW)
    rest = x - high.astype(F32)
    mid = rest.astype(LOW)
    return high, mid, (rest - mid.astype(F32)).astype(LOW)


def time_features(steps):
    half = FREQ // 2
    freqs = jnp.exp(-math.log(10000.0) * jnp.arange(half, dtype=F32) / half)
    angles = steps.astype(F32)[:, None] * freqs
    return jnp.concatenate([jnp.cos(angles), jnp.sin(angles)], -1)


def silu_slope(x):
    s = jax.nn.sigmoid(x)
    return s * (1.0 + x * (1.0 - s))


def params():
    return pltpu.CompilerParams(vmem_limit_bytes=48 * 2**20)


def turned(x):
    return x.astype(F32).T.astype(x.dtype)


def attend_kernel(single_ref, qkv_ref, mixed_ref, total_ref, vt_ref):
    part, width = mixed_ref.shape
    i = pl.program_id(0)
    mine = pl.ds(pl.multiple_of(i * part, part), part)

    @pl.when(i == 0)
    def _():
        vt_ref[...] = turned(qkv_ref[:, 2 * width :])

    def run(keys):
        outs = []
        for h in range(width // HEAD_DIM):
            lo = h * HEAD_DIM
            q = qkv_ref[mine, lo : lo + HEAD_DIM] * HEAD_DIM**-0.5
            k = qkv_ref[keys, width + lo : width + lo + HEAD_DIM]
            s = dot(k, q, ACROSS)
            top = jnp.max(s, axis=0, keepdims=True)
            e = jnp.exp(s - top)
            z = jnp.sum(e, axis=0, keepdims=True)
            total_ref[h : h + 1, :] = top + jnp.log(z)
            outs.append(dot(vt_ref[lo : lo + HEAD_DIM, keys], (e * (1.0 / z)).astype(LOW)))
        mixed_ref[...] = jnp.concatenate(outs, 0).T.astype(LOW)

    @pl.when(single_ref[0] == 1)
    def _():
        run(slice(None))

    @pl.when(single_ref[0] != 1)
    def _():
        run(mine)


def attend(single, qkv, part):
    tokens, columns = qkv.shape
    width = columns // 3
    return pl.pallas_call(
        attend_kernel,
        grid=(tokens // part,),
        out_shape=(
            jax.ShapeDtypeStruct((tokens, width), LOW),
            jax.ShapeDtypeStruct((8, tokens), F32),
        ),
        in_specs=[
            pl.BlockSpec(memory_space=pltpu.SMEM),
            pl.BlockSpec((tokens, columns), lambda i: (0, 0)),
        ],
        out_specs=(
            pl.BlockSpec((part, width), lambda i: (i, 0)),
            pl.BlockSpec((8, part), lambda i: (0, i)),
        ),
        scratch_shapes=[pltpu.VMEM((width, tokens), LOW)],
        compiler_params=params(),
        cost_estimate=pl.CostEstimate(
            flops=4 * tokens * tokens * width,
            bytes_accessed=8 * tokens * width,
            transcendentals=tokens * tokens * width // HEAD_DIM,
        ),
        name="attend",
    )(single, qkv)


def attend_back_kernel(single_ref, qkv_ref, grad_ref, total_ref, out_ref, kt_ref, dk_ref, dv_ref):
    width = qkv_ref.shape[1] // 3
    part = grad_ref.shape[0]
    heads = width // HEAD_DIM
    i = pl.program_id(0)
    mine = pl.ds(pl.multiple_of(i * part, part), part)

    @pl.when(i == 0)
    def _():
        kt_ref[...] = turned(qkv_ref[:, width : 2 * width] * HEAD_DIM**-0.5)
        dk_ref[...] = jnp.zeros_like(dk_ref)
        dv_ref[...] = jnp.zeros_like(dv_ref)

    def run(keys):
        outs = []
        for h in range(heads):
            lo = h * HEAD_DIM
            q = qkv_ref[mine, lo : lo + HEAD_DIM] * HEAD_DIM**-0.5
            k = qkv_ref[keys, width + lo : width + lo + HEAD_DIM]
            v = qkv_ref[keys, 2 * width + lo : 2 * width + lo + HEAD_DIM]
            g = grad_ref[:, lo : lo + HEAD_DIM]
            p = jnp.exp(dot(k, q, ACROSS) - total_ref[h : h + 1, :])
            dp = dot(v, g, ACROSS)
            delta = jnp.sum(dp * p, axis=0, keepdims=True)
            ds = (p * (dp - delta)).astype(LOW)
            dv_ref[h, keys, :] += dot(p.astype(LOW), g)
            dk_ref[h, keys, :] += dot(ds, q)
            outs.append(dot(kt_ref[lo : lo + HEAD_DIM, keys], ds))
        out_ref[mine, :width] = jnp.concatenate(outs, 0).T.astype(LOW)

    @pl.when(single_ref[0] == 1)
    def _():
        run(slice(None))

    @pl.when(single_ref[0] != 1)
    def _():
        run(mine)

    @pl.when(i == pl.num_programs(0) - 1)
    def _():
        for h in range(heads):
            lo = h * HEAD_DIM
            out_ref[:, width + lo : width + lo + HEAD_DIM] = dk_ref[h].astype(LOW)
            out_ref[:, 2 * width + lo : 2 * width + lo + HEAD_DIM] = dv_ref[h].astype(LOW)


def attend_back(single, qkv, grad, totals, part):
    tokens, columns = qkv.shape
    width = columns // 3
    heads = width // HEAD_DIM
    return pl.pallas_call(
        attend_back_kernel,
        grid=(tokens // part,),
        out_shape=jax.ShapeDtypeStruct((tokens, columns), LOW),
        in_specs=[
            pl.BlockSpec(memory_space=pltpu.SMEM),
            pl.BlockSpec((tokens, columns), lambda i: (0, 0)),
            pl.BlockSpec((part, width), lambda i: (i, 0)),
            pl.BlockSpec((8, part), lambda i: (0, i)),
        ],
        out_specs=pl.BlockSpec((tokens, columns), lambda i: (0, 0)),
        scratch_shapes=[
            pltpu.VMEM((width, tokens), LOW),
            pltpu.VMEM((heads, tokens, HEAD_DIM), F32),
            pltpu.VMEM((heads, tokens, HEAD_DIM), F32),
        ],
        compiler_params=params(),
        cost_estimate=pl.CostEstimate(
            flops=10 * tokens * tokens * width,
            bytes_accessed=14 * tokens * width,
            transcendentals=tokens * tokens * heads,
        ),
        name="attend_back",
    )(single, qkv, grad, totals)


def muon_kernel(tile, columns, own_ref, coef_ref, mom_ref, *refs):
    grads, (out_ref, x_ref, a_ref, b_ref, e_ref, eb_ref) = refs[:-6], refs[-6:]
    first, second, third = NS_COEF
    size, count = x_ref.shape[0], out_ref.shape[0]
    tiles = size // tile
    coef = coef_ref[0]
    span = slice(*columns)

    def rows(i):
        return pl.ds(pl.multiple_of(i * tile, tile), tile)

    def load(i, total):
        if len(grads) == 2:
            grad = dot(grads[0][rows(i), :], grads[1][...])
        else:
            grad = grads[0][rows(i), span].astype(F32)
        x = MU * mom_ref[rows(i), span].astype(F32) + coef * grad
        x_ref[rows(i), :] = x
        return total + jnp.sum(x * x, axis=0, keepdims=True)

    squares = lax.fori_loop(0, tiles, load, jnp.zeros((1, x_ref.shape[1]), F32))
    inv = 1.0 / (jnp.sqrt(jnp.sum(squares, axis=1, keepdims=True)) + 1e-07)

    def scale(i, carry):
        x = x_ref[rows(i), :] * inv
        x_ref[rows(i), :] = x
        a_ref[rows(i), :] = x.astype(LOW)
        return carry

    lax.fori_loop(0, tiles, scale, 0)
    cur, new = a_ref, b_ref
    for turn, shift in enumerate(NS_SHIFT):
        centre = first + second * shift + third * shift * shift
        slope = second + 2.0 * third * shift

        def gram(i, carry):
            e = dot(cur[rows(i), :], cur[...], ACROSS)
            if shift:
                row = lax.broadcasted_iota(jnp.int32, e.shape, 0) + i * tile
                column = lax.broadcasted_iota(jnp.int32, e.shape, 1)
                e = e - jnp.where(row == column, shift, 0.0)
            e_ref[rows(i), :] = e
            eb_ref[rows(i), :] = e.astype(LOW)
            return carry

        def step(i, carry):
            poly = slope * e_ref[rows(i), :] + third * dot(eb_ref[rows(i), :], eb_ref[...])
            x = centre * x_ref[rows(i), :] + dot(poly.astype(LOW), cur[...])
            x_ref[rows(i), :] = x
            new[rows(i), :] = x.astype(LOW)
            return carry

        lax.fori_loop(0, tiles, gram, 0)
        if turn < len(NS_SHIFT) - 1:
            lax.fori_loop(0, tiles, step, 0)
            cur, new = new, cur
        else:
            own = pl.ds(pl.multiple_of(own_ref[0], 16), count)
            e = e_ref[own, :]
            poly = slope * e + third * dot(e.astype(LOW), eb_ref[...])
            x = centre * x_ref[own, :] + dot(poly.astype(LOW), cur[...])
            out_ref[...] = (0.2 * math.sqrt(max(x_ref.shape)) * x).astype(LOW)


def muon_rows(own, count, coef, mom, mom_block, grads, grad_block, block, columns):
    size = mom.shape[0]
    width = columns[1] - columns[0]
    tile = size // 2 if width > size else size
    whole = lambda a: pl.BlockSpec(a.shape, lambda i: (0, 0))
    packed = lambda k: pl.BlockSpec((size, block), lambda i: (0, k))
    smem = pl.BlockSpec(memory_space=pltpu.SMEM)
    return pl.pallas_call(
        functools.partial(muon_kernel, tile, columns),
        grid=(1,),
        out_shape=jax.ShapeDtypeStruct((count, width), LOW),
        in_specs=[smem, smem, packed(mom_block)]
        + ([whole(g) for g in grads] if len(grads) == 2 else [packed(grad_block)]),
        out_specs=pl.BlockSpec((count, width), lambda i: (0, 0)),
        scratch_shapes=[
            pltpu.VMEM((size, width), F32),
            pltpu.VMEM((size, width), LOW),
            pltpu.VMEM((size, width), LOW),
            pltpu.VMEM((size, size), F32),
            pltpu.VMEM((size, size), LOW),
        ],
        compiler_params=params(),
        cost_estimate=pl.CostEstimate(
            flops=10 * size * size * (2 * width + size), bytes_accessed=6 * size * width, transcendentals=0
        ),
        name="muon",
    )(own, coef, mom, *grads)


def body(
    latents,
    noise,
    segment_ids,
    timesteps,
    labels,
    w_qkv,
    w_out,
    w_fc1,
    w_fc2,
    w_mod,
    w_head,
    w_cond,
    mom_qkv,
    mom_out,
    mom_fc1,
    mom_fc2,
    mom_mod,
    first_head,
    second_head,
    first_cond,
    second_cond,
):
    n_dp, n_mp = lax.axis_size("dp"), lax.axis_size("mp")
    me, rank = lax.axis_index("dp"), lax.axis_index("mp")
    tokens = latents.shape[0]
    part = tokens // n_mp
    rows = w_qkv.shape[0]
    width = w_qkv.shape[2]
    hidden = w_fc1.shape[1]

    qkv_way = Course(gather_steps(w_qkv.reshape(rows, -1).astype(LOW), "dp"))
    rest_way = Course(gather_steps(jnp.concatenate([w_out, w_fc1, w_fc2], 1).astype(LOW), "dp"))

    single = jnp.max(segment_ids) == 0
    note = jnp.concatenate(
        [
            timesteps.reshape(-1).astype(F32),
            labels.reshape(-1).astype(F32),
            single.astype(F32)[None],
            jnp.zeros((2 * PIN - 2 * SLOTS - 1,), F32),
        ]
    )
    thin = jnp.concatenate([w_cond[:, :PIN], w_head], 1)
    packet = spread(jnp.concatenate([thin, jnp.broadcast_to(note, (8, 2 * PIN))], 0), "dp")
    packet = packet.reshape(n_dp, rows + 8, 2 * PIN)
    thin_b = packet[:, :rows].reshape(n_dp * rows, 2 * PIN).astype(LOW)
    patch_b, head_b = thin_b[:, :PIN], thin_b[:, PIN:]
    notes = packet[:, rows]
    steps = notes[:, :SLOTS].astype(jnp.int32)
    kinds = notes[:, SLOTS : 2 * SLOTS].astype(jnp.int32).reshape(-1)
    singles = notes[:, 2 * SLOTS] > 0.5

    abar = pick(plan(), steps)
    snr = abar / (1.0 - abar)
    slot_weight = jnp.minimum(snr, GAMMA) / snr
    weight_total = part * jnp.sum(jnp.where(singles[:, None], n_mp * slot_weight[:, :1] / SLOTS, slot_weight))

    time1_b = w_cond[:, PIN : PIN + FREQ].astype(LOW)
    time2_b = w_cond[:, PIN + FREQ : PIN + FREQ + D].astype(LOW)
    table_b = w_cond[:, PIN + FREQ + D :].astype(LOW)
    mod_b = w_mod.reshape(rows, -1).astype(LOW)
    feat_b = time_features(steps.reshape(-1)).astype(LOW)
    slots_all = feat_b.shape[0]
    hidden_t = dot(feat_b, time1_b, ACROSS)
    silu_own = qkv_way.step(jax.nn.silu(hidden_t).astype(LOW))
    silu_t = spread(silu_own, "dp").reshape(n_dp, slots_all, rows)
    silu_t_b = silu_t.transpose(1, 0, 2).reshape(slots_all, n_dp * rows)
    onehot = (kinds[:, None] == jnp.arange(CLASSES, dtype=jnp.int32)).astype(F32)
    cond = dot(silu_t_b, time2_b, ACROSS) + dot(onehot.astype(LOW), table_b, ACROSS)
    silu_c_b = jax.nn.silu(cond).astype(LOW)
    mod_part = rest_way.step(qkv_way.step(dot(silu_c_b, mod_b)))
    mod_cols = jnp.sum(exchange(mod_part.reshape(n_dp, SLOTS, -1), "dp"), 0).reshape(SLOTS, 8, width)
    mod_cols = rest_way.step(mod_cols)
    part_slots = segment_ids[::part]
    outgoing = jnp.sum(
        jnp.where((part_slots[:, None] == jnp.arange(SLOTS))[:, :, None, None], mod_cols[None], 0.0), 1
    )
    mods = exchange(outgoing, "mp").transpose(1, 0, 2).reshape(8, n_mp * width)
    slot = lax.dynamic_index_in_dim(part_slots, rank, 0, keepdims=False)

    my_row = lambda a: lax.dynamic_index_in_dim(a, me, 0, keepdims=False)
    my_slot = lambda a: lax.dynamic_index_in_dim(my_row(a), slot, 0, keepdims=False)
    abar_tok, weight_tok = my_slot(abar), my_slot(slot_weight)
    lat = lax.dynamic_slice_in_dim(latents, rank * part, part, 0)
    noi = lax.dynamic_slice_in_dim(noise, rank * part, part, 0)
    noisy_b = (jnp.sqrt(abar_tok) * lat + jnp.sqrt(1.0 - abar_tok) * noi).astype(LOW)
    picks = place_select(single, part, rank).astype(LOW)
    left = jnp.concatenate([noisy_b, picks, picks, picks], 1)
    x_in = dot(left, jnp.concatenate([patch_b.T, *thirds(place_table())], 0))
    unit1, inv1 = normalize(x_in)
    h_in = gather_rows((unit1 * (1.0 + mods[1]) + mods[0]).astype(LOW), "mp")

    alone = single.astype(jnp.int32)[None]
    qkv_b = qkv_way.finish()
    qkv = dot(h_in, qkv_b).astype(LOW)
    rest = rest_way.finish()
    out_b, fc1_b, fc2_b = rest[:, :width], rest[:, width : width + hidden], rest[:, width + hidden :]
    mixed_b, totals = attend(alone, after(qkv, rest), part)
    attn = scatter_sum(dot(mixed_b, out_b, ACROSS), "mp")
    x_mid = x_in + mods[2] * attn
    unit2, inv2 = normalize(x_mid)
    h_mid = gather_rows((unit2 * (1.0 + mods[4]) + mods[3]).astype(LOW), "mp")
    upper = dot(h_mid, fc1_b)
    act_b = jax.nn.gelu(upper, approximate=False).astype(LOW)
    mlp = scatter_sum(dot(act_b, fc2_b, ACROSS), "mp")
    x_out = x_mid + mods[5] * mlp
    unit3, inv3 = normalize(x_out)
    h_fin = (unit3 * (1.0 + mods[7]) + mods[6]).astype(LOW)
    pred = dot(h_fin, head_b)
    diff = pred - noi
    loss_part = weight_tok * jnp.sum(diff * diff)

    d_pred = (2.0 * diff * (weight_tok / weight_total)).astype(LOW)
    d_head = dot(h_fin, d_pred, DOWN)
    d_out, d_shiftf, d_scalef = norm_back(dot(d_pred, head_b, ACROSS), unit3, inv3, mods[7])
    d_gate2 = jnp.sum(d_out * mlp, 0)
    d_mlp = gather_rows((d_out * mods[5]).astype(LOW), "mp")
    moms = [m.reshape(rows, -1) for m in (mom_mod, mom_fc1, mom_fc2, mom_qkv, mom_out)]
    old = jnp.concatenate([m.astype(LOW) for m in moms], 1)
    old = lax.all_gather(after(old, mixed_b), "dp", axis=0, tiled=True)
    d_mlp = after(d_mlp, old)
    d_fc2 = dot(d_mlp, act_b, DOWN)
    d_act = dot(d_mlp, fc2_b)
    _, gelu_back = jax.vjp(lambda v: jax.nn.gelu(v, approximate=False), upper)
    d_upper = gelu_back(d_act)[0].astype(LOW)
    d_fc1 = dot(h_mid, d_upper, DOWN)
    fc_way = Course(sum_steps(jnp.concatenate([d_fc1, d_fc2], 1), "dp"))
    d_hmid = scatter_sum(dot(d_upper, fc1_b, ACROSS), "mp")
    dx_mid, d_shift2, d_scale2 = norm_back(d_hmid, unit2, inv2, mods[4])
    d_mid = d_out + dx_mid
    d_gate1 = jnp.sum(d_mid * attn, 0)
    d_attn = gather_rows((d_mid * mods[2]).astype(LOW), "mp")
    d_outw = dot(d_attn, mixed_b, DOWN)
    d_mixed = fc_way.step(dot(d_attn, out_b).astype(LOW))
    d_qkv = fc_way.step(attend_back(alone, qkv, d_mixed, totals, part))
    d_wqkv = dot(h_in, d_qkv, DOWN)
    at_way = Course(sum_steps(jnp.concatenate([d_wqkv, d_outw], 1), "dp"))
    d_hin = fc_way.step(scatter_sum(dot(d_qkv, qkv_b, ACROSS), "mp"))
    sum_fc = fc_way.finish()
    fc_way = Course(gather_steps(sum_fc.astype(LOW), "dp"))
    dx_in, d_shift1, d_scale1 = norm_back(d_hin, unit1, inv1, mods[1])
    d_x = (d_mid + dx_in).astype(LOW)
    d_patch = dot(d_x, noisy_b, DOWN)

    d_mods = jnp.stack([d_shift1, d_scale1, d_gate1, d_shift2, d_scale2, d_gate2, d_shiftf, d_scalef])
    blocks = exchange(d_mods.reshape(8, n_mp, width).transpose(1, 0, 2), "mp")
    first_only = (jnp.arange(SLOTS) == 0)[:, None, None]
    d_mod = jnp.where(single, jnp.where(first_only, jnp.sum(blocks, 0, keepdims=True), 0.0), blocks)
    d_mod = d_mod.astype(LOW).reshape(SLOTS, 8 * width)
    bundle = at_way.step(jnp.concatenate([d_mod, silu_c_b.reshape(SLOTS, -1)], 1))
    bundle = spread(bundle, "dp").reshape(n_dp, SLOTS, -1)
    d_mod_all = bundle[:, :, : 8 * width].reshape(slots_all, 8 * width)
    silu_c_all = (
        bundle[:, :, 8 * width :].reshape(n_dp, slots_all, rows).transpose(0, 2, 1).reshape(-1, slots_all)
    )
    g_mod = dot(silu_c_b, d_mod_all, DOWN)
    d_cond_part = dot(d_mod_all, mod_b, ACROSS) * silu_slope(cond)
    d_silu_t_part = lax.dot_general(d_cond_part, time2_b.astype(F32), ALONG, precision=HIGH)
    thick = jnp.concatenate([d_silu_t_part.T, d_patch, d_head], 1)
    thick = fc_way.step(at_way.step(thick))
    thick = jnp.sum(exchange(thick.reshape(n_dp, rows, -1), "dp"), 0)
    thick = sum_all(jnp.concatenate([thick, d_cond_part.T], 1), "mp")
    d_silu_t = thick[:, :slots_all].T
    g_patch = thick[:, slots_all : slots_all + PIN]
    g_head = thick[:, slots_all + PIN : slots_all + 2 * PIN]
    d_cond = thick[:, slots_all + 2 * PIN :]
    g_table = lax.dot_general(d_cond, onehot, ALONG, precision=HIGH)
    g_time2 = lax.dot_general(d_cond, silu_t_b.astype(F32), ALONG, precision=HIGH)
    d_hidden = d_silu_t * silu_slope(hidden_t)
    g_time1 = lax.dot_general(d_hidden, feat_b.astype(F32), DOWN, precision=HIGH)
    g_cond = jnp.concatenate([g_patch, g_time1, g_time2, g_table], 1)

    sum_at = at_way.finish()
    at_way = Course(gather_steps(sum_at.astype(LOW), "dp"))

    square = lambda g: jnp.sum(g * g)
    split_sq = square(sum_fc) + square(sum_at) + square(g_mod)
    shared = sum_all(jnp.stack([split_sq, loss_part]), "mp")
    tally = jnp.stack([shared[0] + square(g_head) + square(g_cond), shared[1]])
    tally = fc_way.step(at_way.step(jnp.broadcast_to(tally[:, None], (2, 128))))
    tally = jnp.sum(spread(tally, "dp"), 0)
    grad_norm = jnp.sqrt(tally[0, 0])
    loss_sum = tally[1, 0]
    coef = jnp.minimum(1.0, CLIP / (grad_norm + 1e-06))

    all_fc = fc_way.finish()
    all_at = at_way.finish()
    near = me % 2
    own = ((me // 2) * (2 * rows))[None].astype(jnp.int32)
    factor = coef[None]
    rows_of_block = functools.partial(muon_rows, own, 2 * rows, factor, old)

    def one_mod():
        return rows_of_block(0, (silu_c_all, d_mod_all), 0, 8 * width, (0, 8 * width))

    def both_fc():
        base = 8 * width // hidden
        return jnp.concatenate(
            [rows_of_block(base + k, (all_fc,), k, hidden, (0, hidden)) for k in range(2)], 1
        )

    last = (8 * width + 2 * hidden) // (4 * width)

    def one_qkv():
        return rows_of_block(last, (all_at,), 0, 4 * width, (0, 3 * width))

    def one_out():
        mine = rows_of_block(last, (all_at,), 0, 4 * width, (3 * width, 4 * width))
        return jnp.pad(mine, ((0, 0), (0, 2 * width)))

    def shared_rows(both):
        mine = lax.dynamic_slice_in_dim(both, near * rows, rows, 0)
        theirs = lax.dynamic_slice_in_dim(both, (1 - near) * rows, rows, 0)
        theirs = swap(theirs, "dp", 1)
        return jnp.where(near == 0, mine, theirs), jnp.where(near == 0, theirs, mine)

    u_mod, u_fc = shared_rows(lax.cond(near == 0, one_mod, both_fc))
    u_qkv, u_out = shared_rows(lax.cond(near == 0, one_qkv, one_out))
    masters = (w_qkv, w_out, w_fc1, w_fc2, w_mod)
    old_moms = (mom_qkv, mom_out, mom_fc1, mom_fc2, mom_mod)
    fresh = (sum_at[:, : 3 * width], sum_at[:, 3 * width :], sum_fc[:, :hidden], sum_fc[:, hidden:], g_mod)
    updates = (u_qkv, u_out[:, :width], u_fc[:, :hidden], u_fc[:, hidden:], u_mod)
    new_weights = [
        w * (1.0 - LR_MUON * DECAY) - LR_MUON * u.astype(F32).reshape(w.shape) for w, u in zip(masters, updates)
    ]
    new_moms = [MU * m + coef * g.reshape(m.shape) for m, g in zip(old_moms, fresh)]

    adam_out = []
    for master, first, second, grad in (
        (w_head, first_head, second_head, g_head),
        (w_cond, first_cond, second_cond, g_cond),
    ):
        clipped = coef * grad
        first = BETA_ONE * first + (1.0 - BETA_ONE) * clipped
        second = BETA_TWO * second + (1.0 - BETA_TWO) * clipped * clipped
        update = first / (1.0 - BETA_ONE**STEP) / (jnp.sqrt(second / (1.0 - BETA_TWO**STEP)) + EPS_ADAM)
        adam_out.append((master - LR_ADAM * (update + DECAY * master), first, second))
    return (
        *new_weights,
        adam_out[0][0],
        adam_out[1][0],
        *new_moms,
        adam_out[0][1],
        adam_out[0][2],
        adam_out[1][1],
        adam_out[1][2],
        loss_sum,
        weight_total,
        grad_norm,
    )


def solution(mesh):
    row, wide, cube = P("dp", None), P("dp", "mp"), P("dp", None, "mp")
    in_specs = (
        *(row, row, P("dp"), row, row),
        *(cube, wide, wide, wide, cube, row, row),
        *(cube, wide, wide, wide, cube),
        *(row, row, row, row),
    )
    out_specs = (
        *(cube, wide, wide, wide, cube, row, row),
        *(cube, wide, wide, wide, cube),
        *(row, row, row, row),
        *(P(), P(), P()),
    )
    return jax.shard_map(body, mesh=mesh, in_specs=in_specs, out_specs=out_specs, check_vma=False)
```

```python
import functools
import math

import jax
import jax.numpy as jnp
from jax import lax
from jax.experimental import pallas as pl
from jax.experimental.pallas import tpu as pltpu
from jax.sharding import PartitionSpec as P

SIDE = 32
D = 768
HEAD_DIM = 64
CLASSES = 1001
FREQ = 256
PIN = 16
STEP = 10
SLOTS = 4

HIGH = lax.Precision.HIGHEST
GAMMA = 5.0
CLIP = 0.05
MU = 0.95
LR_MUON = 0.1
DECAY = 0.01
BETA_ONE = 0.9
BETA_TWO = 0.95
LR_ADAM = 0.08
EPS_ADAM = 1e-08
NS_COEF = (3.4445, -4.775, 2.0315)
NS_SHIFT = (0.0, 0.1, 0.5, 0.8, 0.8)
ACROSS = (((1,), (1,)), ((), ()))
DOWN = (((0,), (0,)), ((), ()))
ALONG = (((1,), (0,)), ((), ()))
LOW = jnp.bfloat16
F32 = jnp.float32


def dot(a, b, dims=ALONG):
    return lax.dot_general(a, b, dims, preferred_element_type=F32)


def order_of(size):
    order, bit = [0], size // 2
    while bit:
        order += [o ^ bit for o in order]
        bit //= 2
    return order


def swap(x, axis, bit):
    size = lax.axis_size(axis)
    return lax.ppermute(x, axis, [(i, i ^ bit) for i in range(size)])


def after(x, *others):
    return lax.optimization_barrier((x,) + others)[0]


class Course:
    def __init__(self, steps):
        self.steps = steps
        self.result = None
        self.flight = next(steps, None)

    def step(self, x, start=None):
        arrived = self.flight
        if arrived is None:
            return x
        x = after(x, arrived)
        try:
            self.flight = self.steps.send((arrived, start))
        except StopIteration as stop:
            self.flight, self.result = None, stop.value
        return x

    def finish(self):
        while self.flight is not None:
            self.step(jnp.zeros((), F32))
        return self.result


def late(x, start):
    return x if start is None else after(x, start)


def gather_steps(x, axis):
    bit = lax.axis_size(axis) // 2
    start, last = None, 1
    while bit > last:
        other, start = yield swap(late(x, start), axis, bit)
        x = jnp.concatenate([x, other], 0)
        bit //= 2
    _, start = yield x
    other, start = yield swap(late(x, start), axis, bit)
    return x, other


def joined(pair):
    return jnp.concatenate(pair, 0)


def sum_steps(keep, send, axis):
    bit, size = 1, lax.axis_size(axis)
    other, start = yield swap(send, axis, bit)
    total = keep + other.astype(F32)
    while bit < size // 2:
        bit *= 2
        half = total.shape[0] // 2
        other, start = yield swap(late(total[half:].astype(LOW), start), axis, bit)
        total = total[:half] + other.astype(F32)
    return total


def sum_all(x, axis):
    bit = 1
    while bit < lax.axis_size(axis):
        x = x + swap(x, axis, bit)
        bit *= 2
    return x


def parts_of(h):
    two = swap(h, "mp", 2)
    one = swap(h, "mp", 1)
    return [h, one, two, swap(two, "mp", 1)]


def parts_sum(even, odd):
    near = swap(odd, "mp", 1)
    send = (even[1] + near[1].astype(F32)).astype(LOW)
    return [even, near, swap(send, "mp", 2)], send


def turned_over(v, me):
    size, bit = v.shape[-2], 1
    lead, k = v.shape[:-2], v.shape[-1]
    while bit < size:
        pair = v.reshape(lead + (size // (2 * bit), 2, bit, k))
        flipped = jnp.concatenate([pair[..., 1:, :, :], pair[..., :1, :, :]], -3)
        v = jnp.where((me // bit) % 2 == 1, flipped, pair).reshape(lead + (size, k))
        bit *= 2
    return v


def to_local(v, me, size):
    blocks = turned_over(v.reshape(v.shape[:-1] + (size, v.shape[-1] // size)), me)
    return jnp.concatenate([blocks[..., o, :] for o in order_of(size)], -1)


def from_local(v, me, size):
    blocks = v.reshape(v.shape[:-1] + (size, v.shape[-1] // size))
    order = order_of(size)
    return turned_over(jnp.stack([blocks[..., order.index(k), :] for k in range(size)], -2), me)


def spread(x, axis):
    size = math.prod(lax.axis_size(a) for a in ((axis,) if isinstance(axis, str) else axis))
    copies = jnp.broadcast_to(x[None], (size,) + x.shape)
    return lax.all_to_all(copies, axis, 0, 0, tiled=True)


def exchange(x, axis):
    return lax.all_to_all(x, axis, 0, 0, tiled=True)


def plan():
    betas = jnp.linspace(0.0001, 0.02, 1000, dtype=F32)
    return jnp.cumprod(1.0 - betas)


def pick(table, index):
    grid = jnp.arange(table.shape[0], dtype=jnp.int32)
    return jnp.sum(jnp.where(index[..., None] == grid, table, 0.0), -1)


def normalize(x):
    cent = x - jnp.mean(x, -1, keepdims=True)
    inv = lax.rsqrt(jnp.mean(cent * cent, -1, keepdims=True) + 1e-06)
    return cent * inv, inv


def norm_back(grad, unit, inv, scale):
    d_shift = jnp.sum(grad, 0, keepdims=True)
    d_scale = jnp.sum(grad * unit, 0, keepdims=True)
    g = grad * (1.0 + scale)
    dx = inv * (g - jnp.mean(g, -1, keepdims=True) - unit * jnp.mean(g * unit, -1, keepdims=True))
    return dx, d_shift, d_scale


def place_table(column):
    quarter = D // 4
    omega = 1.0 / 10000.0 ** ((column % quarter).astype(F32) / quarter)
    angle = jnp.arange(SIDE, dtype=F32)[:, None] * omega
    wave = jnp.where((column // quarter) % 2 == 0, jnp.sin(angle), jnp.cos(angle))
    down = column < D // 2
    return jnp.concatenate([jnp.where(down, wave, 0.0), jnp.where(down, 0.0, wave)], 0)


def place_select(single, part, rank):
    local = jnp.arange(part, dtype=jnp.int32)
    full = rank * part + local
    half = SIDE // 2
    down = jnp.where(single, full // SIDE, local // half)
    across = jnp.where(single, full % SIDE, local % half)
    grid = jnp.arange(SIDE, dtype=jnp.int32)
    return jnp.concatenate([down[:, None] == grid, across[:, None] == grid], 1)


def thirds(x):
    high = x.astype(LOW)
    rest = x - high.astype(F32)
    mid = rest.astype(LOW)
    return high, mid, (rest - mid.astype(F32)).astype(LOW)


def time_features(steps):
    half = FREQ // 2
    freqs = jnp.exp(-math.log(10000.0) * jnp.arange(half, dtype=F32) / half)
    angles = steps.astype(F32)[:, None] * freqs
    return jnp.concatenate([jnp.cos(angles), jnp.sin(angles)], -1)


def silu_slope(x):
    s = jax.nn.sigmoid(x)
    return s * (1.0 + x * (1.0 - s))


def call(kernel, name, outs, *args, scalars=0, scratch=(), flops=0):
    smem, vmem = pl.BlockSpec(memory_space=pltpu.SMEM), pl.BlockSpec(memory_space=pltpu.VMEM)
    size = sum(math.prod(o[0]) * jnp.dtype(o[1]).itemsize for o in outs)
    return pl.pallas_call(
        kernel,
        out_shape=[jax.ShapeDtypeStruct(*o) for o in outs],
        in_specs=[smem] * scalars + [vmem] * (len(args) - scalars),
        out_specs=[vmem] * len(outs),
        scratch_shapes=[pltpu.VMEM(*t) for t in scratch],
        compiler_params=pltpu.CompilerParams(vmem_limit_bytes=48 * 2**20),
        cost_estimate=pl.CostEstimate(flops=1, bytes_accessed=1, transcendentals=0),
        name=name,
    )(*args)


def turned(x):
    return x.astype(F32).T.astype(x.dtype)


def added(even_ref, near_ref, far_ref):
    return even_ref[0] + near_ref[0].astype(F32) + far_ref[...].astype(F32)


def enter_kernel(x_ref, mods_ref, h_ref):
    unit, _ = normalize(x_ref[...])
    h_ref[...] = (unit * (1.0 + mods_ref[1:2, :]) + mods_ref[0:1, :]).astype(LOW)


def middle_kernel(even_ref, near_ref, far_ref, x_ref, mods_ref, attn_ref, mid_ref, h_ref):
    attn = added(even_ref, near_ref, far_ref)
    attn_ref[...] = attn
    mid = x_ref[...] + mods_ref[2:3, :] * attn
    mid_ref[...] = mid
    unit, _ = normalize(mid)
    h_ref[...] = (unit * (1.0 + mods_ref[4:5, :]) + mods_ref[3:4, :]).astype(LOW)


def final_kernel(
    scale_ref, even_ref, near_ref, far_ref, mid_ref, mods_ref, head_ref, noise_ref,
    out_ref, mlp_ref, head_grad_ref, sums_ref, loss_ref,
):
    mlp = added(even_ref, near_ref, far_ref)
    unit, inv = normalize(mid_ref[...] + mods_ref[5:6, :] * mlp)
    h = (unit * (1.0 + mods_ref[7:8, :]) + mods_ref[6:7, :]).astype(LOW)
    diff = dot(h, head_ref[...], ACROSS) - noise_ref[...]
    loss = jnp.sum(jnp.sum(diff * diff, axis=1, keepdims=True), axis=0, keepdims=True)
    loss_ref[...] = jnp.broadcast_to(scale_ref[0] * loss, loss_ref.shape)
    d_pred = (2.0 * diff * scale_ref[1]).astype(LOW)
    head_grad_ref[...] = dot(d_pred, h, DOWN)
    d_out, d_shift, d_scale = norm_back(dot(d_pred, head_ref[...]), unit, inv, mods_ref[7:8, :])
    out_ref[...] = d_out
    mlp_ref[...] = (d_out * mods_ref[5:6, :]).astype(LOW)
    sums_ref[0:1, :] = jnp.sum(d_out * mlp, 0, keepdims=True)
    sums_ref[1:2, :] = d_shift
    sums_ref[2:3, :] = d_scale


def turn_kernel(
    even_ref, near_ref, far_ref, mid_ref, out_ref, attn_ref, mods_ref, d_mid_ref, d_attn_ref, sums_ref
):
    unit, inv = normalize(mid_ref[...])
    dx, d_shift, d_scale = norm_back(added(even_ref, near_ref, far_ref), unit, inv, mods_ref[4:5, :])
    d_mid = out_ref[...] + dx
    d_mid_ref[...] = d_mid
    d_attn_ref[...] = (d_mid * mods_ref[2:3, :]).astype(LOW)
    sums_ref[0:1, :] = jnp.sum(d_mid * attn_ref[...], 0, keepdims=True)
    sums_ref[1:2, :] = d_shift
    sums_ref[2:3, :] = d_scale


def leave_kernel(
    even_ref, near_ref, far_ref, x_ref, d_mid_ref, mods_ref, noisy_ref, mid_sums_ref, end_sums_ref,
    patch_ref, sums_ref,
):
    unit, inv = normalize(x_ref[...])
    dx, d_shift, d_scale = norm_back(added(even_ref, near_ref, far_ref), unit, inv, mods_ref[1:2, :])
    patch_ref[...] = dot(noisy_ref[...], (d_mid_ref[...] + dx).astype(LOW), DOWN)
    sums_ref[0:1, :] = d_shift
    sums_ref[1:2, :] = d_scale
    sums_ref[2:5, :] = mid_sums_ref[0:3, :]
    sums_ref[5:8, :] = end_sums_ref[0:3, :]


def attend_kernel(
    single_ref, h0_ref, h1_ref, h2_ref, h3_ref, w_ref, o_ref,
    qkv_ref, total_ref, mixed_ref, even_ref, odd_ref, vt_ref,
):
    part = h0_ref.shape[0]
    width = mixed_ref.shape[1]
    for j, ref in enumerate((h0_ref, h1_ref, h2_ref, h3_ref)):
        qkv_ref[j * part : (j + 1) * part, :] = dot(ref[...], w_ref[...]).astype(LOW)
    vt_ref[...] = turned(qkv_ref[:, 2 * width :])

    def run(i, keys):
        mine = pl.ds(pl.multiple_of(i * part, part), part)
        outs = []
        for h in range(width // HEAD_DIM):
            lo = h * HEAD_DIM
            q = qkv_ref[mine, lo : lo + HEAD_DIM] * HEAD_DIM**-0.5
            k = qkv_ref[keys, width + lo : width + lo + HEAD_DIM]
            s = dot(k, q, ACROSS)
            top = jnp.max(s, axis=0, keepdims=True)
            e = jnp.exp(s - top)
            z = jnp.sum(e, axis=0, keepdims=True)
            total_ref[h : h + 1, mine] = top + jnp.log(z)
            outs.append(dot(vt_ref[lo : lo + HEAD_DIM, keys], (e * (1.0 / z)).astype(LOW)))
        mixed_ref[mine, :] = jnp.concatenate(outs, 0).T.astype(LOW)

    def block(i, carry):
        mine = pl.ds(pl.multiple_of(i * part, part), part)

        @pl.when(single_ref[0] == 1)
        def _():
            run(i, slice(None))

        @pl.when(single_ref[0] != 1)
        def _():
            run(i, mine)

        return carry

    lax.fori_loop(0, 4, block, 0)
    for j in range(4):
        term = dot(mixed_ref[j * part : (j + 1) * part, :], o_ref[...], ACROSS)
        if j % 2 == 0:
            even_ref[j // 2] = term
        else:
            odd_ref[j // 2] = term.astype(LOW)


def attend_back_kernel(
    single_ref, qkv_ref, total_ref, d0_ref, d1_ref, d2_ref, d3_ref, w_ref, o_ref,
    grad_ref, even_ref, odd_ref, kt_ref, dk_ref, dv_ref, g_ref,
):
    part = d0_ref.shape[0]
    width = qkv_ref.shape[1] // 3
    heads = width // HEAD_DIM
    for j, ref in enumerate((d0_ref, d1_ref, d2_ref, d3_ref)):
        g_ref[j * part : (j + 1) * part, :] = dot(ref[...], o_ref[...]).astype(LOW)
    kt_ref[...] = turned(qkv_ref[:, width : 2 * width] * HEAD_DIM**-0.5)
    dk_ref[...] = jnp.zeros_like(dk_ref)
    dv_ref[...] = jnp.zeros_like(dv_ref)

    def run(i, keys):
        mine = pl.ds(pl.multiple_of(i * part, part), part)
        outs = []
        for h in range(heads):
            lo = h * HEAD_DIM
            q = qkv_ref[mine, lo : lo + HEAD_DIM] * HEAD_DIM**-0.5
            k = qkv_ref[keys, width + lo : width + lo + HEAD_DIM]
            v = qkv_ref[keys, 2 * width + lo : 2 * width + lo + HEAD_DIM]
            g = g_ref[mine, lo : lo + HEAD_DIM]
            p = jnp.exp(dot(k, q, ACROSS) - total_ref[h : h + 1, mine])
            dp = dot(v, g, ACROSS)
            delta = jnp.sum(dp * p, axis=0, keepdims=True)
            ds = (p * (dp - delta)).astype(LOW)
            dv_ref[h, keys, :] += dot(p.astype(LOW), g)
            dk_ref[h, keys, :] += dot(ds, q)
            outs.append(dot(kt_ref[lo : lo + HEAD_DIM, keys], ds))
        grad_ref[mine, :width] = jnp.concatenate(outs, 0).T.astype(LOW)

    def block(i, carry):
        @pl.when(single_ref[0] == 1)
        def _():
            run(i, slice(None))

        @pl.when(single_ref[0] != 1)
        def _():
            run(i, pl.ds(pl.multiple_of(i * part, part), part))

        return carry

    lax.fori_loop(0, 4, block, 0)
    for h in range(heads):
        lo = h * HEAD_DIM
        grad_ref[:, width + lo : width + lo + HEAD_DIM] = dk_ref[h].astype(LOW)
        grad_ref[:, 2 * width + lo : 2 * width + lo + HEAD_DIM] = dv_ref[h].astype(LOW)
    for j in range(4):
        term = dot(grad_ref[j * part : (j + 1) * part, :], w_ref[...], ACROSS)
        if j % 2 == 0:
            even_ref[j // 2] = term
        else:
            odd_ref[j // 2] = term.astype(LOW)


def halves(keep_ref, send_ref, columns, value):
    half = keep_ref.shape[0]
    keep_ref[:, columns] = value[:half]
    send_ref[:, columns] = value[half:].astype(LOW)


def attend_grads_kernel(h0, h1, h2, h3, grad_ref, d0, d1, d2, d3, mixed_ref, keep_ref, send_ref):
    part, width = h0.shape[0], mixed_ref.shape[1]
    rows = lambda j: slice(j * part, (j + 1) * part)
    halves(
        keep_ref, send_ref, slice(0, 3 * width),
        sum(dot(h[...], grad_ref[rows(j), :], DOWN) for j, h in enumerate((h0, h1, h2, h3))),
    )
    halves(
        keep_ref, send_ref, slice(3 * width, 4 * width),
        sum(dot(d[...], mixed_ref[rows(j), :], DOWN) for j, d in enumerate((d0, d1, d2, d3))),
    )


def feed_kernel(h0, h1, h2, h3, w_ref, act_ref, slope_ref, even_ref, odd_ref):
    part, hidden = h0.shape[0], act_ref.shape[1]
    for j, h in enumerate((h0, h1, h2, h3)):
        rows = slice(j * part, (j + 1) * part)
        upper = dot(h[...], w_ref[:, :hidden])
        gate = 0.5 * (1.0 + lax.erf(upper * 0.5**0.5))
        act = (upper * gate).astype(LOW)
        act_ref[rows, :] = act
        slope_ref[rows, :] = gate + upper * jnp.exp(-0.5 * upper * upper) * (2.0 * math.pi) ** -0.5
        term = dot(act, w_ref[:, hidden:], ACROSS)
        if j % 2 == 0:
            even_ref[j // 2] = term
        else:
            odd_ref[j // 2] = term.astype(LOW)


def feed_back_kernel(d0, d1, d2, d3, slope_ref, w_ref, upper_ref, even_ref, odd_ref):
    part, hidden = d0.shape[0], slope_ref.shape[1]
    for j, d in enumerate((d0, d1, d2, d3)):
        rows = slice(j * part, (j + 1) * part)
        d_upper = (dot(d[...], w_ref[:, hidden:]) * slope_ref[rows, :]).astype(LOW)
        upper_ref[rows, :] = d_upper
        term = dot(d_upper, w_ref[:, :hidden], ACROSS)
        if j % 2 == 0:
            even_ref[j // 2] = term
        else:
            odd_ref[j // 2] = term.astype(LOW)


def feed_grads_kernel(h0, h1, h2, h3, x_ref, keep_ref, send_ref):
    part = h0.shape[0]
    value = sum(
        dot(h[...], x_ref[j * part : (j + 1) * part, :], DOWN) for j, h in enumerate((h0, h1, h2, h3))
    )
    halves(keep_ref, send_ref, slice(None), value)


def muon_kernel(columns, span, order_ref, coef_ref, plan_ref, mom_ref, *refs):
    grads, (out_ref, x_ref, b_ref, e_ref, r_ref) = refs[:-5], refs[-5:]
    third = NS_COEF[2]
    size, width = x_ref.shape
    count, pairs = mom_ref.shape[2], mom_ref.shape[0]
    coef = coef_ref[0]
    spans = [slice(i, min(i + size, width)) for i in range(0, width, size)]

    squares = jnp.zeros((1, width), F32)
    for place in range(2 * pairs):
        true = order_ref[place]
        if len(grads) == 1:
            grad = grads[0][true, :, slice(*span)].astype(F32)
        elif grads[0].shape[0] == 2 * pairs:
            grad = dot(grads[0][true], grads[1][...])
        else:
            grad = grads[place // pairs][place % pairs].astype(F32)
        mom = mom_ref[lax.shift_right_logical(true, 1), place // pairs, :, slice(*columns)]
        x = MU * mom.astype(F32) + coef * grad
        x_ref[place * count : (place + 1) * count, :] = x
        squares = squares + jnp.sum(x * x, axis=0, keepdims=True)
    inv = 1.0 / (jnp.sqrt(jnp.sum(squares, axis=1, keepdims=True)) + 1e-07)
    x_ref[...] = x_ref[...] * inv
    b_ref[...] = x_ref[...].astype(LOW)

    def gram(shift):
        e = sum(dot(b_ref[:, span], b_ref[:, span], ACROSS) for span in spans)
        row = lax.broadcasted_iota(jnp.int32, e.shape, 0)
        column = lax.broadcasted_iota(jnp.int32, e.shape, 1)
        e = e - jnp.where(row == column, shift, 0.0)
        e_ref[...] = e
        r_ref[...] = e.astype(LOW)

    def turn(i, carry):
        centre, slope = plan_ref[i, 0], plan_ref[i, 1]
        gram(plan_ref[i, 2])
        r_ref[...] = (slope * e_ref[...] + third * dot(r_ref[...], r_ref[...])).astype(LOW)
        for span in spans:
            x = centre * x_ref[:, span] + dot(r_ref[...], b_ref[:, span])
            x_ref[:, span] = x
            b_ref[:, span] = x.astype(LOW)
        return carry

    last = len(NS_SHIFT) - 1
    lax.fori_loop(0, last, turn, 0)
    gram(plan_ref[last, 2])
    both = [slice(0, count), slice(pairs * count, (pairs + 1) * count)]
    e = jnp.concatenate([e_ref[own, :] for own in both], 0)
    poly = (plan_ref[last, 1] * e + third * dot(e.astype(LOW), r_ref[...])).astype(LOW)
    scaled = 0.2 * math.sqrt(max(size, width))
    for span in spans:
        x = jnp.concatenate([x_ref[own, span] for own in both], 0)
        x = scaled * (plan_ref[last, 0] * x + dot(poly, b_ref[:, span]))
        out_ref[0, :, span] = x[:count].astype(LOW)
        out_ref[1, :, span] = x[count:].astype(LOW)


def muon_rows(order, coef, old, block, columns, grads, span=None):
    pairs, _, count, _ = old.shape
    size = 2 * pairs * count
    width = columns[1] - columns[0]
    first, second, third = NS_COEF
    plan = [[first + second * s + third * s * s, second + 2.0 * third * s, s] for s in NS_SHIFT]
    smem, vmem = pl.BlockSpec(memory_space=pltpu.SMEM), pl.BlockSpec(memory_space=pltpu.VMEM)
    return pl.pallas_call(
        functools.partial(muon_kernel, columns, span),
        grid=(1,),
        out_shape=jax.ShapeDtypeStruct((2, count, width), LOW),
        in_specs=[smem, smem, smem, pl.BlockSpec((pairs, 2, count, block[0]), lambda i: (0, 0, 0, block[1]))]
        + [vmem] * len(grads),
        out_specs=vmem,
        scratch_shapes=[
            pltpu.VMEM((size, width), F32),
            pltpu.VMEM((size, width), LOW),
            pltpu.VMEM((size, size), F32),
            pltpu.VMEM((size, size), LOW),
        ],
        compiler_params=pltpu.CompilerParams(vmem_limit_bytes=48 * 2**20),
        cost_estimate=pl.CostEstimate(flops=1, bytes_accessed=1, transcendentals=0),
        name="muon",
    )(order, coef, jnp.array(plan, F32), old, *grads)


def finish_kernel(
    near_ref, coef_ref, own_a, got_a, own_b, got_b, g_at, g_fc1, g_fc2, g_mod,
    w_qkv, w_out, w_fc1, w_fc2, w_mod, m_qkv, m_out, m_fc1, m_fc2, m_mod,
    n_qkv, n_out, n_fc1, n_fc2, n_mod, k_qkv, k_out, k_fc1, k_fc2, k_mod,
):
    width, hidden = w_out.shape[1], w_fc1.shape[1]
    coef = coef_ref[0]
    mine = near_ref[0] == 0

    def put(place, weight, mom, new, kept, update, grad):
        new[place] = weight[place] * (1.0 - LR_MUON * DECAY) - LR_MUON * update
        kept[place] = MU * mom[place] + coef * grad

    a, b = own_a[...].astype(F32), got_a[...].astype(F32)
    u_mod, u_fc = jnp.where(mine, a, b), jnp.where(mine, b, a)
    a, b = own_b[...].astype(F32), got_b[...].astype(F32)
    u_qkv, u_out = jnp.where(mine, a, b), jnp.where(mine, b, a)[:, :width]
    for k in range(3):
        span = slice(k * width, (k + 1) * width)
        put(k, w_qkv, m_qkv, n_qkv, k_qkv, u_qkv[:, span], g_at[:, span])
    for k in range(8):
        span = slice(k * width, (k + 1) * width)
        put((slice(None), k), w_mod, m_mod, n_mod, k_mod, u_mod[:, span], g_mod[:, span])
    put(slice(None), w_out, m_out, n_out, k_out, u_out, g_at[:, 3 * width :])
    put(slice(None), w_fc2, m_fc2, n_fc2, k_fc2, u_fc[:, :hidden], g_fc2[...])
    put(slice(None), w_fc1, m_fc1, n_fc1, k_fc1, u_fc[:, hidden:], g_fc1[...])


def finish(near, coef, flats, weights, moms):
    rows = flats[0].shape[0]
    step = rows // 2 if rows % 32 == 0 else rows
    smem = pl.BlockSpec(memory_space=pltpu.SMEM)

    def block(a):
        if a.ndim == 2:
            return pl.BlockSpec((step, a.shape[1]), lambda i: (i, 0))
        if a.shape[0] == rows:
            return pl.BlockSpec((step,) + a.shape[1:], lambda i: (i, 0, 0))
        return pl.BlockSpec((a.shape[0], step, a.shape[2]), lambda i: (0, i, 0))

    first = lambda a: a.transpose(1, 0, 2)
    arrays = [first(weights[0]), *weights[1:], first(moms[0]), *moms[1:]]
    outs = pl.pallas_call(
        finish_kernel,
        grid=(rows // step,),
        out_shape=[jax.ShapeDtypeStruct(a.shape, F32) for a in arrays],
        in_specs=[smem, smem] + [block(a) for a in (*flats, *arrays)],
        out_specs=[block(a) for a in arrays],
        compiler_params=pltpu.CompilerParams(vmem_limit_bytes=48 * 2**20),
        name="finish",
    )(near, coef, *flats, *arrays)
    return [first(outs[0]), *outs[1:5]], [first(outs[5]), *outs[6:]]


def body(
    latents,
    noise,
    segment_ids,
    timesteps,
    labels,
    w_qkv,
    w_out,
    w_fc1,
    w_fc2,
    w_mod,
    w_head,
    w_cond,
    mom_qkv,
    mom_out,
    mom_fc1,
    mom_fc2,
    mom_mod,
    first_head,
    second_head,
    first_cond,
    second_cond,
):
    n_dp, n_mp = lax.axis_size("dp"), lax.axis_size("mp")
    me, rank = lax.axis_index("dp"), lax.axis_index("mp")
    near = me % 2
    tokens = latents.shape[0]
    part = tokens // n_mp
    rows = w_qkv.shape[0]
    width = w_qkv.shape[2]
    hidden = w_fc1.shape[1]
    half = D // 2
    place = [me ^ o for o in order_of(n_dp)]
    places = me ^ jnp.array(order_of(n_dp), jnp.int32)

    single = jnp.max(segment_ids) == 0
    time1_own = w_cond[:, PIN : PIN + FREQ].astype(LOW)
    digits = [v for a in (timesteps, labels) for v in (a.reshape(-1) // SIDE, a.reshape(-1) % SIDE)]
    note = jnp.concatenate(digits + [single.astype(jnp.int32)[None]]).astype(LOW)
    note = jnp.pad(note, (0, FREQ - note.shape[0]))
    thin = jnp.concatenate([w_cond[:, :PIN].astype(LOW), w_head.astype(LOW)], 1).reshape(-1, FREQ)
    thin_rows = thin.shape[0]
    fill = -(rows + thin_rows) % 16 or 16
    packet = spread(jnp.concatenate([time1_own, thin, jnp.broadcast_to(note, (fill, FREQ))], 0), "dp")
    packet = packet.reshape(n_dp, rows + thin_rows + fill, FREQ)

    qkv_own = jnp.concatenate([w_qkv[:, k].astype(LOW) for k in range(3)] + [w_out.astype(LOW)], 1)
    proj_way = Course(gather_steps(qkv_own, "dp"))

    time1_b = packet[:, :rows].reshape(D, FREQ)
    thin = packet[:, rows : rows + thin_rows].reshape(n_dp, rows, 2 * PIN).astype(F32)
    thin = jnp.concatenate([lax.dynamic_index_in_dim(thin, p, 0) for p in place], 0)
    thin = thin.reshape(D, 2 * PIN).T.astype(LOW)
    patch_b, head_b = thin[:PIN], thin[PIN:]
    notes = packet[:, rows + thin_rows].astype(jnp.int32)
    steps = notes[:, :SLOTS] * SIDE + notes[:, SLOTS : 2 * SLOTS]
    kinds = (notes[:, 2 * SLOTS : 3 * SLOTS] * SIDE + notes[:, 3 * SLOTS : 4 * SLOTS]).reshape(-1)
    singles = notes[:, 4 * SLOTS] == 1

    time2_b = w_cond[:, PIN + FREQ : PIN + FREQ + D].astype(LOW)
    table_b = w_cond[:, PIN + FREQ + D :].astype(LOW)
    mod_b = jnp.concatenate([w_mod[:, k].astype(LOW) for k in range(8)], 1)
    feat_b = time_features(steps.reshape(-1)).astype(LOW)
    slots_all = feat_b.shape[0]
    silu_t_b = jax.nn.silu(dot(feat_b, time1_b, ACROSS)).astype(LOW)
    onehot = (kinds[:, None] == jnp.arange(CLASSES, dtype=jnp.int32)).astype(LOW)
    cond = dot(silu_t_b, time2_b, ACROSS) + dot(onehot, table_b, ACROSS)
    silu_c_b = jax.nn.silu(cond).astype(LOW)
    mod_part = dot(silu_c_b, mod_b).reshape(n_dp, SLOTS, -1)
    own_silu = silu_c_b.astype(F32).reshape(-1, 8 * width)
    own_silu = jnp.broadcast_to(own_silu[None], (n_dp,) + own_silu.shape)
    mod_part = exchange(jnp.concatenate([mod_part, own_silu], 1), "dp")
    mod_cols = jnp.sum(mod_part[:, :SLOTS], 0).reshape(SLOTS, 8, width)
    silu_c_all = mod_part[:, SLOTS:].astype(LOW).reshape(n_dp, slots_all, rows).transpose(0, 2, 1)
    mod_cols = proj_way.step(mod_cols, mod_cols)
    flat = lambda m: [m[:, k].astype(LOW) for k in range(m.shape[1])]
    zeros = jnp.zeros((rows, width), LOW)
    pack_zero = jnp.concatenate(flat(mom_mod) + flat(mom_qkv) + [zeros], 1)
    pack_one = jnp.concatenate([m.astype(LOW) for m in (mom_fc1, mom_fc2, mom_out)] + [zeros] * 3, 1)
    own_pack = jnp.where(near == 0, pack_zero, pack_one)
    other_pack = jnp.where(near == 0, pack_one, pack_zero)
    other_pack = swap(after(other_pack, mod_cols), "dp", 1)
    feed_own = jnp.concatenate([w_fc1, w_fc2], 1).astype(LOW)
    feed_way = Course(gather_steps(after(feed_own, mod_cols), "dp"))
    part_slots = segment_ids[::part]
    outgoing = jnp.sum(
        jnp.where((part_slots[:, None] == jnp.arange(SLOTS))[:, :, None, None], mod_cols[None], 0.0), 1
    )
    mods = exchange(outgoing, "mp").transpose(1, 0, 2).reshape(8, n_mp * width)
    mods = to_local(mods, me, n_dp)
    mods = proj_way.step(proj_way.step(mods, mods), mods)
    slot = jnp.sum(jnp.where(jnp.arange(n_mp) == rank, part_slots, 0))

    abar = pick(plan(), steps)
    snr = abar / (1.0 - abar)
    slot_weight = jnp.minimum(snr, GAMMA) / snr
    weight_total = part * jnp.sum(jnp.where(singles[:, None], n_mp * slot_weight[:, :1] / SLOTS, slot_weight))
    mine = (jnp.arange(n_dp)[:, None] == me) & (jnp.arange(SLOTS) == slot)
    my_slot = lambda a: jnp.sum(jnp.where(mine, a, 0.0))
    abar_tok, weight_tok = my_slot(abar), my_slot(slot_weight)
    lat = lax.dynamic_slice_in_dim(latents, rank * part, part, 0)
    noi = lax.dynamic_slice_in_dim(noise, rank * part, part, 0)
    noisy_b = (jnp.sqrt(abar_tok) * lat + jnp.sqrt(1.0 - abar_tok) * noi).astype(LOW)
    picks = place_select(single, part, rank).astype(LOW)
    left = jnp.concatenate([noisy_b, picks, picks, picks], 1)
    column = (places[:, None] * rows + jnp.arange(rows, dtype=jnp.int32)).reshape(-1)
    x_in = dot(left, jnp.concatenate([patch_b, *thirds(place_table(column))], 0))
    alone = single.astype(jnp.int32)[None]

    tile = ((part, D), F32)
    tile_b = ((part, D), LOW)
    terms = [((2, part, D), F32), ((2, part, D), LOW)]
    sums = ((8, D), F32)
    thin_grad = ((PIN, D), F32)
    shares = [((half, D), F32), ((half, D), LOW)]
    (h_in,) = call(enter_kernel, "enter", [tile_b], x_in, mods)
    h_in = parts_of(h_in)
    h_in[3] = feed_way.step(proj_way.step(after(h_in[3], other_pack)))
    proj = joined(proj_way.finish())
    qkv_b, out_b = proj[:, : 3 * width], proj[:, 3 * width :]
    qkv, totals, mixed_b, *attn_terms = call(
        attend_kernel,
        "attend",
        [((tokens, 3 * width), LOW), ((8, tokens), F32), ((tokens, width), LOW), *terms],
        *(alone, *h_in, qkv_b, out_b),
        scalars=1,
        scratch=[((width, tokens), LOW)],
        flops=8 * tokens * tokens * width + 8 * tokens * D * width,
    )
    attn_terms[1] = feed_way.step(feed_way.step(attn_terms[1]))
    sides = [[side + 2 * i for i in range(n_dp // 2)] for side in range(2)]
    old = after(jnp.stack([own_pack, other_pack]), attn_terms[1])
    old = lax.all_gather(old, "dp", axis=0, axis_index_groups=sides)
    attn_terms, _ = parts_sum(*attn_terms)
    attn, x_mid, h_mid = call(middle_kernel, "middle", [tile, tile, tile_b], *attn_terms, x_in, mods)
    h_mid = parts_of(h_mid)
    feed_b = joined(feed_way.finish())

    act_b, slope, *mlp_terms = call(
        feed_kernel,
        "feed",
        [((tokens, hidden), LOW), ((tokens, hidden), F32), *terms],
        *(*h_mid, feed_b),
        flops=4 * tokens * D * hidden,
    )
    scales = jnp.stack([weight_tok, weight_tok / weight_total])
    mlp_terms, _ = parts_sum(*mlp_terms)
    d_out, d_mlp, d_head, end_sums, loss_part = call(
        final_kernel,
        "final",
        [tile, tile_b, thin_grad, sums, ((1, 128), F32)],
        *(scales, *mlp_terms, x_mid, mods, head_b, noi),
        scalars=1,
    )

    d_mlp = parts_of(d_mlp)
    d_mlp[3] = after(d_mlp[3], old)
    flops = 2 * tokens * D * hidden
    fc2_terms = call(feed_grads_kernel, "feed_grads", shares, *d_mlp, act_b, flops=flops)
    fc2_way = Course(sum_steps(*fc2_terms, "dp"))
    d_mlp[0] = after(d_mlp[0], fc2_terms[1])
    d_upper, *terms_mid = call(
        feed_back_kernel,
        "feed_back",
        [((tokens, hidden), LOW), *terms],
        *(*d_mlp, slope, feed_b),
        flops=2 * flops,
    )
    terms_mid, sent = parts_sum(*terms_mid)
    d_upper = after(d_upper, sent)
    fc1_terms = call(feed_grads_kernel, "feed_grads", shares, *h_mid, d_upper, flops=flops)
    fc1_way = Course(sum_steps(*fc1_terms, "dp"))
    terms_mid[2] = fc2_way.step(terms_mid[2])
    d_mid, d_attn, mid_sums = call(
        turn_kernel, "turn", [tile, tile_b, sums], *terms_mid, x_mid, d_out, attn, mods
    )
    d_attn = parts_of(d_attn)
    d_attn[3] = fc1_way.step(fc2_way.step(d_attn[3]))
    d_qkv, even, odd = call(
        attend_back_kernel,
        "attend_back",
        [((tokens, 3 * width), LOW), *terms],
        *(alone, qkv, totals, *d_attn, qkv_b, out_b),
        scalars=1,
        scratch=[((width, tokens), LOW)]
        + [((width // HEAD_DIM, tokens, HEAD_DIM), F32)] * 2
        + [((tokens, width), LOW)],
        flops=20 * tokens * tokens * width + 8 * tokens * D * width,
    )
    odd = fc1_way.step(fc2_way.step(odd))
    sum_fc2 = fc2_way.finish()
    fc2_way = Course(gather_steps(sum_fc2.astype(LOW), "dp"))
    terms_in, sent = parts_sum(even, odd)
    at_terms = call(
        attend_grads_kernel,
        "attend_grads",
        shares,
        *(*h_in, after(d_qkv, sent), *d_attn, mixed_b),
        flops=8 * tokens * D * width,
    )
    at_way = Course(sum_steps(*at_terms, "dp"))
    terms_in[2] = fc2_way.step(fc1_way.step(terms_in[2]))
    sum_fc1 = fc1_way.finish()
    fc1_way = Course(gather_steps(sum_fc1.astype(LOW), "dp"))
    d_patch, d_mods = call(
        leave_kernel, "leave", [thin_grad, sums], *terms_in, x_in, d_mid, mods, noisy_b, mid_sums, end_sums
    )

    d_mods = from_local(d_mods, me, n_dp).reshape(8, n_mp, width).transpose(1, 0, 2)
    blocks = jnp.broadcast_to(d_mods[None], (n_dp,) + d_mods.shape).reshape((n_dp * n_mp,) + d_mods.shape[1:])
    blocks = exchange(blocks, ("dp", "mp")).reshape(n_dp, n_mp, 8, width)
    blocks = at_way.step(blocks, blocks)
    first_only = (jnp.arange(SLOTS) == 0)[:, None, None]
    d_mod_all = jnp.where(
        singles[:, None, None, None], jnp.where(first_only, jnp.sum(blocks, 1, keepdims=True), 0.0), blocks
    )
    d_mod_all = d_mod_all.astype(LOW).reshape(slots_all, 8 * width)
    g_mod = dot(silu_c_b, d_mod_all, DOWN)
    d_cond_part = dot(d_mod_all, mod_b, ACROSS) * silu_slope(cond)
    d_silu_t_part = lax.dot_general(d_cond_part, time2_b.astype(F32), ALONG, precision=HIGH)
    thick = jnp.concatenate(
        [d_silu_t_part.reshape(-1, n_dp, rows), from_local(jnp.concatenate([d_patch, d_head], 0), me, n_dp)], 0
    )
    thick = jnp.sum(exchange(thick.transpose(1, 0, 2), "dp"), 0)
    for way in (at_way, fc1_way, fc2_way, fc2_way):
        thick = way.step(thick, thick)
    thick = sum_all(jnp.concatenate([thick, d_cond_part], 0), "mp")
    hidden_t = dot(feat_b, time1_own, ACROSS)
    d_hidden = thick[:slots_all] * silu_slope(hidden_t)
    g_patch = thick[slots_all : slots_all + PIN]
    g_head = thick[slots_all + PIN : slots_all + 2 * PIN].T
    d_cond = thick[slots_all + 2 * PIN :]
    right = jnp.concatenate(
        [
            jnp.concatenate([jnp.zeros((slots_all, PIN), LOW), feat_b, jnp.zeros((slots_all, D + CLASSES), LOW)], 1),
            jnp.eye(PIN, PIN + FREQ + D + CLASSES, dtype=LOW),
            jnp.concatenate([jnp.zeros((slots_all, PIN + FREQ), LOW), silu_t_b, onehot], 1),
        ],
        0,
    )
    g_cond = dot(
        jnp.concatenate(thirds(jnp.concatenate([d_hidden, g_patch, d_cond], 0)), 0),
        jnp.concatenate([right] * 3, 0),
        DOWN,
    )

    square = lambda g: jnp.sum(g * g)
    sum_at = at_way.finish()
    split_sq = square(sum_fc1) + square(sum_fc2) + square(sum_at) + square(g_mod)
    tally = jnp.stack([split_sq + (square(g_head) + square(g_cond)) / n_mp, loss_part[0, 0]])
    tally = fc1_way.step(fc1_way.step(fc2_way.step(jnp.broadcast_to(tally[:, None], (2, 128)))))
    at_copies = jnp.broadcast_to(sum_at.astype(LOW)[None], (n_dp,) + sum_at.shape)
    tally = after(tally, at_copies)
    tally = jnp.sum(spread(tally, ("dp", "mp")), 0)
    grad_norm = jnp.sqrt(tally[0, 0])
    loss_sum = tally[1, 0]
    coef = jnp.minimum(1.0, CLIP / (grad_norm + 1e-06))

    halves_of = lambda way: [g.reshape(n_dp // 2, rows, -1) for g in way.finish()]
    all_fc2 = halves_of(fc2_way)
    all_fc1 = halves_of(fc1_way)
    all_at = exchange(after(at_copies, tally), "dp")
    factor = coef[None]
    span = 8 * width

    def one_mod():
        return muon_rows(places, factor, old, (span, 0), (0, span), (silu_c_all, d_mod_all))

    def one_fc2():
        mine = muon_rows(places, factor, old, (hidden, 1), (0, hidden), all_fc2)
        return jnp.pad(mine, ((0, 0), (0, 0), (0, span - hidden)))

    def one_fc1():
        mine = muon_rows(places, factor, old, (hidden, 0), (0, hidden), all_fc1)
        return jnp.concatenate([both[:, :, :hidden], mine], 2)

    at_block = (4 * width, 2)

    def one_qkv():
        return muon_rows(places, factor, old, at_block, (0, 3 * width), (all_at,), (0, 3 * width))

    def one_out():
        mine = muon_rows(places, factor, old, at_block, (0, width), (all_at,), (3 * width, 4 * width))
        return jnp.pad(mine, ((0, 0), (0, 0), (0, 2 * width)))

    both = lax.cond(near == 0, one_mod, one_fc2)
    both = lax.cond(near == 0, lambda: both, one_fc1)
    last = lax.cond(near == 0, one_qkv, one_out)
    both = after(both, last)
    new_weights, new_moms = finish(
        near[None],
        factor,
        (both[0], swap(both[1], "dp", 1), last[0], swap(last[1], "dp", 1), sum_at, sum_fc1, sum_fc2, g_mod),
        (w_qkv, w_out, w_fc1, w_fc2, w_mod),
        (mom_qkv, mom_out, mom_fc1, mom_fc2, mom_mod),
    )
    coef = after(coef, last)

    adam_out = []
    for master, first, second, grad in (
        (w_head, first_head, second_head, g_head),
        (w_cond, first_cond, second_cond, g_cond),
    ):
        clipped = coef * grad
        first = BETA_ONE * first + (1.0 - BETA_ONE) * clipped
        second = BETA_TWO * second + (1.0 - BETA_TWO) * clipped * clipped
        update = first / (1.0 - BETA_ONE**STEP) / (jnp.sqrt(second / (1.0 - BETA_TWO**STEP)) + EPS_ADAM)
        adam_out.append((master - LR_ADAM * (update + DECAY * master), first, second))
    return (
        *new_weights,
        adam_out[0][0],
        adam_out[1][0],
        *new_moms,
        adam_out[0][1],
        adam_out[0][2],
        adam_out[1][1],
        adam_out[1][2],
        loss_sum,
        weight_total,
        grad_norm,
    )


def solution(mesh):
    row, wide, cube = P("dp", None), P("dp", "mp"), P("dp", None, "mp")
    in_specs = (
        *(row, row, P("dp"), row, row),
        *(cube, wide, wide, wide, cube, row, row),
        *(cube, wide, wide, wide, cube),
        *(row, row, row, row),
    )
    out_specs = (
        *(cube, wide, wide, wide, cube, row, row),
        *(cube, wide, wide, wide, cube),
        *(row, row, row, row),
        *(P(), P(), P()),
    )
    return jax.shard_map(body, mesh=mesh, in_specs=in_specs, out_specs=out_specs, check_vma=False)
```

```python
import functools
import math

import jax
import jax.numpy as jnp
from jax import lax
from jax.experimental import pallas as pl
from jax.experimental.pallas import tpu as pltpu
from jax.sharding import PartitionSpec as P

SIDE = 32
D = 768
HEAD_DIM = 64
CLASSES = 1001
FREQ = 256
PIN = 16
STEP = 10
SLOTS = 4

HIGH = lax.Precision.HIGHEST
GAMMA = 5.0
CLIP = 0.05
MU = 0.95
LR_MUON = 0.1
DECAY = 0.01
BETA_ONE = 0.9
BETA_TWO = 0.95
LR_ADAM = 0.08
EPS_ADAM = 1e-08
NS_COEF = (3.4445, -4.775, 2.0315)
NS_SHIFT = (0.0, 0.1, 0.5, 0.8, 0.8)
ACROSS = (((1,), (1,)), ((), ()))
DOWN = (((0,), (0,)), ((), ()))
ALONG = (((1,), (0,)), ((), ()))
LOW = jnp.bfloat16
F32 = jnp.float32


def dot(a, b, dims=ALONG):
    return lax.dot_general(a, b, dims, preferred_element_type=F32)


def order_of(size):
    order, bit = [0], size // 2
    while bit:
        order += [o ^ bit for o in order]
        bit //= 2
    return order


def swap(x, axis, bit):
    size = lax.axis_size(axis)
    return lax.ppermute(x, axis, [(i, i ^ bit) for i in range(size)])


def after(x, *others):
    return lax.optimization_barrier((x,) + others)[0]


class Course:
    def __init__(self, steps):
        self.steps = steps
        self.result = None
        self.flight = next(steps, None)

    def step(self, x, start=None, behind=None):
        arrived = self.flight
        if arrived is None:
            return x
        arrived = late(arrived, behind)
        x = after(x, arrived)
        try:
            self.flight = self.steps.send((arrived, start))
        except StopIteration as stop:
            self.flight, self.result = None, stop.value
        return x

    def finish(self):
        while self.flight is not None:
            self.step(jnp.zeros((), F32))
        return self.result


def late(x, start):
    return x if start is None else after(x, start)


def gather_steps(x, axis):
    bit = lax.axis_size(axis) // 2
    start, last = None, 1
    while bit > last:
        other, start = yield swap(late(x, start), axis, bit)
        x = jnp.concatenate([x, other], 0)
        bit //= 2
    _, start = yield x
    other, start = yield swap(late(x, start), axis, bit)
    return x, other


def joined(pair):
    return jnp.concatenate(pair, 0)


def sum_steps(keep, send, axis):
    bit, size = 1, lax.axis_size(axis)
    other, start = yield swap(send, axis, bit)
    total = keep + other.astype(F32)
    while bit < size // 2:
        bit *= 2
        half = total.shape[0] // 2
        other, start = yield swap(late(total[half:].astype(LOW), start), axis, bit)
        total = total[:half] + other.astype(F32)
    return total


def sum_all(x, axis):
    bit = 1
    while bit < lax.axis_size(axis):
        x = x + swap(x, axis, bit)
        bit *= 2
    return x


def parts_of(h):
    two = swap(h, "mp", 2)
    one = swap(h, "mp", 1)
    return [h, one, two, swap(two, "mp", 1)]


def parts_sum(even, odd, then=lambda x: x):
    near = then(swap(odd, "mp", 1))
    send = (even[1] + near[1].astype(F32)).astype(LOW)
    return [even, near, swap(send, "mp", 2)], send


def turned_over(v, me):
    size, bit = v.shape[-2], 1
    lead, k = v.shape[:-2], v.shape[-1]
    while bit < size:
        pair = v.reshape(lead + (size // (2 * bit), 2, bit, k))
        flipped = jnp.concatenate([pair[..., 1:, :, :], pair[..., :1, :, :]], -3)
        v = jnp.where((me // bit) % 2 == 1, flipped, pair).reshape(lead + (size, k))
        bit *= 2
    return v


def to_local(v, me, size):
    blocks = turned_over(v.reshape(v.shape[:-1] + (size, v.shape[-1] // size)), me)
    return jnp.concatenate([blocks[..., o, :] for o in order_of(size)], -1)


def from_local(v, me, size):
    blocks = v.reshape(v.shape[:-1] + (size, v.shape[-1] // size))
    order = order_of(size)
    return turned_over(jnp.stack([blocks[..., order.index(k), :] for k in range(size)], -2), me)


def spread(x, axis):
    size = math.prod(lax.axis_size(a) for a in ((axis,) if isinstance(axis, str) else axis))
    copies = jnp.broadcast_to(x[None], (size,) + x.shape)
    return lax.all_to_all(copies, axis, 0, 0, tiled=True)


def exchange(x, axis):
    return lax.all_to_all(x, axis, 0, 0, tiled=True)


def plan():
    betas = jnp.linspace(0.0001, 0.02, 1000, dtype=F32)
    return jnp.cumprod(1.0 - betas)


def pick(table, index):
    grid = jnp.arange(table.shape[0], dtype=jnp.int32)
    return jnp.sum(jnp.where(index[..., None] == grid, table, 0.0), -1)


def normalize(x):
    cent = x - jnp.mean(x, -1, keepdims=True)
    inv = lax.rsqrt(jnp.mean(cent * cent, -1, keepdims=True) + 1e-06)
    return cent * inv, inv


def norm_back(grad, unit, inv, scale):
    d_shift = jnp.sum(grad, 0, keepdims=True)
    d_scale = jnp.sum(grad * unit, 0, keepdims=True)
    g = grad * (1.0 + scale)
    dx = inv * (g - jnp.mean(g, -1, keepdims=True) - unit * jnp.mean(g * unit, -1, keepdims=True))
    return dx, d_shift, d_scale


def place_table(column):
    quarter = D // 4
    omega = 1.0 / 10000.0 ** ((column % quarter).astype(F32) / quarter)
    angle = jnp.arange(SIDE, dtype=F32)[:, None] * omega
    wave = jnp.where((column // quarter) % 2 == 0, jnp.sin(angle), jnp.cos(angle))
    down = column < D // 2
    return jnp.concatenate([jnp.where(down, wave, 0.0), jnp.where(down, 0.0, wave)], 0)


def place_select(single, part, rank):
    local = jnp.arange(part, dtype=jnp.int32)
    full = rank * part + local
    half = SIDE // 2
    down = jnp.where(single, full // SIDE, local // half)
    across = jnp.where(single, full % SIDE, local % half)
    grid = jnp.arange(SIDE, dtype=jnp.int32)
    return jnp.concatenate([down[:, None] == grid, across[:, None] == grid], 1)


def thirds(x):
    high = x.astype(LOW)
    rest = x - high.astype(F32)
    mid = rest.astype(LOW)
    return high, mid, (rest - mid.astype(F32)).astype(LOW)


def time_features(steps):
    half = FREQ // 2
    freqs = jnp.exp(-math.log(10000.0) * jnp.arange(half, dtype=F32) / half)
    angles = steps.astype(F32)[:, None] * freqs
    return jnp.concatenate([jnp.cos(angles), jnp.sin(angles)], -1)


def silu_slope(x):
    s = jax.nn.sigmoid(x)
    return s * (1.0 + x * (1.0 - s))


def call(kernel, name, outs, *args, scalars=0, scratch=(), flops=0, vmem_mb=16):
    smem, vmem = pl.BlockSpec(memory_space=pltpu.SMEM), pl.BlockSpec(memory_space=pltpu.VMEM)
    size = sum(math.prod(o[0]) * jnp.dtype(o[1]).itemsize for o in outs)
    return pl.pallas_call(
        kernel,
        out_shape=[jax.ShapeDtypeStruct(*o) for o in outs],
        in_specs=[smem] * scalars + [vmem] * (len(args) - scalars),
        out_specs=[vmem] * len(outs),
        scratch_shapes=[pltpu.VMEM(*t) for t in scratch],
        compiler_params=pltpu.CompilerParams(vmem_limit_bytes=vmem_mb * 2**20),
        cost_estimate=pl.CostEstimate(flops=1, bytes_accessed=1, transcendentals=0),
        name=name,
    )(*args)


def turned(x):
    return x.astype(F32).T.astype(x.dtype)


def added(even_ref, near_ref, far_ref):
    return even_ref[0] + near_ref[0].astype(F32) + far_ref[...].astype(F32)


def pack_kernel(near_ref, slots_ref, m_mod, m_qkv, m_fc1, m_fc2, m_out, own_ref, other_ref):
    width, hidden = m_out.shape[1], m_fc1.shape[1]

    def put(even, odd):
        at = 0
        for piece in [m_mod[:, k] for k in range(8)] + [m_qkv[k] for k in range(3)] + [slots_ref[...].astype(F32)]:
            even[:, at : at + width] = piece.astype(LOW)
            at += width
        odd[:, :hidden] = m_fc1[...].astype(LOW)
        odd[:, hidden : 2 * hidden] = m_fc2[...].astype(LOW)
        odd[:, 2 * hidden : 2 * hidden + width] = m_out[...].astype(LOW)
        odd[:, 2 * hidden + width :] = jnp.zeros((odd.shape[0], 3 * width), LOW)

    @pl.when(near_ref[0] == 0)
    def _():
        put(own_ref.at[0], other_ref)

    @pl.when(near_ref[0] != 0)
    def _():
        put(other_ref, own_ref.at[0])


def pack(near, slots, m_mod, m_qkv, m_fc1, m_fc2, m_out):
    shape = (m_mod.shape[0], 12 * m_out.shape[1])
    return call(
        pack_kernel,
        "pack",
        [((2,) + shape, LOW), (shape, LOW)],
        *(near, slots, m_mod, m_qkv.transpose(1, 0, 2), m_fc1, m_fc2, m_out),
        scalars=1,
    )


def enter_kernel(x_ref, mods_ref, h_ref):
    unit, _ = normalize(x_ref[...])
    h_ref[...] = (unit * (1.0 + mods_ref[1:2, :]) + mods_ref[0:1, :]).astype(LOW)


def middle_kernel(even_ref, near_ref, far_ref, x_ref, mods_ref, attn_ref, mid_ref, h_ref):
    attn = added(even_ref, near_ref, far_ref)
    attn_ref[...] = attn
    mid = x_ref[...] + mods_ref[2:3, :] * attn
    mid_ref[...] = mid
    unit, _ = normalize(mid)
    h_ref[...] = (unit * (1.0 + mods_ref[4:5, :]) + mods_ref[3:4, :]).astype(LOW)


def final_kernel(
    scale_ref, even_ref, near_ref, far_ref, mid_ref, mods_ref, head_ref, noise_ref,
    out_ref, mlp_ref, head_grad_ref, sums_ref, loss_ref,
):
    mlp = added(even_ref, near_ref, far_ref)
    unit, inv = normalize(mid_ref[...] + mods_ref[5:6, :] * mlp)
    h = (unit * (1.0 + mods_ref[7:8, :]) + mods_ref[6:7, :]).astype(LOW)
    diff = dot(h, head_ref[...], ACROSS) - noise_ref[...]
    loss = jnp.sum(jnp.sum(diff * diff, axis=1, keepdims=True), axis=0, keepdims=True)
    loss_ref[...] = jnp.broadcast_to(scale_ref[0] * loss, loss_ref.shape)
    d_pred = (2.0 * diff * scale_ref[1]).astype(LOW)
    head_grad_ref[...] = dot(d_pred, h, DOWN)
    d_out, d_shift, d_scale = norm_back(dot(d_pred, head_ref[...]), unit, inv, mods_ref[7:8, :])
    out_ref[...] = d_out
    mlp_ref[...] = (d_out * mods_ref[5:6, :]).astype(LOW)
    sums_ref[0:1, :] = jnp.sum(d_out * mlp, 0, keepdims=True)
    sums_ref[1:2, :] = d_shift
    sums_ref[2:3, :] = d_scale


def turn_kernel(
    even_ref, near_ref, far_ref, mid_ref, out_ref, attn_ref, mods_ref, d_mid_ref, d_attn_ref, sums_ref
):
    unit, inv = normalize(mid_ref[...])
    dx, d_shift, d_scale = norm_back(added(even_ref, near_ref, far_ref), unit, inv, mods_ref[4:5, :])
    d_mid = out_ref[...] + dx
    d_mid_ref[...] = d_mid
    d_attn_ref[...] = (d_mid * mods_ref[2:3, :]).astype(LOW)
    sums_ref[0:1, :] = jnp.sum(d_mid * attn_ref[...], 0, keepdims=True)
    sums_ref[1:2, :] = d_shift
    sums_ref[2:3, :] = d_scale


def leave_kernel(
    even_ref, near_ref, far_ref, x_ref, d_mid_ref, mods_ref, noisy_ref, mid_sums_ref, end_sums_ref,
    patch_ref, sums_ref,
):
    unit, inv = normalize(x_ref[...])
    dx, d_shift, d_scale = norm_back(added(even_ref, near_ref, far_ref), unit, inv, mods_ref[1:2, :])
    patch_ref[...] = dot(noisy_ref[...], (d_mid_ref[...] + dx).astype(LOW), DOWN)
    sums_ref[0:1, :] = d_shift
    sums_ref[1:2, :] = d_scale
    sums_ref[2:5, :] = mid_sums_ref[0:3, :]
    sums_ref[5:8, :] = end_sums_ref[0:3, :]


def attend_kernel(
    single_ref, h0_ref, h1_ref, h2_ref, h3_ref, w_ref, o_ref,
    qkv_ref, total_ref, mixed_ref, even_ref, odd_ref, vt_ref,
):
    part = h0_ref.shape[0]
    width = mixed_ref.shape[1]
    for j, ref in enumerate((h0_ref, h1_ref, h2_ref, h3_ref)):
        qkv_ref[j * part : (j + 1) * part, :] = dot(ref[...], w_ref[...]).astype(LOW)
    vt_ref[...] = turned(qkv_ref[:, 2 * width :])

    def run(i, keys):
        mine = pl.ds(pl.multiple_of(i * part, part), part)
        outs = []
        for h in range(width // HEAD_DIM):
            lo = h * HEAD_DIM
            q = qkv_ref[mine, lo : lo + HEAD_DIM] * HEAD_DIM**-0.5
            k = qkv_ref[keys, width + lo : width + lo + HEAD_DIM]
            s = dot(k, q, ACROSS)
            top = jnp.max(s, axis=0, keepdims=True)
            e = jnp.exp(s - top)
            z = jnp.sum(e, axis=0, keepdims=True)
            total_ref[h : h + 1, mine] = top + jnp.log(z)
            outs.append(dot(vt_ref[lo : lo + HEAD_DIM, keys], (e * (1.0 / z)).astype(LOW)))
        mixed_ref[mine, :] = jnp.concatenate(outs, 0).T.astype(LOW)

    def block(i, carry):
        mine = pl.ds(pl.multiple_of(i * part, part), part)

        @pl.when(single_ref[0] == 1)
        def _():
            run(i, slice(None))

        @pl.when(single_ref[0] != 1)
        def _():
            run(i, mine)

        return carry

    lax.fori_loop(0, 4, block, 0)
    for j in range(4):
        term = dot(mixed_ref[j * part : (j + 1) * part, :], o_ref[...], ACROSS)
        if j % 2 == 0:
            even_ref[j // 2] = term
        else:
            odd_ref[j // 2] = term.astype(LOW)


def attend_back_kernel(
    single_ref, qkv_ref, total_ref, d0_ref, d1_ref, d2_ref, d3_ref, w_ref, o_ref,
    grad_ref, even_ref, odd_ref, kt_ref, dk_ref, dv_ref, g_ref,
):
    part = d0_ref.shape[0]
    width = qkv_ref.shape[1] // 3
    heads = width // HEAD_DIM
    for j, ref in enumerate((d0_ref, d1_ref, d2_ref, d3_ref)):
        g_ref[j * part : (j + 1) * part, :] = dot(ref[...], o_ref[...]).astype(LOW)
    kt_ref[...] = turned(qkv_ref[:, width : 2 * width] * HEAD_DIM**-0.5)
    dk_ref[...] = jnp.zeros_like(dk_ref)
    dv_ref[...] = jnp.zeros_like(dv_ref)

    def run(i, keys):
        mine = pl.ds(pl.multiple_of(i * part, part), part)
        outs = []
        for h in range(heads):
            lo = h * HEAD_DIM
            q = qkv_ref[mine, lo : lo + HEAD_DIM] * HEAD_DIM**-0.5
            k = qkv_ref[keys, width + lo : width + lo + HEAD_DIM]
            v = qkv_ref[keys, 2 * width + lo : 2 * width + lo + HEAD_DIM]
            g = g_ref[mine, lo : lo + HEAD_DIM]
            p = jnp.exp(dot(k, q, ACROSS) - total_ref[h : h + 1, mine])
            dp = dot(v, g, ACROSS)
            delta = jnp.sum(dp * p, axis=0, keepdims=True)
            ds = (p * (dp - delta)).astype(LOW)
            dv_ref[h, keys, :] += dot(p.astype(LOW), g)
            dk_ref[h, keys, :] += dot(ds, q)
            outs.append(dot(kt_ref[lo : lo + HEAD_DIM, keys], ds))
        grad_ref[mine, :width] = jnp.concatenate(outs, 0).T.astype(LOW)

    def block(i, carry):
        @pl.when(single_ref[0] == 1)
        def _():
            run(i, slice(None))

        @pl.when(single_ref[0] != 1)
        def _():
            run(i, pl.ds(pl.multiple_of(i * part, part), part))

        return carry

    lax.fori_loop(0, 4, block, 0)
    for h in range(heads):
        lo = h * HEAD_DIM
        grad_ref[:, width + lo : width + lo + HEAD_DIM] = dk_ref[h].astype(LOW)
        grad_ref[:, 2 * width + lo : 2 * width + lo + HEAD_DIM] = dv_ref[h].astype(LOW)
    for j in range(4):
        term = dot(grad_ref[j * part : (j + 1) * part, :], w_ref[...], ACROSS)
        if j % 2 == 0:
            even_ref[j // 2] = term
        else:
            odd_ref[j // 2] = term.astype(LOW)


def halves(keep_ref, send_ref, columns, value):
    half = keep_ref.shape[0]
    keep_ref[:, columns] = value[:half]
    send_ref[:, columns] = value[half:].astype(LOW)


def attend_grads_kernel(h0, h1, h2, h3, grad_ref, d0, d1, d2, d3, mixed_ref, keep_ref, send_ref):
    part, width = h0.shape[0], mixed_ref.shape[1]
    rows = lambda j: slice(j * part, (j + 1) * part)
    halves(
        keep_ref, send_ref, slice(0, 3 * width),
        sum(dot(h[...], grad_ref[rows(j), :], DOWN) for j, h in enumerate((h0, h1, h2, h3))),
    )
    halves(
        keep_ref, send_ref, slice(3 * width, 4 * width),
        sum(dot(d[...], mixed_ref[rows(j), :], DOWN) for j, d in enumerate((d0, d1, d2, d3))),
    )


def feed_kernel(h0, h1, h2, h3, w_ref, act_ref, slope_ref, even_ref, odd_ref):
    part, hidden = h0.shape[0], act_ref.shape[1]
    for j, h in enumerate((h0, h1, h2, h3)):
        rows = slice(j * part, (j + 1) * part)
        upper = dot(h[...], w_ref[:, :hidden])
        gate = 0.5 * (1.0 + lax.erf(upper * 0.5**0.5))
        act = (upper * gate).astype(LOW)
        act_ref[rows, :] = act
        slope = gate + upper * jnp.exp(-0.5 * upper * upper) * (2.0 * math.pi) ** -0.5
        slope_ref[rows, :] = slope.astype(LOW)
        term = dot(act, w_ref[:, hidden:], ACROSS)
        if j % 2 == 0:
            even_ref[j // 2] = term
        else:
            odd_ref[j // 2] = term.astype(LOW)


def feed_back_kernel(d0, d1, d2, d3, slope_ref, w_ref, upper_ref, even_ref, odd_ref):
    part, hidden = d0.shape[0], slope_ref.shape[1]
    for j, d in enumerate((d0, d1, d2, d3)):
        rows = slice(j * part, (j + 1) * part)
        d_upper = (dot(d[...], w_ref[:, hidden:]) * slope_ref[rows, :].astype(F32)).astype(LOW)
        upper_ref[rows, :] = d_upper
        term = dot(d_upper, w_ref[:, :hidden], ACROSS)
        if j % 2 == 0:
            even_ref[j // 2] = term
        else:
            odd_ref[j // 2] = term.astype(LOW)


def feed_grads_kernel(h0, h1, h2, h3, x_ref, keep_ref, send_ref):
    part = h0.shape[0]
    value = sum(
        dot(h[...], x_ref[j * part : (j + 1) * part, :], DOWN) for j, h in enumerate((h0, h1, h2, h3))
    )
    halves(keep_ref, send_ref, slice(None), value)


def muon_kernel(columns, span, order_ref, coef_ref, plan_ref, mom_ref, *refs):
    grads, (out_ref, x_ref, b_ref, e_ref, r_ref, turn_ref) = refs[:-6], refs[-6:]
    third = NS_COEF[2]
    size, width = x_ref.shape
    count, pairs = mom_ref.shape[2], mom_ref.shape[0]
    coef = coef_ref[0]
    spans = [slice(i, min(i + size, width)) for i in range(0, width, size)]

    tall = size < count * 2 * pairs
    squares = jnp.zeros((1, 1), F32)
    for place in range(2 * pairs):
        true = order_ref[place]
        if len(grads) == 1:
            grad = grads[0][true, :, slice(*span)].astype(F32)
        elif len(grads[0].shape) == 4:
            grad = dot(grads[0][lax.shift_right_logical(true, 1), place // pairs], grads[1][...])
        else:
            grad = grads[place // pairs][place % pairs].astype(F32)
        mom = mom_ref[lax.shift_right_logical(true, 1), place // pairs, :, slice(*columns)]
        x = MU * mom.astype(F32) + coef * grad
        if tall:
            turn_ref[place * count : (place + 1) * count, :] = x
        else:
            x_ref[place * count : (place + 1) * count, :] = x
        squares = squares + jnp.sum(jnp.sum(x * x, axis=0, keepdims=True), axis=1, keepdims=True)
    inv = 1.0 / (jnp.sqrt(squares) + 1e-07)
    x_ref[...] = (turn_ref[...].T if tall else x_ref[...]) * inv
    b_ref[...] = x_ref[...].astype(LOW)

    def gram(shift):
        e = sum(dot(b_ref[:, span], b_ref[:, span], ACROSS) for span in spans)
        row = lax.broadcasted_iota(jnp.int32, e.shape, 0)
        column = lax.broadcasted_iota(jnp.int32, e.shape, 1)
        e = e - jnp.where(row == column, shift, 0.0)
        e_ref[...] = e
        r_ref[...] = e.astype(LOW)

    def turn(i, carry):
        centre, slope = plan_ref[i, 0], plan_ref[i, 1]
        gram(plan_ref[i, 2])
        r_ref[...] = (slope * e_ref[...] + third * dot(r_ref[...], r_ref[...])).astype(LOW)
        for span in spans:
            x = centre * x_ref[:, span] + dot(r_ref[...], b_ref[:, span])
            x_ref[:, span] = x
            b_ref[:, span] = x.astype(LOW)
        return carry

    last = len(NS_SHIFT) - 1
    lax.fori_loop(0, last, turn, 0)
    gram(plan_ref[last, 2])
    both = [slice(0, count), slice(pairs * count, (pairs + 1) * count)]
    scaled = 0.2 * math.sqrt(max(size, width))
    if tall:
        poly = plan_ref[last, 1] * e_ref[...] + third * dot(r_ref[...], r_ref[...])
        x = jnp.concatenate([x_ref[:, own].T for own in both], 0)
        x = scaled * (plan_ref[last, 0] * x + dot(x.astype(LOW), poly.astype(LOW)))
        out_ref[0] = x[:count].astype(LOW)
        out_ref[1] = x[count:].astype(LOW)
        return
    e = jnp.concatenate([e_ref[own, :] for own in both], 0)
    poly = (plan_ref[last, 1] * e + third * dot(e.astype(LOW), r_ref[...])).astype(LOW)
    for span in spans:
        x = jnp.concatenate([x_ref[own, span] for own in both], 0)
        x = scaled * (plan_ref[last, 0] * x + dot(poly, b_ref[:, span]))
        out_ref[0, :, span] = x[:count].astype(LOW)
        out_ref[1, :, span] = x[count:].astype(LOW)


def muon_rows(order, coef, old, block, columns, grads, span=None):
    pairs, _, count, _ = old.shape
    deep, width = 2 * pairs * count, columns[1] - columns[0]
    size, long = (width, deep) if 2 * width <= deep else (deep, width)
    first, second, third = NS_COEF
    plan = [[first + second * s + third * s * s, second + 2.0 * third * s, s] for s in NS_SHIFT]
    smem, vmem = pl.BlockSpec(memory_space=pltpu.SMEM), pl.BlockSpec(memory_space=pltpu.VMEM)
    return pl.pallas_call(
        functools.partial(muon_kernel, columns, span),
        grid=(1,),
        out_shape=jax.ShapeDtypeStruct((2, count, width), LOW),
        in_specs=[smem, smem, smem, pl.BlockSpec((pairs, 2, count, block[0]), lambda i: (0, 0, 0, block[1]))]
        + [vmem] * len(grads),
        out_specs=vmem,
        scratch_shapes=[
            pltpu.VMEM((size, long), F32),
            pltpu.VMEM((size, long), LOW),
            pltpu.VMEM((size, size), F32),
            pltpu.VMEM((size, size), LOW),
            pltpu.VMEM((deep, width) if size < deep else (8, 128), F32),
        ],
        compiler_params=pltpu.CompilerParams(vmem_limit_bytes=32 * 2**20),
        cost_estimate=pl.CostEstimate(flops=1, bytes_accessed=1, transcendentals=0),
        name="muon",
    )(order, coef, jnp.array(plan, F32), old, *grads)


def finish_kernel(
    near_ref, coef_ref, own_a, got_a, own_b, got_b, g_at, g_fc1, g_fc2, g_mod,
    w_qkv, w_out, w_fc1, w_fc2, w_mod, m_qkv, m_out, m_fc1, m_fc2, m_mod,
    n_qkv, n_out, n_fc1, n_fc2, n_mod, k_qkv, k_out, k_fc1, k_fc2, k_mod,
):
    width, hidden = w_out.shape[1], w_fc1.shape[1]
    coef = coef_ref[0]
    mine = near_ref[0] == 0

    def put(place, weight, mom, new, kept, update, grad):
        new[place] = weight[place] * (1.0 - LR_MUON * DECAY) - LR_MUON * update
        kept[place] = MU * mom[place] + coef * grad

    a, b = own_a[...].astype(F32), got_a[...].astype(F32)
    u_mod, u_fc = jnp.where(mine, a, b), jnp.where(mine, b, a)
    a, b = own_b[...].astype(F32), got_b[...].astype(F32)
    u_qkv, u_out = jnp.where(mine, a, b), jnp.where(mine, b, a)[:, :width]
    for k in range(3):
        span = slice(k * width, (k + 1) * width)
        put(k, w_qkv, m_qkv, n_qkv, k_qkv, u_qkv[:, span], g_at[:, span])
    for k in range(8):
        span = slice(k * width, (k + 1) * width)
        put((slice(None), k), w_mod, m_mod, n_mod, k_mod, u_mod[:, span], g_mod[:, span])
    put(slice(None), w_out, m_out, n_out, k_out, u_out, g_at[:, 3 * width :])
    put(slice(None), w_fc2, m_fc2, n_fc2, k_fc2, u_fc[:, :hidden], g_fc2[...])
    put(slice(None), w_fc1, m_fc1, n_fc1, k_fc1, u_fc[:, hidden:], g_fc1[...])


def finish(near, coef, flats, weights, moms):
    rows = flats[0].shape[0]
    step = rows // 2 if rows % 32 == 0 else rows
    smem = pl.BlockSpec(memory_space=pltpu.SMEM)

    def block(a):
        if a.ndim == 2:
            return pl.BlockSpec((step, a.shape[1]), lambda i: (i, 0))
        if a.shape[0] == rows:
            return pl.BlockSpec((step,) + a.shape[1:], lambda i: (i, 0, 0))
        return pl.BlockSpec((a.shape[0], step, a.shape[2]), lambda i: (0, i, 0))

    first = lambda a: a.transpose(1, 0, 2)
    arrays = [first(weights[0]), *weights[1:], first(moms[0]), *moms[1:]]
    outs = pl.pallas_call(
        finish_kernel,
        grid=(rows // step,),
        out_shape=[jax.ShapeDtypeStruct(a.shape, F32) for a in arrays],
        in_specs=[smem, smem] + [block(a) for a in (*flats, *arrays)],
        out_specs=[block(a) for a in arrays],
        compiler_params=pltpu.CompilerParams(vmem_limit_bytes=32 * 2**20),
        name="finish",
    )(near, coef, *flats, *arrays)
    return [first(outs[0]), *outs[1:5]], [first(outs[5]), *outs[6:]]


def body(
    latents,
    noise,
    segment_ids,
    timesteps,
    labels,
    w_qkv,
    w_out,
    w_fc1,
    w_fc2,
    w_mod,
    w_head,
    w_cond,
    mom_qkv,
    mom_out,
    mom_fc1,
    mom_fc2,
    mom_mod,
    first_head,
    second_head,
    first_cond,
    second_cond,
):
    n_dp, n_mp = lax.axis_size("dp"), lax.axis_size("mp")
    me, rank = lax.axis_index("dp"), lax.axis_index("mp")
    near = me % 2
    tokens = latents.shape[0]
    part = tokens // n_mp
    rows = w_qkv.shape[0]
    width = w_qkv.shape[2]
    hidden = w_fc1.shape[1]
    half = D // 2
    place = [me ^ o for o in order_of(n_dp)]
    places = me ^ jnp.array(order_of(n_dp), jnp.int32)

    single = jnp.max(segment_ids) == 0
    time1_own = w_cond[:, PIN : PIN + FREQ].astype(LOW)
    digits = [v for a in (timesteps, labels) for v in (a.reshape(-1) // SIDE, a.reshape(-1) % SIDE)]
    note = jnp.concatenate(digits + [single.astype(jnp.int32)[None]]).astype(LOW)
    note = jnp.pad(note, (0, FREQ - note.shape[0]))
    thin = jnp.concatenate([w_cond[:, :PIN].astype(LOW), w_head.astype(LOW)], 1).reshape(-1, FREQ)
    thin_rows = thin.shape[0]
    fill = -(rows + thin_rows) % 16 or 16
    packet = spread(jnp.concatenate([time1_own, thin, jnp.broadcast_to(note, (fill, FREQ))], 0), "dp")
    packet = packet.reshape(n_dp, rows + thin_rows + fill, FREQ)

    time1_b = packet[:, :rows].reshape(D, FREQ)
    thin = packet[:, rows : rows + thin_rows].reshape(n_dp, rows, 2 * PIN).astype(F32)
    thin = jnp.concatenate([lax.dynamic_index_in_dim(thin, p, 0) for p in place], 0)
    thin = thin.reshape(D, 2 * PIN).T.astype(LOW)
    patch_b, head_b = thin[:PIN], thin[PIN:]
    notes = packet[:, rows + thin_rows].astype(jnp.int32)
    steps = notes[:, :SLOTS] * SIDE + notes[:, SLOTS : 2 * SLOTS]
    kinds = (notes[:, 2 * SLOTS : 3 * SLOTS] * SIDE + notes[:, 3 * SLOTS : 4 * SLOTS]).reshape(-1)
    singles = notes[:, 4 * SLOTS] == 1

    time2_b = w_cond[:, PIN + FREQ : PIN + FREQ + D].astype(LOW)
    table_b = w_cond[:, PIN + FREQ + D :].astype(LOW)
    mod_b = jnp.concatenate([w_mod[:, k].astype(LOW) for k in range(8)], 1)
    feat_b = time_features(steps.reshape(-1)).astype(LOW)
    slots_all = feat_b.shape[0]
    silu_t_b = jax.nn.silu(dot(feat_b, time1_b, ACROSS)).astype(LOW)
    onehot = (kinds[:, None] == jnp.arange(CLASSES, dtype=jnp.int32)).astype(LOW)
    qkv_own = jnp.concatenate([w_qkv[:, k].astype(LOW) for k in range(3)] + [w_out.astype(LOW)], 1)
    proj_way = Course(gather_steps(after(qkv_own, silu_t_b), "dp"))
    cond = dot(silu_t_b, time2_b, ACROSS) + dot(onehot, table_b, ACROSS)
    silu_c_b = jax.nn.silu(cond).astype(LOW)
    mod_part = exchange(dot(silu_c_b, mod_b).reshape(n_dp, SLOTS, -1), "dp")
    mod_cols = jnp.sum(mod_part, 0).reshape(SLOTS, 8, width)
    mod_cols = proj_way.step(mod_cols, mod_cols)
    slots_own = jnp.pad(silu_c_b.T, ((0, 0), (0, width - slots_all)))
    own_pack, other_pack = pack(near[None], slots_own, mom_mod, mom_qkv, mom_fc1, mom_fc2, mom_out)
    other_pack = swap(other_pack, "dp", 1)
    part_slots = segment_ids[::part]
    outgoing = jnp.sum(
        jnp.where((part_slots[:, None] == jnp.arange(SLOTS))[:, :, None, None], mod_cols[None], 0.0), 1
    )
    mods = exchange(outgoing, "mp").transpose(1, 0, 2).reshape(8, n_mp * width)
    mods = after(to_local(mods, me, n_dp), other_pack)
    slot = jnp.sum(jnp.where(jnp.arange(n_mp) == rank, part_slots, 0))

    abar = pick(plan(), steps)
    snr = abar / (1.0 - abar)
    slot_weight = jnp.minimum(snr, GAMMA) / snr
    weight_total = part * jnp.sum(jnp.where(singles[:, None], n_mp * slot_weight[:, :1] / SLOTS, slot_weight))
    mine = (jnp.arange(n_dp)[:, None] == me) & (jnp.arange(SLOTS) == slot)
    my_slot = lambda a: jnp.sum(jnp.where(mine, a, 0.0))
    abar_tok, weight_tok = my_slot(abar), my_slot(slot_weight)
    lat = lax.dynamic_slice_in_dim(latents, rank * part, part, 0)
    noi = lax.dynamic_slice_in_dim(noise, rank * part, part, 0)
    noisy_b = (jnp.sqrt(abar_tok) * lat + jnp.sqrt(1.0 - abar_tok) * noi).astype(LOW)
    picks = place_select(single, part, rank).astype(LOW)
    left = jnp.concatenate([noisy_b, picks, picks, picks], 1)
    column = (after(places, silu_t_b)[:, None] * rows + jnp.arange(rows, dtype=jnp.int32)).reshape(-1)
    x_in = dot(left, jnp.concatenate([patch_b, *thirds(place_table(column))], 0))
    alone = single.astype(jnp.int32)[None]

    tile = ((part, D), F32)
    tile_b = ((part, D), LOW)
    terms = [((2, part, D), F32), ((2, part, D), LOW)]
    sums = ((8, D), F32)
    thin_grad = ((PIN, D), F32)
    shares = [((half, D), F32), ((half, D), LOW)]
    (h_in,) = call(enter_kernel, "enter", [tile_b], x_in, mods)
    h_in = proj_way.step(h_in)
    feed_own = jnp.concatenate([w_fc1, w_fc2], 1).astype(LOW)
    feed_way = Course(gather_steps(after(feed_own, h_in), "dp"))
    h_in = parts_of(h_in)
    h_in[1] = proj_way.step(h_in[1])
    h_in[3] = feed_way.step(h_in[3])
    proj = joined(proj_way.finish())
    qkv_b, out_b = proj[:, : 3 * width], proj[:, 3 * width :]
    qkv, totals, mixed_b, *attn_terms = call(
        attend_kernel,
        "attend",
        [((tokens, 3 * width), LOW), ((8, tokens), F32), ((tokens, width), LOW), *terms],
        *(alone, *h_in, qkv_b, out_b),
        scalars=1,
        scratch=[((width, tokens), LOW)],
        flops=8 * tokens * tokens * width + 8 * tokens * D * width,
    )
    attn_terms, sent = parts_sum(*attn_terms, lambda near: feed_way.step(feed_way.step(near)))
    sides = [[side + 2 * i for i in range(n_dp // 2)] for side in range(2)]
    old = after(lax.dynamic_update_slice(own_pack, other_pack[None], (1, 0, 0)), sent)
    old = lax.all_gather(old, "dp", axis=0, axis_index_groups=sides)
    attn, x_mid, h_mid = call(middle_kernel, "middle", [tile, tile, tile_b], *attn_terms, x_in, mods)
    h_mid = parts_of(h_mid)
    feed_b = joined(feed_way.finish())

    act_b, slope, *mlp_terms = call(
        feed_kernel,
        "feed",
        [((tokens, hidden), LOW), ((tokens, hidden), LOW), *terms],
        *(*h_mid, feed_b),
        flops=4 * tokens * D * hidden,
    )
    scales = jnp.stack([weight_tok, weight_tok / weight_total])
    mlp_terms, _ = parts_sum(*mlp_terms)
    d_out, d_mlp, d_head, end_sums, loss_part = call(
        final_kernel,
        "final",
        [tile, tile_b, thin_grad, sums, ((1, 128), F32)],
        *(scales, *mlp_terms, x_mid, mods, head_b, noi),
        scalars=1,
    )

    d_mlp = parts_of(d_mlp)
    d_mlp[3] = after(d_mlp[3], old)
    flops = 2 * tokens * D * hidden
    d_upper, *terms_mid = call(
        feed_back_kernel,
        "feed_back",
        [((tokens, hidden), LOW), *terms],
        *(*d_mlp, slope, feed_b),
        flops=2 * flops,
    )
    terms_mid, sent = parts_sum(*terms_mid)
    act_late, d_upper = lax.optimization_barrier((act_b, d_upper, sent))[:2]
    fc2_terms = call(feed_grads_kernel, "feed_grads", shares, *d_mlp, act_late, flops=flops)
    fc2_way = Course(sum_steps(*fc2_terms, "dp"))
    fc1_terms = call(feed_grads_kernel, "feed_grads", shares, *h_mid, d_upper, flops=flops)
    fc1_way = Course(sum_steps(*fc1_terms, "dp"))
    d_mid, d_attn, mid_sums = call(
        turn_kernel, "turn", [tile, tile_b, sums], *terms_mid, x_mid, d_out, attn, mods
    )
    d_attn = parts_of(d_attn)
    d_attn[1] = fc2_way.step(d_attn[1])
    d_attn[3] = fc1_way.step(fc2_way.step(d_attn[3]))
    d_qkv, even, odd = call(
        attend_back_kernel,
        "attend_back",
        [((tokens, 3 * width), LOW), *terms],
        *(alone, qkv, totals, *d_attn, qkv_b, out_b),
        scalars=1,
        scratch=[((width, tokens), LOW)]
        + [((width // HEAD_DIM, tokens, HEAD_DIM), F32)] * 2
        + [((tokens, width), LOW)],
        flops=20 * tokens * tokens * width + 8 * tokens * D * width,
    )
    odd = fc1_way.step(fc2_way.step(odd))
    sum_fc2 = fc2_way.finish()
    fc2_way = Course(gather_steps(sum_fc2.astype(LOW), "dp"))
    terms_in, sent = parts_sum(even, odd)
    at_terms = call(
        attend_grads_kernel,
        "attend_grads",
        shares,
        *(*h_in, after(d_qkv, sent), *d_attn, mixed_b),
        flops=8 * tokens * D * width,
    )
    at_way = Course(sum_steps(*at_terms, "dp"))
    terms_in[2] = fc2_way.step(fc1_way.step(terms_in[2], behind=at_terms[1]), behind=at_terms[1])
    sum_fc1 = fc1_way.finish()
    fc1_way = Course(gather_steps(sum_fc1.astype(LOW), "dp"))
    d_patch, d_mods = call(
        leave_kernel, "leave", [thin_grad, sums], *terms_in, x_in, d_mid, mods, noisy_b, mid_sums, end_sums
    )

    d_mods = from_local(d_mods, me, n_dp).reshape(8, n_mp, width).transpose(1, 0, 2)
    blocks = jnp.broadcast_to(d_mods[None], (n_dp,) + d_mods.shape).reshape((n_dp * n_mp,) + d_mods.shape[1:])
    blocks = exchange(blocks, ("dp", "mp")).reshape(n_dp, n_mp, 8, width)
    blocks = at_way.step(blocks, blocks)
    first_only = (jnp.arange(SLOTS) == 0)[:, None, None]
    d_mod_all = jnp.where(
        singles[:, None, None, None], jnp.where(first_only, jnp.sum(blocks, 1, keepdims=True), 0.0), blocks
    )
    d_mod_all = d_mod_all.astype(LOW).reshape(slots_all, 8 * width)
    g_mod = dot(silu_c_b, d_mod_all, DOWN)
    d_cond_part = dot(d_mod_all, mod_b, ACROSS) * silu_slope(cond)
    d_silu_t_part = lax.dot_general(d_cond_part, time2_b.astype(F32), ALONG, precision=HIGH)
    thick = jnp.concatenate(
        [d_silu_t_part.reshape(-1, n_dp, rows), from_local(jnp.concatenate([d_patch, d_head], 0), me, n_dp)], 0
    )
    thick = jnp.sum(exchange(thick.transpose(1, 0, 2), "dp"), 0)
    for way in (at_way, fc1_way, fc2_way, fc2_way):
        thick = way.step(thick, thick)
    thick = sum_all(jnp.concatenate([thick, d_cond_part], 0), "mp")
    hidden_t = dot(feat_b, time1_own, ACROSS)
    d_hidden = thick[:slots_all] * silu_slope(hidden_t)
    g_patch = thick[slots_all : slots_all + PIN]
    g_head = thick[slots_all + PIN : slots_all + 2 * PIN].T
    d_cond = thick[slots_all + 2 * PIN :]
    right = jnp.concatenate(
        [
            jnp.concatenate([jnp.zeros((slots_all, PIN), LOW), feat_b, jnp.zeros((slots_all, D + CLASSES), LOW)], 1),
            jnp.eye(PIN, PIN + FREQ + D + CLASSES, dtype=LOW),
            jnp.concatenate([jnp.zeros((slots_all, PIN + FREQ), LOW), silu_t_b, onehot], 1),
        ],
        0,
    )
    g_cond = dot(
        jnp.concatenate(thirds(jnp.concatenate([d_hidden, g_patch, d_cond], 0)), 0),
        jnp.concatenate([right] * 3, 0),
        DOWN,
    )

    square = lambda g: jnp.sum(g * g)
    sum_at = at_way.finish()
    split_sq = square(sum_fc1) + square(sum_fc2) + square(sum_at) + square(g_mod)
    tally = jnp.stack([split_sq + (square(g_head) + square(g_cond)) / n_mp, loss_part[0, 0]])
    tally = jnp.sum(spread(jnp.broadcast_to(tally[:, None], (2, 128)), ("dp", "mp")), 0)
    tally = fc1_way.step(fc1_way.step(fc2_way.step(tally)), tally)
    grad_norm = jnp.sqrt(tally[0, 0])
    loss_sum = tally[1, 0]
    coef = jnp.minimum(1.0, CLIP / (grad_norm + 1e-06))

    halves_of = lambda way: [g.reshape(n_dp // 2, rows, -1) for g in way.finish()]
    all_fc2 = halves_of(fc2_way)
    all_fc1 = halves_of(fc1_way)
    factor = coef[None]
    all_at = jnp.broadcast_to(sum_at.astype(LOW)[None], (n_dp,) + sum_at.shape)
    all_at = exchange(after(all_at, factor), "dp")
    span = 8 * width

    silu_c_all = old[:, :, :, 11 * width : 11 * width + slots_all]

    def one_mod():
        return muon_rows(places, factor, old, (span, 0), (0, span), (silu_c_all, d_mod_all))

    def one_fc2():
        mine = muon_rows(places, factor, old, (hidden, 1), (0, hidden), all_fc2)
        return jnp.pad(mine, ((0, 0), (0, 0), (0, span - hidden)))

    def one_fc1():
        mine = muon_rows(places, factor, old, (hidden, 0), (0, hidden), all_fc1)
        return jnp.concatenate([both[:, :, :hidden], mine], 2)

    at_block = (4 * width, 2)

    def one_qkv():
        return muon_rows(places, factor, old, at_block, (0, 3 * width), (all_at,), (0, 3 * width))

    def one_out():
        mine = muon_rows(places, factor, old, at_block, (0, width), (all_at,), (3 * width, 4 * width))
        return jnp.pad(mine, ((0, 0), (0, 0), (0, 2 * width)))

    both = lax.cond(near == 0, one_mod, one_fc2)
    both = lax.cond(near == 0, lambda: both, one_fc1)
    last = lax.cond(near == 0, one_qkv, one_out)
    both = after(both, last)
    new_weights, new_moms = finish(
        near[None],
        factor,
        (both[0], swap(both[1], "dp", 1), last[0], swap(last[1], "dp", 1), sum_at, sum_fc1, sum_fc2, g_mod),
        (w_qkv, w_out, w_fc1, w_fc2, w_mod),
        (mom_qkv, mom_out, mom_fc1, mom_fc2, mom_mod),
    )
    coef = after(coef, last)

    adam_out = []
    for master, first, second, grad in (
        (w_head, first_head, second_head, g_head),
        (w_cond, first_cond, second_cond, g_cond),
    ):
        clipped = coef * grad
        first = BETA_ONE * first + (1.0 - BETA_ONE) * clipped
        second = BETA_TWO * second + (1.0 - BETA_TWO) * clipped * clipped
        update = first / (1.0 - BETA_ONE**STEP) / (jnp.sqrt(second / (1.0 - BETA_TWO**STEP)) + EPS_ADAM)
        adam_out.append((master - LR_ADAM * (update + DECAY * master), first, second))
    return (
        *new_weights,
        adam_out[0][0],
        adam_out[1][0],
        *new_moms,
        adam_out[0][1],
        adam_out[0][2],
        adam_out[1][1],
        adam_out[1][2],
        loss_sum,
        weight_total,
        grad_norm,
    )


def solution(mesh):
    row, wide, cube = P("dp", None), P("dp", "mp"), P("dp", None, "mp")
    in_specs = (
        *(row, row, P("dp"), row, row),
        *(cube, wide, wide, wide, cube, row, row),
        *(cube, wide, wide, wide, cube),
        *(row, row, row, row),
    )
    out_specs = (
        *(cube, wide, wide, wide, cube, row, row),
        *(cube, wide, wide, wide, cube),
        *(row, row, row, row),
        *(P(), P(), P()),
    )
    return jax.shard_map(body, mesh=mesh, in_specs=in_specs, out_specs=out_specs, check_vma=False)
```

```python
import functools
import math

import jax
import jax.numpy as jnp
from jax import lax
from jax.experimental import pallas as pl
from jax.experimental.pallas import tpu as pltpu
from jax.sharding import PartitionSpec as P

SIDE = 32
D = 768
HEAD_DIM = 64
CLASSES = 1001
FREQ = 256
PIN = 16
STEP = 10
SLOTS = 4

HIGH = lax.Precision.HIGHEST
GAMMA = 5.0
CLIP = 0.05
MU = 0.95
LR_MUON = 0.1
DECAY = 0.01
BETA_ONE = 0.9
BETA_TWO = 0.95
LR_ADAM = 0.08
EPS_ADAM = 1e-08
NS_COEF = (3.4445, -4.775, 2.0315)
NS_SHIFT = (0.0, 0.1, 0.5, 0.8, 0.8)
ACROSS = (((1,), (1,)), ((), ()))
DOWN = (((0,), (0,)), ((), ()))
ALONG = (((1,), (0,)), ((), ()))
LOW = jnp.bfloat16
F32 = jnp.float32


def dot(a, b, dims=ALONG):
    return lax.dot_general(a, b, dims, preferred_element_type=F32)


def order_of(size):
    order, bit = [0], size // 2
    while bit:
        order += [o ^ bit for o in order]
        bit //= 2
    return order


def swap(x, axis, bit):
    size = lax.axis_size(axis)
    return lax.ppermute(x, axis, [(i, i ^ bit) for i in range(size)])


def after(x, *others):
    return lax.optimization_barrier((x,) + others)[0]


class Course:
    def __init__(self, steps):
        self.steps = steps
        self.result = None
        self.flight = next(steps, None)

    def step(self, x, start=None, behind=None):
        arrived = self.flight
        if arrived is None:
            return x
        arrived = late(arrived, behind)
        x = after(x, *arrived) if isinstance(arrived, tuple) else after(x, arrived)
        try:
            self.flight = self.steps.send((arrived, start))
        except StopIteration as stop:
            self.flight, self.result = None, stop.value
        return x

    def finish(self):
        while self.flight is not None:
            self.step(jnp.zeros((), F32))
        return self.result


def late(x, start):
    if start is None:
        return x
    return lax.optimization_barrier((*x, start))[:-1] if isinstance(x, tuple) else after(x, start)


def gather_steps(x, axis):
    bit = lax.axis_size(axis) // 2
    start, last = None, 1
    while bit > last:
        other, start = yield swap(late(x, start), axis, bit)
        x = jnp.concatenate([x, other], 0)
        bit //= 2
    _, start = yield x
    other, start = yield swap(late(x, start), axis, bit)
    return x, other


def quarter_steps(x, axis):
    bit, start = lax.axis_size(axis) // 2, None
    while bit > 2:
        other, start = yield swap(late(x, start), axis, bit)
        x = jnp.concatenate([x, other], 0)
        bit //= 2
    x = late(x, start)
    (second, third), start = yield swap(x, axis, 2), swap(x, axis, 1)
    fourth, start = yield swap(late(second, start), axis, 1)
    return [x, second, third, fourth]


def joined(pair):
    return jnp.concatenate(pair, 0)


def sum_steps(keep, send, axis):
    bit, size = 1, lax.axis_size(axis)
    other, start = yield swap(send, axis, bit)
    total = keep + other.astype(F32)
    while bit < size // 2:
        bit *= 2
        half = total.shape[0] // 2
        other, start = yield swap(late(total[half:].astype(LOW), start), axis, bit)
        total = total[:half] + other.astype(F32)
    return total


def sum_all(x, axis):
    bit = 1
    while bit < lax.axis_size(axis):
        x = x + swap(x, axis, bit)
        bit *= 2
    return x


def parts_of(h):
    two = swap(h, "mp", 2)
    one = swap(h, "mp", 1)
    return [h, one, two, swap(two, "mp", 1)]


def parts_sum(even, odd, then=lambda x: x):
    near = then(swap(odd, "mp", 1))
    send = (even[1] + near[1].astype(F32)).astype(LOW)
    return [even, near, swap(send, "mp", 2)], send


def turned_over(v, me):
    size, bit = v.shape[-2], 1
    lead, k = v.shape[:-2], v.shape[-1]
    while bit < size:
        pair = v.reshape(lead + (size // (2 * bit), 2, bit, k))
        flipped = jnp.concatenate([pair[..., 1:, :, :], pair[..., :1, :, :]], -3)
        v = jnp.where((me // bit) % 2 == 1, flipped, pair).reshape(lead + (size, k))
        bit *= 2
    return v


def to_local(v, me, size):
    blocks = turned_over(v.reshape(v.shape[:-1] + (size, v.shape[-1] // size)), me)
    return jnp.concatenate([blocks[..., o, :] for o in order_of(size)], -1)


def from_local(v, me, size):
    blocks = v.reshape(v.shape[:-1] + (size, v.shape[-1] // size))
    order = order_of(size)
    return turned_over(jnp.stack([blocks[..., order.index(k), :] for k in range(size)], -2), me)


def spread(x, axis):
    size = math.prod(lax.axis_size(a) for a in ((axis,) if isinstance(axis, str) else axis))
    copies = jnp.broadcast_to(x[None], (size,) + x.shape)
    return lax.all_to_all(copies, axis, 0, 0, tiled=True)


def exchange(x, axis):
    return lax.all_to_all(x, axis, 0, 0, tiled=True)


def plan():
    betas = jnp.linspace(0.0001, 0.02, 1000, dtype=F32)
    return jnp.cumprod(1.0 - betas)


def pick(table, index):
    grid = jnp.arange(table.shape[0], dtype=jnp.int32)
    return jnp.sum(jnp.where(index[..., None] == grid, table, 0.0), -1)


def normalize(x):
    cent = x - jnp.mean(x, -1, keepdims=True)
    inv = lax.rsqrt(jnp.mean(cent * cent, -1, keepdims=True) + 1e-06)
    return cent * inv, inv


def norm_back(grad, unit, inv, scale):
    d_shift = jnp.sum(grad, 0, keepdims=True)
    d_scale = jnp.sum(grad * unit, 0, keepdims=True)
    g = grad * (1.0 + scale)
    dx = inv * (g - jnp.mean(g, -1, keepdims=True) - unit * jnp.mean(g * unit, -1, keepdims=True))
    return dx, d_shift, d_scale


def place_table(column):
    quarter = D // 4
    omega = 1.0 / 10000.0 ** ((column % quarter).astype(F32) / quarter)
    angle = jnp.arange(SIDE, dtype=F32)[:, None] * omega
    wave = jnp.where((column // quarter) % 2 == 0, jnp.sin(angle), jnp.cos(angle))
    down = column < D // 2
    return jnp.concatenate([jnp.where(down, wave, 0.0), jnp.where(down, 0.0, wave)], 0)


def place_select(single, part, rank):
    local = jnp.arange(part, dtype=jnp.int32)
    full = rank * part + local
    half = SIDE // 2
    down = jnp.where(single, full // SIDE, local // half)
    across = jnp.where(single, full % SIDE, local % half)
    grid = jnp.arange(SIDE, dtype=jnp.int32)
    return jnp.concatenate([down[:, None] == grid, across[:, None] == grid], 1)


def thirds(x):
    high = x.astype(LOW)
    rest = x - high.astype(F32)
    mid = rest.astype(LOW)
    return high, mid, (rest - mid.astype(F32)).astype(LOW)


def time_features(steps):
    half = FREQ // 2
    freqs = jnp.exp(-math.log(10000.0) * jnp.arange(half, dtype=F32) / half)
    angles = steps.astype(F32)[:, None] * freqs
    return jnp.concatenate([jnp.cos(angles), jnp.sin(angles)], -1)


def silu_slope(x):
    s = jax.nn.sigmoid(x)
    return s * (1.0 + x * (1.0 - s))


def call(kernel, name, outs, *args, scalars=0, scratch=(), flops=0, vmem_mb=16):
    smem, vmem = pl.BlockSpec(memory_space=pltpu.SMEM), pl.BlockSpec(memory_space=pltpu.VMEM)
    size = sum(math.prod(o[0]) * jnp.dtype(o[1]).itemsize for o in outs)
    return pl.pallas_call(
        kernel,
        out_shape=[jax.ShapeDtypeStruct(*o) for o in outs],
        in_specs=[smem] * scalars + [vmem] * (len(args) - scalars),
        out_specs=[vmem] * len(outs),
        scratch_shapes=[pltpu.VMEM(*t) for t in scratch],
        compiler_params=pltpu.CompilerParams(vmem_limit_bytes=vmem_mb * 2**20),
        cost_estimate=pl.CostEstimate(flops=1, bytes_accessed=1, transcendentals=0),
        name=name,
    )(*args)


def turned(x):
    return x.astype(F32).T.astype(x.dtype)


def added(even_ref, near_ref, far_ref):
    return even_ref[0] + near_ref[0].astype(F32) + far_ref[...].astype(F32)


def pack_kernel(near_ref, slots_ref, m_mod, m_qkv, m_fc1, m_fc2, m_out, own_ref, other_ref):
    width, hidden = m_out.shape[1], m_fc1.shape[1]

    def put(even, odd):
        at = 0
        for piece in [m_mod[:, k] for k in range(8)] + [m_qkv[k] for k in range(3)] + [slots_ref[...].astype(F32)]:
            even[:, at : at + width] = piece.astype(LOW)
            at += width
        odd[:, :hidden] = m_fc1[...].astype(LOW)
        odd[:, hidden : 2 * hidden] = m_fc2[...].astype(LOW)
        odd[:, 2 * hidden : 2 * hidden + width] = m_out[...].astype(LOW)
        odd[:, 2 * hidden + width :] = jnp.zeros((odd.shape[0], 3 * width), LOW)

    @pl.when(near_ref[0] == 0)
    def _():
        put(own_ref.at[0], other_ref)

    @pl.when(near_ref[0] != 0)
    def _():
        put(other_ref, own_ref.at[0])


def pack(near, slots, m_mod, m_qkv, m_fc1, m_fc2, m_out):
    shape = (m_mod.shape[0], 12 * m_out.shape[1])
    return call(
        pack_kernel,
        "pack",
        [((2,) + shape, LOW), (shape, LOW)],
        *(near, slots, m_mod, m_qkv.transpose(1, 0, 2), m_fc1, m_fc2, m_out),
        scalars=1,
    )


def enter_kernel(x_ref, mods_ref, h_ref):
    unit, _ = normalize(x_ref[...])
    h_ref[...] = (unit * (1.0 + mods_ref[1:2, :]) + mods_ref[0:1, :]).astype(LOW)


def middle_kernel(even_ref, near_ref, far_ref, x_ref, mods_ref, attn_ref, mid_ref, h_ref):
    attn = added(even_ref, near_ref, far_ref)
    attn_ref[...] = attn
    mid = x_ref[...] + mods_ref[2:3, :] * attn
    mid_ref[...] = mid
    unit, _ = normalize(mid)
    h_ref[...] = (unit * (1.0 + mods_ref[4:5, :]) + mods_ref[3:4, :]).astype(LOW)


def final_kernel(
    scale_ref, even_ref, near_ref, far_ref, mid_ref, mods_ref, head_ref, noise_ref,
    out_ref, mlp_ref, head_grad_ref, sums_ref, loss_ref,
):
    mlp = added(even_ref, near_ref, far_ref)
    unit, inv = normalize(mid_ref[...] + mods_ref[5:6, :] * mlp)
    h = (unit * (1.0 + mods_ref[7:8, :]) + mods_ref[6:7, :]).astype(LOW)
    diff = dot(h, head_ref[...], ACROSS) - noise_ref[...]
    loss = jnp.sum(jnp.sum(diff * diff, axis=1, keepdims=True), axis=0, keepdims=True)
    loss_ref[...] = jnp.broadcast_to(scale_ref[0] * loss, loss_ref.shape)
    d_pred = (2.0 * diff * scale_ref[1]).astype(LOW)
    head_grad_ref[...] = dot(d_pred, h, DOWN)
    d_out, d_shift, d_scale = norm_back(dot(d_pred, head_ref[...]), unit, inv, mods_ref[7:8, :])
    out_ref[...] = d_out
    mlp_ref[...] = (d_out * mods_ref[5:6, :]).astype(LOW)
    sums_ref[0:1, :] = jnp.sum(d_out * mlp, 0, keepdims=True)
    sums_ref[1:2, :] = d_shift
    sums_ref[2:3, :] = d_scale


def turn_kernel(
    even_ref, near_ref, far_ref, mid_ref, out_ref, attn_ref, mods_ref, d_mid_ref, d_attn_ref, sums_ref
):
    unit, inv = normalize(mid_ref[...])
    dx, d_shift, d_scale = norm_back(added(even_ref, near_ref, far_ref), unit, inv, mods_ref[4:5, :])
    d_mid = out_ref[...] + dx
    d_mid_ref[...] = d_mid
    d_attn_ref[...] = (d_mid * mods_ref[2:3, :]).astype(LOW)
    sums_ref[0:1, :] = jnp.sum(d_mid * attn_ref[...], 0, keepdims=True)
    sums_ref[1:2, :] = d_shift
    sums_ref[2:3, :] = d_scale


def leave_kernel(
    even_ref, near_ref, far_ref, x_ref, d_mid_ref, mods_ref, noisy_ref, mid_sums_ref, end_sums_ref,
    patch_ref, sums_ref,
):
    unit, inv = normalize(x_ref[...])
    dx, d_shift, d_scale = norm_back(added(even_ref, near_ref, far_ref), unit, inv, mods_ref[1:2, :])
    patch_ref[...] = dot(noisy_ref[...], (d_mid_ref[...] + dx).astype(LOW), DOWN)
    sums_ref[0:1, :] = d_shift
    sums_ref[1:2, :] = d_scale
    sums_ref[2:5, :] = mid_sums_ref[0:3, :]
    sums_ref[5:8, :] = end_sums_ref[0:3, :]


def attend_kernel(
    single_ref, h0_ref, h1_ref, h2_ref, h3_ref, w_ref, o_ref,
    qkv_ref, total_ref, mixed_ref, even_ref, odd_ref, vt_ref,
):
    part = h0_ref.shape[0]
    width = mixed_ref.shape[1]
    for j, ref in enumerate((h0_ref, h1_ref, h2_ref, h3_ref)):
        qkv_ref[j * part : (j + 1) * part, :] = dot(ref[...], w_ref[...]).astype(LOW)
    vt_ref[...] = turned(qkv_ref[:, 2 * width :])

    def run(i, keys):
        mine = pl.ds(pl.multiple_of(i * part, part), part)
        outs = []
        for h in range(width // HEAD_DIM):
            lo = h * HEAD_DIM
            q = qkv_ref[mine, lo : lo + HEAD_DIM] * HEAD_DIM**-0.5
            k = qkv_ref[keys, width + lo : width + lo + HEAD_DIM]
            s = dot(k, q, ACROSS)
            top = jnp.max(s, axis=0, keepdims=True)
            e = jnp.exp(s - top)
            z = jnp.sum(e, axis=0, keepdims=True)
            total_ref[h : h + 1, mine] = top + jnp.log(z)
            outs.append(dot(vt_ref[lo : lo + HEAD_DIM, keys], (e * (1.0 / z)).astype(LOW)))
        mixed_ref[mine, :] = jnp.concatenate(outs, 0).T.astype(LOW)

    def block(i, carry):
        mine = pl.ds(pl.multiple_of(i * part, part), part)

        @pl.when(single_ref[0] == 1)
        def _():
            run(i, slice(None))

        @pl.when(single_ref[0] != 1)
        def _():
            run(i, mine)

        return carry

    lax.fori_loop(0, 4, block, 0)
    for j in range(4):
        term = dot(mixed_ref[j * part : (j + 1) * part, :], o_ref[...], ACROSS)
        if j % 2 == 0:
            even_ref[j // 2] = term
        else:
            odd_ref[j // 2] = term.astype(LOW)


def attend_back_kernel(
    single_ref, qkv_ref, total_ref, d0_ref, d1_ref, d2_ref, d3_ref, w_ref, o_ref,
    grad_ref, even_ref, odd_ref, kt_ref, dk_ref, dv_ref, g_ref,
):
    part = d0_ref.shape[0]
    width = qkv_ref.shape[1] // 3
    heads = width // HEAD_DIM
    for j, ref in enumerate((d0_ref, d1_ref, d2_ref, d3_ref)):
        g_ref[j * part : (j + 1) * part, :] = dot(ref[...], o_ref[...]).astype(LOW)
    kt_ref[...] = turned(qkv_ref[:, width : 2 * width] * HEAD_DIM**-0.5)
    dk_ref[...] = jnp.zeros_like(dk_ref)
    dv_ref[...] = jnp.zeros_like(dv_ref)

    def run(i, keys):
        mine = pl.ds(pl.multiple_of(i * part, part), part)
        outs = []
        for h in range(heads):
            lo = h * HEAD_DIM
            q = qkv_ref[mine, lo : lo + HEAD_DIM] * HEAD_DIM**-0.5
            k = qkv_ref[keys, width + lo : width + lo + HEAD_DIM]
            v = qkv_ref[keys, 2 * width + lo : 2 * width + lo + HEAD_DIM]
            g = g_ref[mine, lo : lo + HEAD_DIM]
            p = jnp.exp(dot(k, q, ACROSS) - total_ref[h : h + 1, mine])
            dp = dot(v, g, ACROSS)
            delta = jnp.sum(dp * p, axis=0, keepdims=True)
            ds = (p * (dp - delta)).astype(LOW)
            dv_ref[h, keys, :] += dot(p.astype(LOW), g)
            dk_ref[h, keys, :] += dot(ds, q)
            outs.append(dot(kt_ref[lo : lo + HEAD_DIM, keys], ds))
        grad_ref[mine, :width] = jnp.concatenate(outs, 0).T.astype(LOW)

    def block(i, carry):
        @pl.when(single_ref[0] == 1)
        def _():
            run(i, slice(None))

        @pl.when(single_ref[0] != 1)
        def _():
            run(i, pl.ds(pl.multiple_of(i * part, part), part))

        return carry

    lax.fori_loop(0, 4, block, 0)
    for h in range(heads):
        lo = h * HEAD_DIM
        grad_ref[:, width + lo : width + lo + HEAD_DIM] = dk_ref[h].astype(LOW)
        grad_ref[:, 2 * width + lo : 2 * width + lo + HEAD_DIM] = dv_ref[h].astype(LOW)
    for j in range(4):
        term = dot(grad_ref[j * part : (j + 1) * part, :], w_ref[...], ACROSS)
        if j % 2 == 0:
            even_ref[j // 2] = term
        else:
            odd_ref[j // 2] = term.astype(LOW)


def halves(keep_ref, send_ref, columns, value):
    half = keep_ref.shape[0]
    keep_ref[:, columns] = value[:half]
    send_ref[:, columns] = value[half:].astype(LOW)


def attend_grads_kernel(h0, h1, h2, h3, grad_ref, d0, d1, d2, d3, mixed_ref, keep_ref, send_ref):
    part, width = h0.shape[0], mixed_ref.shape[1]
    rows = lambda j: slice(j * part, (j + 1) * part)
    halves(
        keep_ref, send_ref, slice(0, 3 * width),
        sum(dot(h[...], grad_ref[rows(j), :], DOWN) for j, h in enumerate((h0, h1, h2, h3))),
    )
    halves(
        keep_ref, send_ref, slice(3 * width, 4 * width),
        sum(dot(d[...], mixed_ref[rows(j), :], DOWN) for j, d in enumerate((d0, d1, d2, d3))),
    )


def feed_kernel(h0, h1, h2, h3, w_ref, act_ref, slope_ref, even_ref, odd_ref):
    part, hidden = h0.shape[0], act_ref.shape[1]
    for j, h in enumerate((h0, h1, h2, h3)):
        rows = slice(j * part, (j + 1) * part)
        upper = dot(h[...], w_ref[:, :hidden])
        gate = 0.5 * (1.0 + lax.erf(upper * 0.5**0.5))
        act = (upper * gate).astype(LOW)
        act_ref[rows, :] = act
        slope = gate + upper * jnp.exp(-0.5 * upper * upper) * (2.0 * math.pi) ** -0.5
        slope_ref[rows, :] = slope.astype(LOW)
        term = dot(act, w_ref[:, hidden:], ACROSS)
        if j % 2 == 0:
            even_ref[j // 2] = term
        else:
            odd_ref[j // 2] = term.astype(LOW)


def feed_back_kernel(d0, d1, d2, d3, slope_ref, w_ref, upper_ref, even_ref, odd_ref):
    part, hidden = d0.shape[0], slope_ref.shape[1]
    for j, d in enumerate((d0, d1, d2, d3)):
        rows = slice(j * part, (j + 1) * part)
        d_upper = (dot(d[...], w_ref[:, hidden:]) * slope_ref[rows, :].astype(F32)).astype(LOW)
        upper_ref[rows, :] = d_upper
        term = dot(d_upper, w_ref[:, :hidden], ACROSS)
        if j % 2 == 0:
            even_ref[j // 2] = term
        else:
            odd_ref[j // 2] = term.astype(LOW)


def feed_grads_kernel(h0, h1, h2, h3, x_ref, keep_ref, send_ref):
    part = h0.shape[0]
    value = sum(
        dot(h[...], x_ref[j * part : (j + 1) * part, :], DOWN) for j, h in enumerate((h0, h1, h2, h3))
    )
    halves(keep_ref, send_ref, slice(None), value)


def muon_kernel(columns, span, order_ref, coef_ref, plan_ref, mom_ref, *refs):
    grads, (out_ref, x_ref, b_ref, e_ref, r_ref, turn_ref) = refs[:-6], refs[-6:]
    third = NS_COEF[2]
    size, width = x_ref.shape
    count, pairs = mom_ref.shape[2], mom_ref.shape[0]
    coef = coef_ref[0]
    spans = [slice(i, min(i + size, width)) for i in range(0, width, size)]

    tall = size < count * 2 * pairs
    squares = jnp.zeros((1, 1), F32)
    for place in range(2 * pairs):
        true = order_ref[place]
        if len(grads) == 1:
            grad = grads[0][true, :, slice(*span)].astype(F32)
        elif len(grads) == 2:
            grad = dot(grads[0][lax.shift_right_logical(true, 1), place // pairs], grads[1][...])
        else:
            quarter, row = divmod(place * count, grads[0].shape[0])
            grad = grads[quarter][row : row + count, :].astype(F32)
        mom = mom_ref[lax.shift_right_logical(true, 1), place // pairs, :, slice(*columns)]
        x = MU * mom.astype(F32) + coef * grad
        if tall:
            turn_ref[place * count : (place + 1) * count, :] = x
        else:
            x_ref[place * count : (place + 1) * count, :] = x
        squares = squares + jnp.sum(jnp.sum(x * x, axis=0, keepdims=True), axis=1, keepdims=True)
    inv = 1.0 / (jnp.sqrt(squares) + 1e-07)
    x_ref[...] = (turn_ref[...].T if tall else x_ref[...]) * inv
    b_ref[...] = x_ref[...].astype(LOW)

    def gram(shift):
        e = sum(dot(b_ref[:, span], b_ref[:, span], ACROSS) for span in spans)
        row = lax.broadcasted_iota(jnp.int32, e.shape, 0)
        column = lax.broadcasted_iota(jnp.int32, e.shape, 1)
        e = e - jnp.where(row == column, shift, 0.0)
        e_ref[...] = e
        r_ref[...] = e.astype(LOW)

    def turn(i, carry):
        centre, slope = plan_ref[i, 0], plan_ref[i, 1]
        gram(plan_ref[i, 2])
        r_ref[...] = (slope * e_ref[...] + third * dot(r_ref[...], r_ref[...])).astype(LOW)
        for span in spans:
            x = centre * x_ref[:, span] + dot(r_ref[...], b_ref[:, span])
            x_ref[:, span] = x
            b_ref[:, span] = x.astype(LOW)
        return carry

    last = len(NS_SHIFT) - 1
    lax.fori_loop(0, last, turn, 0)
    gram(plan_ref[last, 2])
    both = [slice(0, count), slice(pairs * count, (pairs + 1) * count)]
    scaled = 0.2 * math.sqrt(max(size, width))
    if tall:
        poly = plan_ref[last, 1] * e_ref[...] + third * dot(r_ref[...], r_ref[...])
        x = jnp.concatenate([x_ref[:, own].T for own in both], 0)
        x = scaled * (plan_ref[last, 0] * x + dot(x.astype(LOW), poly.astype(LOW)))
        out_ref[0] = x[:count].astype(LOW)
        out_ref[1] = x[count:].astype(LOW)
        return
    e = jnp.concatenate([e_ref[own, :] for own in both], 0)
    poly = (plan_ref[last, 1] * e + third * dot(e.astype(LOW), r_ref[...])).astype(LOW)
    for span in spans:
        x = jnp.concatenate([x_ref[own, span] for own in both], 0)
        x = scaled * (plan_ref[last, 0] * x + dot(poly, b_ref[:, span]))
        out_ref[0, :, span] = x[:count].astype(LOW)
        out_ref[1, :, span] = x[count:].astype(LOW)


def muon_rows(order, coef, old, block, columns, grads, span=None):
    pairs, _, count, _ = old.shape
    deep, width = 2 * pairs * count, columns[1] - columns[0]
    size, long = (width, deep) if 2 * width <= deep else (deep, width)
    first, second, third = NS_COEF
    plan = [[first + second * s + third * s * s, second + 2.0 * third * s, s] for s in NS_SHIFT]
    smem, vmem = pl.BlockSpec(memory_space=pltpu.SMEM), pl.BlockSpec(memory_space=pltpu.VMEM)
    return pl.pallas_call(
        functools.partial(muon_kernel, columns, span),
        grid=(1,),
        out_shape=jax.ShapeDtypeStruct((2, count, width), LOW),
        in_specs=[smem, smem, smem, pl.BlockSpec((pairs, 2, count, block[0]), lambda i: (0, 0, 0, block[1]))]
        + [vmem] * len(grads),
        out_specs=vmem,
        scratch_shapes=[
            pltpu.VMEM((size, long), F32),
            pltpu.VMEM((size, long), LOW),
            pltpu.VMEM((size, size), F32),
            pltpu.VMEM((size, size), LOW),
            pltpu.VMEM((deep, width) if size < deep else (8, 128), F32),
        ],
        compiler_params=pltpu.CompilerParams(vmem_limit_bytes=32 * 2**20),
        cost_estimate=pl.CostEstimate(flops=1, bytes_accessed=1, transcendentals=0),
        name="muon",
    )(order, coef, jnp.array(plan, F32), old, *grads)


def weights_kernel(near_ref, own_a, got_a, own_b, got_b, w_qkv, w_out, w_fc1, w_fc2, w_mod, n_qkv, n_out, n_fc1, n_fc2, n_mod):
    width, hidden = w_out.shape[1], w_fc1.shape[1]
    mine = near_ref[0] == 0

    def put(place, weight, new, update):
        new[place] = weight[place] * (1.0 - LR_MUON * DECAY) - LR_MUON * update

    a, b = own_a[...].astype(F32), got_a[...].astype(F32)
    u_mod, u_fc = jnp.where(mine, a, b), jnp.where(mine, b, a)
    a, b = own_b[...].astype(F32), got_b[...].astype(F32)
    u_qkv, u_out = jnp.where(mine, a, b), jnp.where(mine, b, a)[:, :width]
    for k in range(3):
        put(k, w_qkv, n_qkv, u_qkv[:, k * width : (k + 1) * width])
    for k in range(8):
        put((slice(None), k), w_mod, n_mod, u_mod[:, k * width : (k + 1) * width])
    put(slice(None), w_out, n_out, u_out)
    put(slice(None), w_fc2, n_fc2, u_fc[:, :hidden])
    put(slice(None), w_fc1, n_fc1, u_fc[:, hidden:])


def momenta_kernel(coef_ref, g_at, g_fc1, g_fc2, g_mod, m_qkv, m_out, m_fc1, m_fc2, m_mod, k_qkv, k_out, k_fc1, k_fc2, k_mod):
    width = m_out.shape[1]
    coef = coef_ref[0]

    def put(place, mom, kept, grad):
        kept[place] = MU * mom[place] + coef * grad

    for k in range(3):
        put(k, m_qkv, k_qkv, g_at[:, k * width : (k + 1) * width])
    for k in range(8):
        put((slice(None), k), m_mod, k_mod, g_mod[:, k * width : (k + 1) * width])
    put(slice(None), m_out, k_out, g_at[:, 3 * width :])
    put(slice(None), m_fc2, k_fc2, g_fc2[...])
    put(slice(None), m_fc1, k_fc1, g_fc1[...])


def by_rows(kernel, name, scalar, flats, arrays):
    rows = flats[0].shape[0]
    step = rows // 2 if rows % 32 == 0 else rows

    def block(a):
        if a.ndim == 2:
            return pl.BlockSpec((step, a.shape[1]), lambda i: (i, 0))
        if a.shape[0] == rows:
            return pl.BlockSpec((step,) + a.shape[1:], lambda i: (i, 0, 0))
        return pl.BlockSpec((a.shape[0], step, a.shape[2]), lambda i: (0, i, 0))

    arrays = [arrays[0].transpose(1, 0, 2), *arrays[1:]]
    outs = pl.pallas_call(
        kernel,
        grid=(rows // step,),
        out_shape=[jax.ShapeDtypeStruct(a.shape, F32) for a in arrays],
        in_specs=[pl.BlockSpec(memory_space=pltpu.SMEM)] + [block(a) for a in (*flats, *arrays)],
        out_specs=[block(a) for a in arrays],
        compiler_params=pltpu.CompilerParams(vmem_limit_bytes=32 * 2**20),
        name=name,
    )(scalar, *flats, *arrays)
    return [outs[0].transpose(1, 0, 2), *outs[1:]]


def body(
    latents,
    noise,
    segment_ids,
    timesteps,
    labels,
    w_qkv,
    w_out,
    w_fc1,
    w_fc2,
    w_mod,
    w_head,
    w_cond,
    mom_qkv,
    mom_out,
    mom_fc1,
    mom_fc2,
    mom_mod,
    first_head,
    second_head,
    first_cond,
    second_cond,
):
    n_dp, n_mp = lax.axis_size("dp"), lax.axis_size("mp")
    me, rank = lax.axis_index("dp"), lax.axis_index("mp")
    near = me % 2
    tokens = latents.shape[0]
    part = tokens // n_mp
    rows = w_qkv.shape[0]
    width = w_qkv.shape[2]
    hidden = w_fc1.shape[1]
    half = D // 2
    place = [me ^ o for o in order_of(n_dp)]
    places = me ^ jnp.array(order_of(n_dp), jnp.int32)

    single = jnp.max(segment_ids) == 0
    time1_own = w_cond[:, PIN : PIN + FREQ].astype(LOW)
    digits = [v for a in (timesteps, labels) for v in (a.reshape(-1) // SIDE, a.reshape(-1) % SIDE)]
    note = jnp.concatenate(digits + [single.astype(jnp.int32)[None]]).astype(LOW)
    note = jnp.pad(note, (0, FREQ - note.shape[0]))
    thin = jnp.concatenate([w_cond[:, :PIN].astype(LOW), w_head.astype(LOW)], 1).reshape(-1, FREQ)
    thin_rows = thin.shape[0]
    fill = -(rows + thin_rows) % 16 or 16
    packet = spread(jnp.concatenate([time1_own, thin, jnp.broadcast_to(note, (fill, FREQ))], 0), "dp")
    packet = packet.reshape(n_dp, rows + thin_rows + fill, FREQ)

    time1_b = packet[:, :rows].reshape(D, FREQ)
    thin = packet[:, rows : rows + thin_rows].reshape(n_dp, rows, 2 * PIN).astype(F32)
    thin = jnp.concatenate([lax.dynamic_index_in_dim(thin, p, 0) for p in place], 0)
    thin = thin.reshape(D, 2 * PIN).T.astype(LOW)
    patch_b, head_b = thin[:PIN], thin[PIN:]
    notes = packet[:, rows + thin_rows].astype(jnp.int32)
    steps = notes[:, :SLOTS] * SIDE + notes[:, SLOTS : 2 * SLOTS]
    kinds = (notes[:, 2 * SLOTS : 3 * SLOTS] * SIDE + notes[:, 3 * SLOTS : 4 * SLOTS]).reshape(-1)
    singles = notes[:, 4 * SLOTS] == 1

    time2_b = w_cond[:, PIN + FREQ : PIN + FREQ + D].astype(LOW)
    table_b = w_cond[:, PIN + FREQ + D :].astype(LOW)
    mod_b = jnp.concatenate([w_mod[:, k].astype(LOW) for k in range(8)], 1)
    feat_b = time_features(steps.reshape(-1)).astype(LOW)
    slots_all = feat_b.shape[0]
    silu_t_b = jax.nn.silu(dot(feat_b, time1_b, ACROSS)).astype(LOW)
    onehot = (kinds[:, None] == jnp.arange(CLASSES, dtype=jnp.int32)).astype(LOW)
    qkv_own = jnp.concatenate([w_qkv[:, k].astype(LOW) for k in range(3)] + [w_out.astype(LOW)], 1)
    proj_way = Course(gather_steps(after(qkv_own, silu_t_b), "dp"))
    cond = dot(silu_t_b, time2_b, ACROSS) + dot(onehot, table_b, ACROSS)
    silu_c_b = jax.nn.silu(cond).astype(LOW)
    mod_part = exchange(dot(silu_c_b, mod_b).reshape(n_dp, SLOTS, -1), "dp")
    mod_cols = jnp.sum(mod_part, 0).reshape(SLOTS, 8, width)
    mod_cols = proj_way.step(mod_cols, mod_cols)
    slots_own = jnp.pad(silu_c_b.T, ((0, 0), (0, width - slots_all)))
    own_pack, other_pack = pack(near[None], slots_own, mom_mod, mom_qkv, mom_fc1, mom_fc2, mom_out)
    other_pack = swap(other_pack, "dp", 1)
    part_slots = segment_ids[::part]
    outgoing = jnp.sum(
        jnp.where((part_slots[:, None] == jnp.arange(SLOTS))[:, :, None, None], mod_cols[None], 0.0), 1
    )
    mods = exchange(outgoing, "mp").transpose(1, 0, 2).reshape(8, n_mp * width)
    slot = jnp.sum(jnp.where(jnp.arange(n_mp) == rank, part_slots, 0))

    abar = pick(plan(), steps)
    snr = abar / (1.0 - abar)
    slot_weight = jnp.minimum(snr, GAMMA) / snr
    weight_total = part * jnp.sum(jnp.where(singles[:, None], n_mp * slot_weight[:, :1] / SLOTS, slot_weight))
    mine = (jnp.arange(n_dp)[:, None] == me) & (jnp.arange(SLOTS) == slot)
    my_slot = lambda a: jnp.sum(jnp.where(mine, a, 0.0))
    abar_tok, weight_tok = my_slot(abar), my_slot(slot_weight)
    right = jnp.concatenate(
        [
            jnp.concatenate([jnp.zeros((slots_all, PIN), LOW), feat_b, jnp.zeros((slots_all, D + CLASSES), LOW)], 1),
            jnp.eye(PIN, PIN + FREQ + D + CLASSES, dtype=LOW),
            jnp.concatenate([jnp.zeros((slots_all, PIN + FREQ), LOW), silu_t_b, onehot], 1),
        ],
        0,
    )
    right = jnp.concatenate([right] * 3, 0)
    scales = jnp.stack([weight_tok, weight_tok / weight_total])
    mods = after(to_local(mods, me, n_dp), other_pack, right, scales)
    lat = lax.dynamic_slice_in_dim(latents, rank * part, part, 0)
    noi = lax.dynamic_slice_in_dim(noise, rank * part, part, 0)
    noisy_b = (jnp.sqrt(abar_tok) * lat + jnp.sqrt(1.0 - abar_tok) * noi).astype(LOW)
    picks = place_select(single, part, rank).astype(LOW)
    left = jnp.concatenate([noisy_b, picks, picks, picks], 1)
    column = (after(places, silu_t_b)[:, None] * rows + jnp.arange(rows, dtype=jnp.int32)).reshape(-1)
    x_in = dot(left, jnp.concatenate([patch_b, *thirds(place_table(column))], 0))
    alone = single.astype(jnp.int32)[None]

    tile = ((part, D), F32)
    tile_b = ((part, D), LOW)
    terms = [((2, part, D), F32), ((2, part, D), LOW)]
    sums = ((8, D), F32)
    thin_grad = ((PIN, D), F32)
    shares = [((half, D), F32), ((half, D), LOW)]
    (h_in,) = call(enter_kernel, "enter", [tile_b], x_in, mods)
    h_in = proj_way.step(h_in)
    feed_own = jnp.concatenate([w_fc1, w_fc2], 1).astype(LOW)
    feed_way = Course(gather_steps(after(feed_own, h_in), "dp"))
    sides = [[side + 2 * i for i in range(n_dp // 2)] for side in range(2)]
    stacked = lax.dynamic_update_slice(own_pack, other_pack[None], (1, 0, 0))
    old = lax.all_gather(after(stacked, h_in), "dp", axis=0, axis_index_groups=sides)
    h_in = parts_of(h_in)
    h_in[1] = proj_way.step(h_in[1])
    h_in[3] = feed_way.step(h_in[3])
    proj = joined(proj_way.finish())
    qkv_b, out_b = proj[:, : 3 * width], proj[:, 3 * width :]
    qkv, totals, mixed_b, *attn_terms = call(
        attend_kernel,
        "attend",
        [((tokens, 3 * width), LOW), ((8, tokens), F32), ((tokens, width), LOW), *terms],
        *(alone, *h_in, qkv_b, out_b),
        scalars=1,
        scratch=[((width, tokens), LOW)],
        flops=8 * tokens * tokens * width + 8 * tokens * D * width,
    )
    attn_terms, _ = parts_sum(*attn_terms, lambda near: feed_way.step(feed_way.step(near)))
    attn, x_mid, h_mid = call(middle_kernel, "middle", [tile, tile, tile_b], *attn_terms, x_in, mods)
    h_mid = parts_of(h_mid)
    feed_b = joined(feed_way.finish())

    act_b, slope, *mlp_terms = call(
        feed_kernel,
        "feed",
        [((tokens, hidden), LOW), ((tokens, hidden), LOW), *terms],
        *(*h_mid, feed_b),
        flops=4 * tokens * D * hidden,
    )
    mlp_terms, _ = parts_sum(*mlp_terms)
    d_out, d_mlp, d_head, end_sums, loss_part = call(
        final_kernel,
        "final",
        [tile, tile_b, thin_grad, sums, ((1, 128), F32)],
        *(scales, *mlp_terms, x_mid, mods, head_b, noi),
        scalars=1,
    )

    d_mlp = parts_of(d_mlp)
    flops = 2 * tokens * D * hidden
    d_upper, *terms_mid = call(
        feed_back_kernel,
        "feed_back",
        [((tokens, hidden), LOW), *terms],
        *(*d_mlp, slope, feed_b),
        flops=2 * flops,
    )
    terms_mid, sent = parts_sum(*terms_mid)
    act_late, d_upper = lax.optimization_barrier((act_b, d_upper, sent))[:2]
    fc2_terms = call(feed_grads_kernel, "feed_grads", shares, *d_mlp, act_late, flops=flops)
    fc2_way = Course(sum_steps(*fc2_terms, "dp"))
    fc1_terms = call(feed_grads_kernel, "feed_grads", shares, *h_mid, d_upper, flops=flops)
    fc1_way = Course(sum_steps(*fc1_terms, "dp"))
    d_mid, d_attn, mid_sums = call(
        turn_kernel, "turn", [tile, tile_b, sums], *terms_mid, x_mid, d_out, attn, mods
    )
    d_attn = parts_of(after(d_attn, old))
    d_attn[1] = fc2_way.step(d_attn[1])
    d_attn[3] = fc1_way.step(fc2_way.step(d_attn[3]))
    d_qkv, even, odd = call(
        attend_back_kernel,
        "attend_back",
        [((tokens, 3 * width), LOW), *terms],
        *(alone, qkv, totals, *d_attn, qkv_b, out_b),
        scalars=1,
        scratch=[((width, tokens), LOW)]
        + [((width // HEAD_DIM, tokens, HEAD_DIM), F32)] * 2
        + [((tokens, width), LOW)],
        flops=20 * tokens * tokens * width + 8 * tokens * D * width,
    )
    odd = fc1_way.step(fc2_way.step(odd))
    sum_fc2 = fc2_way.finish()
    fc2_way = Course(quarter_steps(sum_fc2.astype(LOW), "dp"))
    terms_in, sent = parts_sum(even, odd)
    at_terms = call(
        attend_grads_kernel,
        "attend_grads",
        shares,
        *(*h_in, after(d_qkv, sent), *d_attn, mixed_b),
        flops=8 * tokens * D * width,
    )
    at_way = Course(sum_steps(*at_terms, "dp"))
    terms_in[2] = fc2_way.step(fc1_way.step(terms_in[2], behind=at_terms[1]), behind=at_terms[1])
    sum_fc1 = fc1_way.finish()
    fc1_way = Course(quarter_steps(sum_fc1.astype(LOW), "dp"))
    d_patch, d_mods = call(
        leave_kernel, "leave", [thin_grad, sums], *terms_in, x_in, d_mid, mods, noisy_b, mid_sums, end_sums
    )

    d_mods = from_local(d_mods, me, n_dp).reshape(8, n_mp, width).transpose(1, 0, 2)
    blocks = jnp.broadcast_to(d_mods[None], (n_dp,) + d_mods.shape).reshape((n_dp * n_mp,) + d_mods.shape[1:])
    blocks = exchange(blocks, ("dp", "mp")).reshape(n_dp, n_mp, 8, width)
    blocks = at_way.step(blocks, blocks)
    first_only = (jnp.arange(SLOTS) == 0)[:, None, None]
    d_mod_all = jnp.where(
        singles[:, None, None, None], jnp.where(first_only, jnp.sum(blocks, 1, keepdims=True), 0.0), blocks
    )
    d_mod_all = d_mod_all.astype(LOW).reshape(slots_all, 8 * width)
    g_mod = dot(silu_c_b, d_mod_all, DOWN)
    d_cond_part = dot(d_mod_all, mod_b, ACROSS) * silu_slope(cond)
    d_silu_t_part = lax.dot_general(d_cond_part, time2_b.astype(F32), ALONG, precision=HIGH)
    thick = jnp.concatenate(
        [d_silu_t_part.reshape(-1, n_dp, rows), from_local(jnp.concatenate([d_patch, d_head], 0), me, n_dp)], 0
    )
    thick = jnp.sum(exchange(thick.transpose(1, 0, 2), "dp"), 0)
    thick = jnp.concatenate([thick, d_cond_part], 0)
    chip = thick + swap(thick, "mp", 1)
    for way in (at_way, fc1_way, fc2_way):
        chip = way.step(chip, thick)
    thick = chip + swap(chip, "mp", 2)
    hidden_t = dot(feat_b, time1_own, ACROSS)
    d_hidden = thick[:slots_all] * silu_slope(hidden_t)
    g_patch = thick[slots_all : slots_all + PIN]
    g_head = thick[slots_all + PIN : slots_all + 2 * PIN].T
    d_cond = thick[slots_all + 2 * PIN :]
    g_cond = dot(
        jnp.concatenate(thirds(jnp.concatenate([d_hidden, g_patch, d_cond], 0)), 0),
        right,
        DOWN,
    )

    square = lambda g: jnp.sum(g * g)
    sum_at = at_way.finish()
    parts = [square(g) for g in (sum_fc1, sum_fc2, sum_at, g_mod, g_head, g_cond)] + [loss_part[0, 0]]
    share = jnp.array([1.0] * 4 + [1.0 / n_mp] * 2 + [1.0], F32)
    tally = jnp.pad(jnp.stack(parts) * share, (0, 128 - len(parts)))[None]
    tally = jnp.sum(spread(tally, ("dp", "mp")), 0)
    tally = fc1_way.step(fc2_way.step(tally), tally)
    lane = jnp.arange(128)[None]
    grad_norm = jnp.sqrt(jnp.sum(jnp.where(lane < 6, tally, 0.0), 1, keepdims=True))
    loss_sum = jnp.sum(jnp.where(lane == 6, tally, 0.0))
    coef = jnp.minimum(1.0, CLIP / (grad_norm + 1e-06))

    all_fc2 = fc2_way.finish()
    all_fc1 = fc1_way.finish()
    factor = coef.reshape(1)
    all_at = jnp.broadcast_to(sum_at.astype(LOW)[None], (n_dp,) + sum_at.shape)
    all_at = exchange(after(all_at, factor), "dp")
    span = 8 * width

    silu_c_all = old[:, :, :, 11 * width : 11 * width + slots_all]

    def one_mod():
        return muon_rows(places, factor, old, (span, 0), (0, span), (silu_c_all, d_mod_all))

    def one_fc2():
        mine = muon_rows(places, factor, old, (hidden, 1), (0, hidden), all_fc2)
        return jnp.pad(mine, ((0, 0), (0, 0), (0, span - hidden)))

    def one_fc1():
        mine = muon_rows(places, factor, old, (hidden, 0), (0, hidden), all_fc1)
        return jnp.concatenate([both[:, :, :hidden], mine], 2)

    at_block = (4 * width, 2)

    def one_qkv():
        return muon_rows(places, factor, old, at_block, (0, 3 * width), (all_at,), (0, 3 * width))

    def one_out():
        mine = muon_rows(places, factor, old, at_block, (0, width), (all_at,), (3 * width, 4 * width))
        return jnp.pad(mine, ((0, 0), (0, 0), (0, 2 * width)))

    both = lax.cond(near == 0, one_mod, one_fc2)
    both = lax.cond(near == 0, lambda: both, one_fc1)
    last = lax.cond(near == 0, one_qkv, one_out)
    both = after(both, last)
    new_moms = by_rows(
        momenta_kernel,
        "momenta",
        after(factor, last),
        (sum_at, sum_fc1, sum_fc2, g_mod),
        (mom_qkv, mom_out, mom_fc1, mom_fc2, mom_mod),
    )
    new_weights = by_rows(
        weights_kernel,
        "weights",
        near[None],
        (both[0], swap(both[1], "dp", 1), last[0], swap(last[1], "dp", 1)),
        (w_qkv, w_out, w_fc1, w_fc2, w_mod),
    )
    coef = after(coef, last)

    adam_out = []
    for master, first, second, grad in (
        (w_head, first_head, second_head, g_head),
        (w_cond, first_cond, second_cond, g_cond),
    ):
        clipped = coef * grad
        first = BETA_ONE * first + (1.0 - BETA_ONE) * clipped
        second = BETA_TWO * second + (1.0 - BETA_TWO) * clipped * clipped
        update = first / (1.0 - BETA_ONE**STEP) / (jnp.sqrt(second / (1.0 - BETA_TWO**STEP)) + EPS_ADAM)
        adam_out.append((master - LR_ADAM * (update + DECAY * master), first, second))
    return (
        *new_weights,
        adam_out[0][0],
        adam_out[1][0],
        *new_moms,
        adam_out[0][1],
        adam_out[0][2],
        adam_out[1][1],
        adam_out[1][2],
        loss_sum,
        weight_total,
        grad_norm[0, 0],
    )


def solution(mesh):
    row, wide, cube = P("dp", None), P("dp", "mp"), P("dp", None, "mp")
    in_specs = (
        *(row, row, P("dp"), row, row),
        *(cube, wide, wide, wide, cube, row, row),
        *(cube, wide, wide, wide, cube),
        *(row, row, row, row),
    )
    out_specs = (
        *(cube, wide, wide, wide, cube, row, row),
        *(cube, wide, wide, wide, cube),
        *(row, row, row, row),
        *(P(), P(), P()),
    )
    return jax.shard_map(body, mesh=mesh, in_specs=in_specs, out_specs=out_specs, check_vma=False)
```

```python
import functools
import math

import jax
import jax.numpy as jnp
from jax import lax
from jax.experimental import pallas as pl
from jax.experimental.pallas import tpu as pltpu
from jax.sharding import PartitionSpec as P

SIDE = 32
D = 768
HEAD_DIM = 64
CLASSES = 1001
FREQ = 256
PIN = 16
STEP = 10
SLOTS = 4

HIGH = lax.Precision.HIGHEST
GAMMA = 5.0
CLIP = 0.05
MU = 0.95
LR_MUON = 0.1
DECAY = 0.01
BETA_ONE = 0.9
BETA_TWO = 0.95
LR_ADAM = 0.08
EPS_ADAM = 1e-08
NS_COEF = (3.4445, -4.775, 2.0315)
NS_SHIFT = (0.0, 0.1, 0.5, 0.8, 0.8)
ACROSS = (((1,), (1,)), ((), ()))
DOWN = (((0,), (0,)), ((), ()))
ALONG = (((1,), (0,)), ((), ()))
LOW = jnp.bfloat16
F32 = jnp.float32


def dot(a, b, dims=ALONG):
    return lax.dot_general(a, b, dims, preferred_element_type=F32)


def order_of(size):
    order, bit = [0], size // 2
    while bit:
        order += [o ^ bit for o in order]
        bit //= 2
    return order


def swap(x, axis, bit):
    size = lax.axis_size(axis)
    return lax.ppermute(x, axis, [(i, i ^ bit) for i in range(size)])


def after(x, *others):
    return lax.optimization_barrier((x,) + others)[0]


class Course:
    def __init__(self, steps):
        self.steps = steps
        self.result = None
        self.flight = next(steps, None)

    def step(self, x, start=None, behind=None):
        arrived = self.flight
        if arrived is None:
            return x
        arrived = late(arrived, behind)
        x = after(x, *arrived) if isinstance(arrived, tuple) else after(x, arrived)
        try:
            self.flight = self.steps.send((arrived, start))
        except StopIteration as stop:
            self.flight, self.result = None, stop.value
        return x

    def finish(self):
        while self.flight is not None:
            self.step(jnp.zeros((), F32))
        return self.result


def late(x, start):
    if start is None:
        return x
    return lax.optimization_barrier((*x, start))[:-1] if isinstance(x, tuple) else after(x, start)


def gather_steps(x, axis):
    bit = lax.axis_size(axis) // 2
    start, last = None, 1
    while bit > last:
        other, start = yield swap(late(x, start), axis, bit)
        x = jnp.concatenate([x, other], 0)
        bit //= 2
    _, start = yield x
    other, start = yield swap(late(x, start), axis, bit)
    return x, other


def quarter_steps(x, axis):
    bit, start = lax.axis_size(axis) // 2, None
    while bit > 2:
        other, start = yield swap(late(x, start), axis, bit)
        x = jnp.concatenate([x, other], 0)
        bit //= 2
    x = late(x, start)
    (second, third), start = yield swap(x, axis, 2), swap(x, axis, 1)
    fourth, start = yield swap(late(second, start), axis, 1)
    return [x, second, third, fourth]


def joined(pair):
    return jnp.concatenate(pair, 0)


def sum_steps(keep, send, axis):
    bit, size = 1, lax.axis_size(axis)
    other, start = yield swap(send, axis, bit)
    total = keep + other.astype(F32)
    while bit < size // 2:
        bit *= 2
        half = total.shape[0] // 2
        other, start = yield swap(late(total[half:].astype(LOW), start), axis, bit)
        total = total[:half] + other.astype(F32)
    return total


def sum_all(x, axis):
    bit = 1
    while bit < lax.axis_size(axis):
        x = x + swap(x, axis, bit)
        bit *= 2
    return x


def parts_of(h):
    two = swap(h, "mp", 2)
    one = swap(h, "mp", 1)
    return [h, one, two, swap(two, "mp", 1)]


def parts_sum(even, odd, then=lambda x: x):
    near = then(swap(odd, "mp", 1))
    send = (even[1] + near[1].astype(F32)).astype(LOW)
    return [even, near, swap(send, "mp", 2)], send


def turned_over(v, me):
    size, bit = v.shape[-2], 1
    lead, k = v.shape[:-2], v.shape[-1]
    while bit < size:
        pair = v.reshape(lead + (size // (2 * bit), 2, bit, k))
        flipped = jnp.concatenate([pair[..., 1:, :, :], pair[..., :1, :, :]], -3)
        v = jnp.where((me // bit) % 2 == 1, flipped, pair).reshape(lead + (size, k))
        bit *= 2
    return v


def to_local(v, me, size):
    blocks = turned_over(v.reshape(v.shape[:-1] + (size, v.shape[-1] // size)), me)
    return jnp.concatenate([blocks[..., o, :] for o in order_of(size)], -1)


def from_local(v, me, size):
    blocks = v.reshape(v.shape[:-1] + (size, v.shape[-1] // size))
    order = order_of(size)
    return turned_over(jnp.stack([blocks[..., order.index(k), :] for k in range(size)], -2), me)


def spread(x, axis):
    size = math.prod(lax.axis_size(a) for a in ((axis,) if isinstance(axis, str) else axis))
    copies = jnp.broadcast_to(x[None], (size,) + x.shape)
    return lax.all_to_all(copies, axis, 0, 0, tiled=True)


def exchange(x, axis):
    return lax.all_to_all(x, axis, 0, 0, tiled=True)


def plan():
    betas = jnp.linspace(0.0001, 0.02, 1000, dtype=F32)
    return jnp.cumprod(1.0 - betas)


def pick(table, index):
    grid = jnp.arange(table.shape[0], dtype=jnp.int32)
    return jnp.sum(jnp.where(index[..., None] == grid, table, 0.0), -1)


def normalize(x):
    cent = x - jnp.mean(x, -1, keepdims=True)
    inv = lax.rsqrt(jnp.mean(cent * cent, -1, keepdims=True) + 1e-06)
    return cent * inv, inv


def norm_back(grad, unit, inv, scale):
    d_shift = jnp.sum(grad, 0, keepdims=True)
    d_scale = jnp.sum(grad * unit, 0, keepdims=True)
    g = grad * (1.0 + scale)
    dx = inv * (g - jnp.mean(g, -1, keepdims=True) - unit * jnp.mean(g * unit, -1, keepdims=True))
    return dx, d_shift, d_scale


def place_table(column):
    quarter = D // 4
    omega = 1.0 / 10000.0 ** ((column % quarter).astype(F32) / quarter)
    angle = jnp.arange(SIDE, dtype=F32)[:, None] * omega
    wave = jnp.where((column // quarter) % 2 == 0, jnp.sin(angle), jnp.cos(angle))
    down = column < D // 2
    return jnp.concatenate([jnp.where(down, wave, 0.0), jnp.where(down, 0.0, wave)], 0)


def place_select(single, part, rank):
    local = jnp.arange(part, dtype=jnp.int32)
    full = rank * part + local
    half = SIDE // 2
    down = jnp.where(single, full // SIDE, local // half)
    across = jnp.where(single, full % SIDE, local % half)
    grid = jnp.arange(SIDE, dtype=jnp.int32)
    return jnp.concatenate([down[:, None] == grid, across[:, None] == grid], 1)


def thirds(x):
    high = x.astype(LOW)
    rest = x - high.astype(F32)
    mid = rest.astype(LOW)
    return high, mid, (rest - mid.astype(F32)).astype(LOW)


def time_features(steps):
    half = FREQ // 2
    freqs = jnp.exp(-math.log(10000.0) * jnp.arange(half, dtype=F32) / half)
    angles = steps.astype(F32)[:, None] * freqs
    return jnp.concatenate([jnp.cos(angles), jnp.sin(angles)], -1)


def silu_slope(x):
    s = jax.nn.sigmoid(x)
    return s * (1.0 + x * (1.0 - s))


def call(kernel, name, outs, *args, scalars=0, scratch=(), flops=0, vmem_mb=16):
    smem, vmem = pl.BlockSpec(memory_space=pltpu.SMEM), pl.BlockSpec(memory_space=pltpu.VMEM)
    size = sum(math.prod(o[0]) * jnp.dtype(o[1]).itemsize for o in outs)
    return pl.pallas_call(
        kernel,
        out_shape=[jax.ShapeDtypeStruct(*o) for o in outs],
        in_specs=[smem] * scalars + [vmem] * (len(args) - scalars),
        out_specs=[vmem] * len(outs),
        scratch_shapes=[pltpu.VMEM(*t) for t in scratch],
        compiler_params=pltpu.CompilerParams(vmem_limit_bytes=vmem_mb * 2**20),
        cost_estimate=pl.CostEstimate(flops=1, bytes_accessed=1, transcendentals=0),
        name=name,
    )(*args)


def turned(x):
    return x.astype(F32).T.astype(x.dtype)


def added(even_ref, near_ref, far_ref):
    return even_ref[0] + near_ref[0].astype(F32) + far_ref[...].astype(F32)


def pack_kernel(near_ref, slots_ref, m_mod, m_qkv, m_fc1, m_fc2, m_out, own_ref, other_ref):
    width, hidden = m_out.shape[1], m_fc1.shape[1]

    def put(even, odd):
        at = 0
        for piece in [m_mod[:, k] for k in range(8)] + [m_qkv[k] for k in range(3)] + [slots_ref[...].astype(F32)]:
            even[:, at : at + width] = piece.astype(LOW)
            at += width
        odd[:, :hidden] = m_fc1[...].astype(LOW)
        odd[:, hidden : 2 * hidden] = m_fc2[...].astype(LOW)
        odd[:, 2 * hidden : 2 * hidden + width] = m_out[...].astype(LOW)
        odd[:, 2 * hidden + width :] = jnp.zeros((odd.shape[0], 3 * width), LOW)

    @pl.when(near_ref[0] == 0)
    def _():
        put(own_ref.at[0], other_ref)

    @pl.when(near_ref[0] != 0)
    def _():
        put(other_ref, own_ref.at[0])


def pack(near, slots, m_mod, m_qkv, m_fc1, m_fc2, m_out):
    shape = (m_mod.shape[0], 12 * m_out.shape[1])
    return call(
        pack_kernel,
        "pack",
        [((2,) + shape, LOW), (shape, LOW)],
        *(near, slots, m_mod, m_qkv.transpose(1, 0, 2), m_fc1, m_fc2, m_out),
        scalars=1,
    )


def enter_kernel(x_ref, mods_ref, h_ref):
    unit, _ = normalize(x_ref[...])
    h_ref[...] = (unit * (1.0 + mods_ref[1:2, :]) + mods_ref[0:1, :]).astype(LOW)


def middle_kernel(even_ref, near_ref, far_ref, x_ref, mods_ref, attn_ref, mid_ref, h_ref):
    attn = added(even_ref, near_ref, far_ref)
    attn_ref[...] = attn
    mid = x_ref[...] + mods_ref[2:3, :] * attn
    mid_ref[...] = mid
    unit, _ = normalize(mid)
    h_ref[...] = (unit * (1.0 + mods_ref[4:5, :]) + mods_ref[3:4, :]).astype(LOW)


def final_kernel(
    scale_ref, even_ref, near_ref, far_ref, mid_ref, mods_ref, head_ref, noise_ref,
    out_ref, mlp_ref, head_grad_ref, sums_ref, loss_ref,
):
    mlp = added(even_ref, near_ref, far_ref)
    unit, inv = normalize(mid_ref[...] + mods_ref[5:6, :] * mlp)
    h = (unit * (1.0 + mods_ref[7:8, :]) + mods_ref[6:7, :]).astype(LOW)
    diff = dot(h, head_ref[...], ACROSS) - noise_ref[...]
    loss = jnp.sum(jnp.sum(diff * diff, axis=1, keepdims=True), axis=0, keepdims=True)
    loss_ref[...] = jnp.broadcast_to(scale_ref[0] * loss, loss_ref.shape)
    d_pred = (2.0 * diff * scale_ref[1]).astype(LOW)
    head_grad_ref[...] = dot(d_pred, h, DOWN)
    d_out, d_shift, d_scale = norm_back(dot(d_pred, head_ref[...]), unit, inv, mods_ref[7:8, :])
    out_ref[...] = d_out
    mlp_ref[...] = (d_out * mods_ref[5:6, :]).astype(LOW)
    sums_ref[0:1, :] = jnp.sum(d_out * mlp, 0, keepdims=True)
    sums_ref[1:2, :] = d_shift
    sums_ref[2:3, :] = d_scale


def turn_kernel(
    even_ref, near_ref, far_ref, mid_ref, out_ref, attn_ref, mods_ref, d_mid_ref, d_attn_ref, sums_ref
):
    unit, inv = normalize(mid_ref[...])
    dx, d_shift, d_scale = norm_back(added(even_ref, near_ref, far_ref), unit, inv, mods_ref[4:5, :])
    d_mid = out_ref[...] + dx
    d_mid_ref[...] = d_mid
    d_attn_ref[...] = (d_mid * mods_ref[2:3, :]).astype(LOW)
    sums_ref[0:1, :] = jnp.sum(d_mid * attn_ref[...], 0, keepdims=True)
    sums_ref[1:2, :] = d_shift
    sums_ref[2:3, :] = d_scale


def leave_kernel(
    even_ref, near_ref, far_ref, x_ref, d_mid_ref, mods_ref, noisy_ref, mid_sums_ref, end_sums_ref,
    patch_ref, sums_ref,
):
    unit, inv = normalize(x_ref[...])
    dx, d_shift, d_scale = norm_back(added(even_ref, near_ref, far_ref), unit, inv, mods_ref[1:2, :])
    patch_ref[...] = dot(noisy_ref[...], (d_mid_ref[...] + dx).astype(LOW), DOWN)
    sums_ref[0:1, :] = d_shift
    sums_ref[1:2, :] = d_scale
    sums_ref[2:5, :] = mid_sums_ref[0:3, :]
    sums_ref[5:8, :] = end_sums_ref[0:3, :]


def attend_kernel(
    single_ref, h0_ref, h1_ref, h2_ref, h3_ref, w_ref, o_ref,
    qkv_ref, total_ref, mixed_ref, even_ref, odd_ref, vt_ref,
):
    part = h0_ref.shape[0]
    width = mixed_ref.shape[1]
    for j, ref in enumerate((h0_ref, h1_ref, h2_ref, h3_ref)):
        qkv_ref[j * part : (j + 1) * part, :] = dot(ref[...], w_ref[...]).astype(LOW)
    vt_ref[...] = turned(qkv_ref[:, 2 * width :])

    def run(i, keys):
        mine = pl.ds(pl.multiple_of(i * part, part), part)
        outs = []
        for h in range(width // HEAD_DIM):
            lo = h * HEAD_DIM
            q = qkv_ref[mine, lo : lo + HEAD_DIM] * HEAD_DIM**-0.5
            k = qkv_ref[keys, width + lo : width + lo + HEAD_DIM]
            s = dot(k, q, ACROSS)
            top = jnp.max(s, axis=0, keepdims=True)
            e = jnp.exp(s - top)
            z = jnp.sum(e, axis=0, keepdims=True)
            total_ref[h : h + 1, mine] = top + jnp.log(z)
            outs.append(dot(vt_ref[lo : lo + HEAD_DIM, keys], (e * (1.0 / z)).astype(LOW)))
        mixed_ref[mine, :] = jnp.concatenate(outs, 0).T.astype(LOW)

    def block(i, carry):
        mine = pl.ds(pl.multiple_of(i * part, part), part)

        @pl.when(single_ref[0] == 1)
        def _():
            run(i, slice(None))

        @pl.when(single_ref[0] != 1)
        def _():
            run(i, mine)

        return carry

    lax.fori_loop(0, 4, block, 0)
    for j in range(4):
        term = dot(mixed_ref[j * part : (j + 1) * part, :], o_ref[...], ACROSS)
        if j % 2 == 0:
            even_ref[j // 2] = term
        else:
            odd_ref[j // 2] = term.astype(LOW)


def attend_back_kernel(
    single_ref, qkv_ref, total_ref, d0_ref, d1_ref, d2_ref, d3_ref, w_ref, o_ref,
    grad_ref, even_ref, odd_ref, kt_ref, dk_ref, dv_ref, g_ref,
):
    part = d0_ref.shape[0]
    width = qkv_ref.shape[1] // 3
    heads = width // HEAD_DIM
    for j, ref in enumerate((d0_ref, d1_ref, d2_ref, d3_ref)):
        g_ref[j * part : (j + 1) * part, :] = dot(ref[...], o_ref[...]).astype(LOW)
    kt_ref[...] = turned(qkv_ref[:, width : 2 * width] * HEAD_DIM**-0.5)
    dk_ref[...] = jnp.zeros_like(dk_ref)
    dv_ref[...] = jnp.zeros_like(dv_ref)

    def run(i, keys):
        mine = pl.ds(pl.multiple_of(i * part, part), part)
        outs = []
        for h in range(heads):
            lo = h * HEAD_DIM
            q = qkv_ref[mine, lo : lo + HEAD_DIM] * HEAD_DIM**-0.5
            k = qkv_ref[keys, width + lo : width + lo + HEAD_DIM]
            v = qkv_ref[keys, 2 * width + lo : 2 * width + lo + HEAD_DIM]
            g = g_ref[mine, lo : lo + HEAD_DIM]
            p = jnp.exp(dot(k, q, ACROSS) - total_ref[h : h + 1, mine])
            dp = dot(v, g, ACROSS)
            delta = jnp.sum(dp * p, axis=0, keepdims=True)
            ds = (p * (dp - delta)).astype(LOW)
            dv_ref[h, keys, :] += dot(p.astype(LOW), g)
            dk_ref[h, keys, :] += dot(ds, q)
            outs.append(dot(kt_ref[lo : lo + HEAD_DIM, keys], ds))
        grad_ref[mine, :width] = jnp.concatenate(outs, 0).T.astype(LOW)

    def block(i, carry):
        @pl.when(single_ref[0] == 1)
        def _():
            run(i, slice(None))

        @pl.when(single_ref[0] != 1)
        def _():
            run(i, pl.ds(pl.multiple_of(i * part, part), part))

        return carry

    lax.fori_loop(0, 4, block, 0)
    for h in range(heads):
        lo = h * HEAD_DIM
        grad_ref[:, width + lo : width + lo + HEAD_DIM] = dk_ref[h].astype(LOW)
        grad_ref[:, 2 * width + lo : 2 * width + lo + HEAD_DIM] = dv_ref[h].astype(LOW)
    for j in range(4):
        term = dot(grad_ref[j * part : (j + 1) * part, :], w_ref[...], ACROSS)
        if j % 2 == 0:
            even_ref[j // 2] = term
        else:
            odd_ref[j // 2] = term.astype(LOW)


def halves(keep_ref, send_ref, columns, value):
    half = keep_ref.shape[0]
    keep_ref[:, columns] = value[:half]
    send_ref[:, columns] = value[half:].astype(LOW)


def attend_grads_kernel(h0, h1, h2, h3, grad_ref, d0, d1, d2, d3, mixed_ref, keep_ref, send_ref):
    part, width = h0.shape[0], mixed_ref.shape[1]
    rows = lambda j: slice(j * part, (j + 1) * part)
    halves(
        keep_ref, send_ref, slice(0, 3 * width),
        sum(dot(h[...], grad_ref[rows(j), :], DOWN) for j, h in enumerate((h0, h1, h2, h3))),
    )
    halves(
        keep_ref, send_ref, slice(3 * width, 4 * width),
        sum(dot(d[...], mixed_ref[rows(j), :], DOWN) for j, d in enumerate((d0, d1, d2, d3))),
    )


def feed_kernel(h0, h1, h2, h3, w_ref, act_ref, slope_ref, even_ref, odd_ref):
    part, hidden = h0.shape[0], act_ref.shape[1]
    for j, h in enumerate((h0, h1, h2, h3)):
        rows = slice(j * part, (j + 1) * part)
        upper = dot(h[...], w_ref[:, :hidden])
        gate = 0.5 * (1.0 + lax.erf(upper * 0.5**0.5))
        act = (upper * gate).astype(LOW)
        act_ref[rows, :] = act
        slope = gate + upper * jnp.exp(-0.5 * upper * upper) * (2.0 * math.pi) ** -0.5
        slope_ref[rows, :] = slope.astype(LOW)
        term = dot(act, w_ref[:, hidden:], ACROSS)
        if j % 2 == 0:
            even_ref[j // 2] = term
        else:
            odd_ref[j // 2] = term.astype(LOW)


def feed_back_kernel(d0, d1, d2, d3, slope_ref, w_ref, upper_ref, even_ref, odd_ref):
    part, hidden = d0.shape[0], slope_ref.shape[1]
    for j, d in enumerate((d0, d1, d2, d3)):
        rows = slice(j * part, (j + 1) * part)
        d_upper = (dot(d[...], w_ref[:, hidden:]) * slope_ref[rows, :].astype(F32)).astype(LOW)
        upper_ref[rows, :] = d_upper
        term = dot(d_upper, w_ref[:, :hidden], ACROSS)
        if j % 2 == 0:
            even_ref[j // 2] = term
        else:
            odd_ref[j // 2] = term.astype(LOW)


def feed_grads_kernel(h0, h1, h2, h3, x_ref, keep_ref, send_ref):
    part = h0.shape[0]
    value = sum(
        dot(h[...], x_ref[j * part : (j + 1) * part, :], DOWN) for j, h in enumerate((h0, h1, h2, h3))
    )
    halves(keep_ref, send_ref, slice(None), value)


def muon_kernel(columns, span, order_ref, coef_ref, plan_ref, mom_ref, *refs):
    grads, (out_ref, x_ref, b_ref, e_ref, r_ref, turn_ref) = refs[:-6], refs[-6:]
    third = NS_COEF[2]
    size, width = x_ref.shape
    count, pairs = mom_ref.shape[2], mom_ref.shape[0]
    coef = coef_ref[0]
    spans = [slice(i, min(i + size, width)) for i in range(0, width, size)]

    tall = size < count * 2 * pairs
    squares = jnp.zeros((1, 1), F32)
    for place in range(2 * pairs):
        true = order_ref[place]
        if len(grads) == 1:
            grad = grads[0][true, :, slice(*span)].astype(F32)
        elif len(grads) == 2:
            grad = dot(grads[0][lax.shift_right_logical(true, 1), place // pairs], grads[1][...])
        else:
            quarter, row = divmod(place * count, grads[0].shape[0])
            grad = grads[quarter][row : row + count, :].astype(F32)
        mom = mom_ref[lax.shift_right_logical(true, 1), place // pairs, :, slice(*columns)]
        x = MU * mom.astype(F32) + coef * grad
        if tall:
            turn_ref[place * count : (place + 1) * count, :] = x
        else:
            x_ref[place * count : (place + 1) * count, :] = x
        squares = squares + jnp.sum(jnp.sum(x * x, axis=0, keepdims=True), axis=1, keepdims=True)
    inv = 1.0 / (jnp.sqrt(squares) + 1e-07)
    x_ref[...] = (turn_ref[...].T if tall else x_ref[...]) * inv
    b_ref[...] = x_ref[...].astype(LOW)

    def gram(shift):
        e = sum(dot(b_ref[:, span], b_ref[:, span], ACROSS) for span in spans)
        row = lax.broadcasted_iota(jnp.int32, e.shape, 0)
        column = lax.broadcasted_iota(jnp.int32, e.shape, 1)
        e = e - jnp.where(row == column, shift, 0.0)
        e_ref[...] = e
        r_ref[...] = e.astype(LOW)

    def turn(i, carry):
        centre, slope = plan_ref[i, 0], plan_ref[i, 1]
        gram(plan_ref[i, 2])
        r_ref[...] = (slope * e_ref[...] + third * dot(r_ref[...], r_ref[...])).astype(LOW)
        for span in spans:
            x = centre * x_ref[:, span] + dot(r_ref[...], b_ref[:, span])
            x_ref[:, span] = x
            b_ref[:, span] = x.astype(LOW)
        return carry

    last = len(NS_SHIFT) - 1
    lax.fori_loop(0, last, turn, 0)
    gram(plan_ref[last, 2])
    both = [slice(0, count), slice(pairs * count, (pairs + 1) * count)]
    scaled = 0.2 * math.sqrt(max(size, width))
    if tall:
        poly = plan_ref[last, 1] * e_ref[...] + third * dot(r_ref[...], r_ref[...])
        x = jnp.concatenate([x_ref[:, own].T for own in both], 0)
        x = scaled * (plan_ref[last, 0] * x + dot(x.astype(LOW), poly.astype(LOW)))
        out_ref[0] = x[:count].astype(LOW)
        out_ref[1] = x[count:].astype(LOW)
        return
    e = jnp.concatenate([e_ref[own, :] for own in both], 0)
    poly = (plan_ref[last, 1] * e + third * dot(e.astype(LOW), r_ref[...])).astype(LOW)
    for span in spans:
        x = jnp.concatenate([x_ref[own, span] for own in both], 0)
        x = scaled * (plan_ref[last, 0] * x + dot(poly, b_ref[:, span]))
        out_ref[0, :, span] = x[:count].astype(LOW)
        out_ref[1, :, span] = x[count:].astype(LOW)


def muon_rows(order, coef, old, block, columns, grads, span=None):
    pairs, _, count, _ = old.shape
    deep, width = 2 * pairs * count, columns[1] - columns[0]
    size, long = (width, deep) if 2 * width <= deep else (deep, width)
    first, second, third = NS_COEF
    plan = [[first + second * s + third * s * s, second + 2.0 * third * s, s] for s in NS_SHIFT]
    smem, vmem = pl.BlockSpec(memory_space=pltpu.SMEM), pl.BlockSpec(memory_space=pltpu.VMEM)
    return pl.pallas_call(
        functools.partial(muon_kernel, columns, span),
        grid=(1,),
        out_shape=jax.ShapeDtypeStruct((2, count, width), LOW),
        in_specs=[smem, smem, smem, pl.BlockSpec((pairs, 2, count, block[0]), lambda i: (0, 0, 0, block[1]))]
        + [vmem] * len(grads),
        out_specs=vmem,
        scratch_shapes=[
            pltpu.VMEM((size, long), F32),
            pltpu.VMEM((size, long), LOW),
            pltpu.VMEM((size, size), F32),
            pltpu.VMEM((size, size), LOW),
            pltpu.VMEM((deep, width) if size < deep else (8, 128), F32),
        ],
        compiler_params=pltpu.CompilerParams(vmem_limit_bytes=32 * 2**20),
        cost_estimate=pl.CostEstimate(flops=1, bytes_accessed=1, transcendentals=0),
        name="muon",
    )(order, coef, jnp.array(plan, F32), old, *grads)


def weights_kernel(near_ref, own_a, got_a, own_b, got_b, w_qkv, w_out, w_fc1, w_fc2, w_mod, n_qkv, n_out, n_fc1, n_fc2, n_mod):
    width, hidden = w_out.shape[1], w_fc1.shape[1]
    mine = near_ref[0] == 0

    def put(place, weight, new, update):
        new[place] = weight[place] * (1.0 - LR_MUON * DECAY) - LR_MUON * update

    a, b = own_a[...].astype(F32), got_a[...].astype(F32)
    u_mod, u_fc = jnp.where(mine, a, b), jnp.where(mine, b, a)
    a, b = own_b[...].astype(F32), got_b[...].astype(F32)
    u_qkv, u_out = jnp.where(mine, a, b), jnp.where(mine, b, a)[:, :width]
    for k in range(3):
        put(k, w_qkv, n_qkv, u_qkv[:, k * width : (k + 1) * width])
    for k in range(8):
        put((slice(None), k), w_mod, n_mod, u_mod[:, k * width : (k + 1) * width])
    put(slice(None), w_out, n_out, u_out)
    put(slice(None), w_fc2, n_fc2, u_fc[:, :hidden])
    put(slice(None), w_fc1, n_fc1, u_fc[:, hidden:])


def momenta_kernel(coef_ref, g_at, g_fc1, g_fc2, g_mod, m_qkv, m_out, m_fc1, m_fc2, m_mod, k_qkv, k_out, k_fc1, k_fc2, k_mod):
    width = m_out.shape[1]
    coef = coef_ref[0]

    def put(place, mom, kept, grad):
        kept[place] = MU * mom[place] + coef * grad

    for k in range(3):
        put(k, m_qkv, k_qkv, g_at[:, k * width : (k + 1) * width])
    for k in range(8):
        put((slice(None), k), m_mod, k_mod, g_mod[:, k * width : (k + 1) * width])
    put(slice(None), m_out, k_out, g_at[:, 3 * width :])
    put(slice(None), m_fc2, k_fc2, g_fc2[...])
    put(slice(None), m_fc1, k_fc1, g_fc1[...])


def by_rows(kernel, name, scalar, flats, arrays):
    rows = flats[0].shape[0]
    step = rows // 2 if rows % 32 == 0 else rows

    def block(a):
        if a.ndim == 2:
            return pl.BlockSpec((step, a.shape[1]), lambda i: (i, 0))
        if a.shape[0] == rows:
            return pl.BlockSpec((step,) + a.shape[1:], lambda i: (i, 0, 0))
        return pl.BlockSpec((a.shape[0], step, a.shape[2]), lambda i: (0, i, 0))

    arrays = [arrays[0].transpose(1, 0, 2), *arrays[1:]]
    outs = pl.pallas_call(
        kernel,
        grid=(rows // step,),
        out_shape=[jax.ShapeDtypeStruct(a.shape, F32) for a in arrays],
        in_specs=[pl.BlockSpec(memory_space=pltpu.SMEM)] + [block(a) for a in (*flats, *arrays)],
        out_specs=[block(a) for a in arrays],
        compiler_params=pltpu.CompilerParams(vmem_limit_bytes=32 * 2**20),
        name=name,
    )(scalar, *flats, *arrays)
    return [outs[0].transpose(1, 0, 2), *outs[1:]]


def body(
    latents,
    noise,
    segment_ids,
    timesteps,
    labels,
    w_qkv,
    w_out,
    w_fc1,
    w_fc2,
    w_mod,
    w_head,
    w_cond,
    mom_qkv,
    mom_out,
    mom_fc1,
    mom_fc2,
    mom_mod,
    first_head,
    second_head,
    first_cond,
    second_cond,
):
    n_dp, n_mp = lax.axis_size("dp"), lax.axis_size("mp")
    me, rank = lax.axis_index("dp"), lax.axis_index("mp")
    near = me % 2
    tokens = latents.shape[0]
    part = tokens // n_mp
    rows = w_qkv.shape[0]
    width = w_qkv.shape[2]
    hidden = w_fc1.shape[1]
    half = D // 2
    place = [me ^ o for o in order_of(n_dp)]
    places = me ^ jnp.array(order_of(n_dp), jnp.int32)

    single = jnp.max(segment_ids) == 0
    time1_own = w_cond[:, PIN : PIN + FREQ].astype(LOW)
    digits = [v for a in (timesteps, labels) for v in (a.reshape(-1) // SIDE, a.reshape(-1) % SIDE)]
    note = jnp.concatenate(digits + [single.astype(jnp.int32)[None]]).astype(LOW)
    note = jnp.pad(note, (0, FREQ - note.shape[0]))
    thin = jnp.concatenate([w_cond[:, :PIN].astype(LOW), w_head.astype(LOW)], 1).reshape(-1, FREQ)
    thin_rows = thin.shape[0]
    fill = -(rows + thin_rows) % 16 or 16
    packet = spread(jnp.concatenate([time1_own, thin, jnp.broadcast_to(note, (fill, FREQ))], 0), "dp")
    packet = packet.reshape(n_dp, rows + thin_rows + fill, FREQ)

    time1_b = packet[:, :rows].reshape(D, FREQ)
    thin = packet[:, rows : rows + thin_rows].reshape(n_dp, rows, 2 * PIN).astype(F32)
    thin = jnp.concatenate([lax.dynamic_index_in_dim(thin, p, 0) for p in place], 0)
    thin = thin.reshape(D, 2 * PIN).T.astype(LOW)
    patch_b, head_b = thin[:PIN], thin[PIN:]
    notes = packet[:, rows + thin_rows].astype(jnp.int32)
    steps = notes[:, :SLOTS] * SIDE + notes[:, SLOTS : 2 * SLOTS]
    kinds = (notes[:, 2 * SLOTS : 3 * SLOTS] * SIDE + notes[:, 3 * SLOTS : 4 * SLOTS]).reshape(-1)
    singles = notes[:, 4 * SLOTS] == 1

    time2_b = w_cond[:, PIN + FREQ : PIN + FREQ + D].astype(LOW)
    table_b = w_cond[:, PIN + FREQ + D :].astype(LOW)
    mod_b = jnp.concatenate([w_mod[:, k].astype(LOW) for k in range(8)], 1)
    feat_b = time_features(steps.reshape(-1)).astype(LOW)
    slots_all = feat_b.shape[0]
    silu_t_b = jax.nn.silu(dot(feat_b, time1_b, ACROSS)).astype(LOW)
    onehot = (kinds[:, None] == jnp.arange(CLASSES, dtype=jnp.int32)).astype(LOW)
    qkv_own = jnp.concatenate([w_qkv[:, k].astype(LOW) for k in range(3)] + [w_out.astype(LOW)], 1)
    proj_way = Course(gather_steps(after(qkv_own, silu_t_b), "dp"))
    cond = dot(silu_t_b, time2_b, ACROSS) + dot(onehot, table_b, ACROSS)
    silu_c_b = jax.nn.silu(cond).astype(LOW)
    mod_part = exchange(dot(silu_c_b, mod_b).reshape(n_dp, SLOTS, -1), "dp")
    mod_cols = jnp.sum(mod_part, 0).reshape(SLOTS, 8, width)
    mod_cols = proj_way.step(mod_cols, mod_cols)
    slots_own = jnp.pad(silu_c_b.T, ((0, 0), (0, width - slots_all)))
    own_pack, other_pack = pack(near[None], slots_own, mom_mod, mom_qkv, mom_fc1, mom_fc2, mom_out)
    other_pack = swap(other_pack, "dp", 1)
    part_slots = segment_ids[::part]
    outgoing = jnp.sum(
        jnp.where((part_slots[:, None] == jnp.arange(SLOTS))[:, :, None, None], mod_cols[None], 0.0), 1
    )
    mods = exchange(outgoing, "mp").transpose(1, 0, 2).reshape(8, n_mp * width)
    slot = jnp.sum(jnp.where(jnp.arange(n_mp) == rank, part_slots, 0))

    abar = pick(plan(), steps)
    snr = abar / (1.0 - abar)
    slot_weight = jnp.minimum(snr, GAMMA) / snr
    weight_total = part * jnp.sum(jnp.where(singles[:, None], n_mp * slot_weight[:, :1] / SLOTS, slot_weight))
    mine = (jnp.arange(n_dp)[:, None] == me) & (jnp.arange(SLOTS) == slot)
    my_slot = lambda a: jnp.sum(jnp.where(mine, a, 0.0))
    abar_tok, weight_tok = my_slot(abar), my_slot(slot_weight)
    right = jnp.concatenate(
        [
            jnp.concatenate([jnp.zeros((slots_all, PIN), LOW), feat_b, jnp.zeros((slots_all, D + CLASSES), LOW)], 1),
            jnp.eye(PIN, PIN + FREQ + D + CLASSES, dtype=LOW),
            jnp.concatenate([jnp.zeros((slots_all, PIN + FREQ), LOW), silu_t_b, onehot], 1),
        ],
        0,
    )
    right = jnp.concatenate([right] * 3, 0)
    scales = jnp.stack([weight_tok, weight_tok / weight_total])
    mods = after(to_local(mods, me, n_dp), other_pack, right, scales)
    lat = lax.dynamic_slice_in_dim(latents, rank * part, part, 0)
    noi = lax.dynamic_slice_in_dim(noise, rank * part, part, 0)
    noisy_b = (jnp.sqrt(abar_tok) * lat + jnp.sqrt(1.0 - abar_tok) * noi).astype(LOW)
    picks = place_select(single, part, rank).astype(LOW)
    left = jnp.concatenate([noisy_b, picks, picks, picks], 1)
    column = (after(places, silu_t_b)[:, None] * rows + jnp.arange(rows, dtype=jnp.int32)).reshape(-1)
    x_in = dot(left, jnp.concatenate([patch_b, *thirds(place_table(column))], 0))
    alone = single.astype(jnp.int32)[None]

    tile = ((part, D), F32)
    tile_b = ((part, D), LOW)
    terms = [((2, part, D), F32), ((2, part, D), LOW)]
    sums = ((8, D), F32)
    thin_grad = ((PIN, D), F32)
    shares = [((half, D), F32), ((half, D), LOW)]
    (h_in,) = call(enter_kernel, "enter", [tile_b], x_in, mods)
    h_in = proj_way.step(h_in)
    feed_own = jnp.concatenate([w_fc1, w_fc2], 1).astype(LOW)
    feed_way = Course(gather_steps(after(feed_own, h_in), "dp"))
    sides = [[side + 2 * i for i in range(n_dp // 2)] for side in range(2)]
    stacked = lax.dynamic_update_slice(own_pack, other_pack[None], (1, 0, 0))
    old = lax.all_gather(after(stacked, h_in), "dp", axis=0, axis_index_groups=sides)
    h_in = parts_of(h_in)
    h_in[1] = proj_way.step(h_in[1])
    h_in[3] = feed_way.step(h_in[3])
    proj = joined(proj_way.finish())
    qkv_b, out_b = proj[:, : 3 * width], proj[:, 3 * width :]
    qkv, totals, mixed_b, *attn_terms = call(
        attend_kernel,
        "attend",
        [((tokens, 3 * width), LOW), ((8, tokens), F32), ((tokens, width), LOW), *terms],
        *(alone, *h_in, qkv_b, out_b),
        scalars=1,
        scratch=[((width, tokens), LOW)],
        flops=8 * tokens * tokens * width + 8 * tokens * D * width,
    )
    attn_terms, _ = parts_sum(*attn_terms, lambda near: feed_way.step(feed_way.step(near)))
    attn, x_mid, h_mid = call(middle_kernel, "middle", [tile, tile, tile_b], *attn_terms, x_in, mods)
    h_mid = parts_of(h_mid)
    feed_b = joined(feed_way.finish())

    act_b, slope, *mlp_terms = call(
        feed_kernel,
        "feed",
        [((tokens, hidden), LOW), ((tokens, hidden), LOW), *terms],
        *(*h_mid, feed_b),
        flops=4 * tokens * D * hidden,
    )
    mlp_terms, _ = parts_sum(*mlp_terms)
    d_out, d_mlp, d_head, end_sums, loss_part = call(
        final_kernel,
        "final",
        [tile, tile_b, thin_grad, sums, ((1, 128), F32)],
        *(scales, *mlp_terms, x_mid, mods, head_b, noi),
        scalars=1,
    )

    d_mlp = parts_of(d_mlp)
    flops = 2 * tokens * D * hidden
    d_upper, *terms_mid = call(
        feed_back_kernel,
        "feed_back",
        [((tokens, hidden), LOW), *terms],
        *(*d_mlp, slope, feed_b),
        flops=2 * flops,
    )
    terms_mid, sent = parts_sum(*terms_mid)
    act_late, d_upper = lax.optimization_barrier((act_b, d_upper, sent))[:2]
    fc2_terms = call(feed_grads_kernel, "feed_grads", shares, *d_mlp, act_late, flops=flops)
    fc2_way = Course(sum_steps(*fc2_terms, "dp"))
    fc1_terms = call(feed_grads_kernel, "feed_grads", shares, *h_mid, d_upper, flops=flops)
    fc1_way = Course(sum_steps(*fc1_terms, "dp"))
    d_mid, d_attn, mid_sums = call(
        turn_kernel, "turn", [tile, tile_b, sums], *terms_mid, x_mid, d_out, attn, mods
    )
    d_attn = parts_of(after(d_attn, old))
    d_attn[1] = fc2_way.step(d_attn[1])
    d_attn[3] = fc1_way.step(fc2_way.step(d_attn[3]))
    d_qkv, even, odd = call(
        attend_back_kernel,
        "attend_back",
        [((tokens, 3 * width), LOW), *terms],
        *(alone, qkv, totals, *d_attn, qkv_b, out_b),
        scalars=1,
        scratch=[((width, tokens), LOW)]
        + [((width // HEAD_DIM, tokens, HEAD_DIM), F32)] * 2
        + [((tokens, width), LOW)],
        flops=20 * tokens * tokens * width + 8 * tokens * D * width,
    )
    odd = fc1_way.step(fc2_way.step(odd))
    sum_fc2 = fc2_way.finish()
    fc2_way = Course(quarter_steps(sum_fc2.astype(LOW), "dp"))
    terms_in, sent = parts_sum(even, odd)
    at_terms = call(
        attend_grads_kernel,
        "attend_grads",
        shares,
        *(*h_in, after(d_qkv, sent), *d_attn, mixed_b),
        flops=8 * tokens * D * width,
    )
    at_way = Course(sum_steps(*at_terms, "dp"))
    terms_in[2] = fc2_way.step(fc1_way.step(terms_in[2], behind=at_terms[1]), behind=at_terms[1])
    sum_fc1 = fc1_way.finish()
    fc1_way = Course(quarter_steps(sum_fc1.astype(LOW), "dp"))
    d_patch, d_mods = call(
        leave_kernel, "leave", [thin_grad, sums], *terms_in, x_in, d_mid, mods, noisy_b, mid_sums, end_sums
    )

    d_mods = from_local(d_mods, me, n_dp).reshape(8, n_mp, width).transpose(1, 0, 2)
    blocks = jnp.broadcast_to(d_mods[None], (n_dp,) + d_mods.shape).reshape((n_dp * n_mp,) + d_mods.shape[1:])
    blocks = exchange(blocks, ("dp", "mp")).reshape(n_dp, n_mp, 8, width)
    blocks = at_way.step(blocks, blocks)
    first_only = (jnp.arange(SLOTS) == 0)[:, None, None]
    d_mod_all = jnp.where(
        singles[:, None, None, None], jnp.where(first_only, jnp.sum(blocks, 1, keepdims=True), 0.0), blocks
    )
    d_mod_all = d_mod_all.astype(LOW).reshape(slots_all, 8 * width)
    g_mod = dot(silu_c_b, d_mod_all, DOWN)
    d_cond_part = dot(d_mod_all, mod_b, ACROSS) * silu_slope(cond)
    d_silu_t_part = lax.dot_general(d_cond_part, time2_b.astype(F32), ALONG, precision=HIGH)
    thick = jnp.concatenate(
        [d_silu_t_part.reshape(-1, n_dp, rows), from_local(jnp.concatenate([d_patch, d_head], 0), me, n_dp)], 0
    )
    thick = jnp.sum(exchange(thick.transpose(1, 0, 2), "dp"), 0)
    thick = jnp.concatenate([thick, d_cond_part], 0)
    chip = thick + swap(thick, "mp", 1)
    for way in (at_way, fc1_way, fc2_way):
        chip = way.step(chip, thick)
    thick = chip + swap(chip, "mp", 2)
    hidden_t = dot(feat_b, time1_own, ACROSS)
    d_hidden = thick[:slots_all] * silu_slope(hidden_t)
    g_patch = thick[slots_all : slots_all + PIN]
    g_head = thick[slots_all + PIN : slots_all + 2 * PIN].T
    d_cond = thick[slots_all + 2 * PIN :]
    g_cond = dot(
        jnp.concatenate(thirds(jnp.concatenate([d_hidden, g_patch, d_cond], 0)), 0),
        right,
        DOWN,
    )

    square = lambda g: jnp.sum(g * g)
    sum_at = at_way.finish()
    parts = [square(g) for g in (sum_fc1, sum_fc2, sum_at, g_mod, g_head, g_cond)] + [loss_part[0, 0]]
    share = jnp.array([1.0] * 4 + [1.0 / n_mp] * 2 + [1.0], F32)
    tally = jnp.pad(jnp.stack(parts) * share, (0, 128 - len(parts)))[None]
    tally = jnp.sum(spread(tally, ("dp", "mp")), 0)
    tally = fc1_way.step(fc2_way.step(tally), tally)
    lane = jnp.arange(128)[None]
    grad_norm = jnp.sqrt(jnp.sum(jnp.where(lane < 6, tally, 0.0), 1, keepdims=True))
    loss_sum = jnp.sum(jnp.where(lane == 6, tally, 0.0))
    coef = jnp.minimum(1.0, CLIP / (grad_norm + 1e-06))

    all_fc2 = fc2_way.finish()
    all_fc1 = fc1_way.finish()
    factor = coef.reshape(1)
    all_at = lax.all_gather(sum_at.astype(LOW), "dp", axis=0)
    span = 8 * width

    silu_c_all = old[:, :, :, 11 * width : 11 * width + slots_all]

    def one_mod():
        return muon_rows(places, factor, old, (span, 0), (0, span), (silu_c_all, d_mod_all))

    def one_fc2():
        mine = muon_rows(places, factor, old, (hidden, 1), (0, hidden), all_fc2)
        return jnp.pad(mine, ((0, 0), (0, 0), (0, span - hidden)))

    def one_fc1():
        mine = muon_rows(places, factor, old, (hidden, 0), (0, hidden), all_fc1)
        return jnp.concatenate([both[:, :, :hidden], mine], 2)

    at_block = (4 * width, 2)

    def one_qkv():
        return muon_rows(places, factor, old, at_block, (0, 3 * width), (all_at,), (0, 3 * width))

    def one_out():
        mine = muon_rows(places, factor, old, at_block, (0, width), (all_at,), (3 * width, 4 * width))
        return jnp.pad(mine, ((0, 0), (0, 0), (0, 2 * width)))

    both = lax.cond(near == 0, one_mod, one_fc2)
    both = lax.cond(near == 0, lambda: both, one_fc1)
    last = lax.cond(near == 0, one_qkv, one_out)
    both = after(both, last)
    new_moms = by_rows(
        momenta_kernel,
        "momenta",
        after(factor, last),
        (sum_at, sum_fc1, sum_fc2, g_mod),
        (mom_qkv, mom_out, mom_fc1, mom_fc2, mom_mod),
    )
    new_weights = by_rows(
        weights_kernel,
        "weights",
        near[None],
        (both[0], swap(both[1], "dp", 1), last[0], swap(last[1], "dp", 1)),
        (w_qkv, w_out, w_fc1, w_fc2, w_mod),
    )
    coef = after(coef, last)

    adam_out = []
    for master, first, second, grad in (
        (w_head, first_head, second_head, g_head),
        (w_cond, first_cond, second_cond, g_cond),
    ):
        clipped = coef * grad
        first = BETA_ONE * first + (1.0 - BETA_ONE) * clipped
        second = BETA_TWO * second + (1.0 - BETA_TWO) * clipped * clipped
        update = first / (1.0 - BETA_ONE**STEP) / (jnp.sqrt(second / (1.0 - BETA_TWO**STEP)) + EPS_ADAM)
        adam_out.append((master - LR_ADAM * (update + DECAY * master), first, second))
    return (
        *new_weights,
        adam_out[0][0],
        adam_out[1][0],
        *new_moms,
        adam_out[0][1],
        adam_out[0][2],
        adam_out[1][1],
        adam_out[1][2],
        loss_sum,
        weight_total,
        grad_norm[0, 0],
    )


def solution(mesh):
    row, wide, cube = P("dp", None), P("dp", "mp"), P("dp", None, "mp")
    in_specs = (
        *(row, row, P("dp"), row, row),
        *(cube, wide, wide, wide, cube, row, row),
        *(cube, wide, wide, wide, cube),
        *(row, row, row, row),
    )
    out_specs = (
        *(cube, wide, wide, wide, cube, row, row),
        *(cube, wide, wide, wide, cube),
        *(row, row, row, row),
        *(P(), P(), P()),
    )
    return jax.shard_map(body, mesh=mesh, in_specs=in_specs, out_specs=out_specs, check_vma=False)
```
